512 devices in a mesh: stream: 64 (over y, z_hi, core), span: 8 (over x, z_lo).
Axes of the slice: x: 4, y: 8, z: 8 (z_hi: 4, z_lo: 2; z = z_hi * 2 + z_lo), core: 2. Of those that a mesh axis runs over, the one named last changes fastest.
Arguments:
- rhs_field: float32 [64, 8, 8, 2, 320], P('stream', 'span'), may hold values from -6 to 6
- guess: float32 [64, 8, 8, 2, 320], P('stream', 'span'), may hold values from -6 to 6
- inverse_diag: float32 [64, 8, 2, 320, 320], P('stream', 'span'), may hold values from -0.3125 to 0.3125
- lower_block: float32 [64, 8, 2, 80, 80], P('stream', 'span'), may hold values from -1.25 to 1.25
- upper_block: float32 [64, 8, 2, 80, 80], P('stream', 'span'), may hold values from -1.25 to 1.25
- west_block: float32 [64, 8, 2, 80, 80], P('stream', 'span'), may hold values from -0.625 to 0.625
- east_block: float32 [64, 8, 2, 80, 80], P('stream', 'span'), may hold values from -0.625 to 0.625
- inflow_map: int32 [64, 8, 2], P('stream', 'span'), may hold values from 0 to 1, each once within a row
Outputs:
- updated: float32 [64, 8, 8, 2, 320], P('stream', 'span')
The draws below stay inside these ranges and needn't reach their ends.
Inputs may be any that keep to these rules, and one draw needn't show every extreme that they name: `inflow_map`: each row of a layer names each of the 2 elements of the layer upstream once.
All inputs are finite; a program needn't handle non-finite values.
Results may differ from the reference program's by a relative error of at most 0.0003.
Values sent between devices are 32-bit elements; how exact they have to be, the bound alone decides.
No kernel may reach another device: no remote copies, remote signals or barrier semaphores. Data moves between devices by JAX's collectives and lax.ppermute only.
A program may use at most 64 MiB of HBM per device.

```python
import jax
import jax.numpy as jnp
from jax import lax

NVAR = 5
NB = 4
DOF = 320
FACE = 80
CN = 2
R = 8
NS = 64
NSPAN = 8


def steps_of(key, shape, cuts, least, high):
    def one(position, shards_of):
        draws = jax.random.uniform(jax.random.fold_in(jax.random.fold_in(key, 6), position), (shards_of,), jnp.float32, least / len(cuts), high / len(cuts))
        return jnp.repeat(jnp.exp(draws), shape[position] // shards_of).reshape((-1,) + (1,) * (len(shape) - position - 1))

    level = one(*cuts[0])
    for cut in cuts[1:]:
        level = level * one(*cut)
    return level


def noise(stream_key, extent, width, limit, cuts=(), kind=jnp.bfloat16):
    result = jax.random.normal(stream_key, extent, jnp.float32) * width
    if len(cuts) > 0:
        result = steps_of(stream_key, extent, cuts, -0.22, 0.18) * result
    return jnp.clip(result, min=-limit, max=limit).astype(kind)


def setup_inputs(seed: int = 0) -> dict:
    streams_of = jax.random.split(jax.random.key(seed), 9)
    return {
        "rhs_field": noise(streams_of[0], (NS, NSPAN, R, CN, DOF), 1.0, 6.0, ((0, 64), (1, 8)), jnp.float32),
        "guess": noise(streams_of[1], (NS, NSPAN, R, CN, DOF), 1.0, 6.0, ((0, 64), (1, 8)), jnp.float32),
        "inverse_diag": noise(streams_of[2], (NS, NSPAN, CN, DOF, DOF), DOF ** -0.5, 0.3125, ((0, 64), (1, 8)), jnp.float32),
        "lower_block": noise(streams_of[3], (NS, NSPAN, CN, FACE, FACE), (17 * NVAR // 4) ** -0.5, 1.25, ((0, 64), (1, 8)), jnp.float32),
        "upper_block": noise(streams_of[4], (NS, NSPAN, CN, FACE, FACE), (17 * NVAR // 4) ** -0.5, 1.25, ((0, 64), (1, 8)), jnp.float32),
        "west_block": noise(streams_of[5], (NS, NSPAN, CN, FACE, FACE), FACE ** -0.5, 0.625, ((0, 64), (1, 8)), jnp.float32),
        "east_block": noise(streams_of[6], (NS, NSPAN, CN, FACE, FACE), FACE ** -0.5, 0.625, ((0, 64), (1, 8)), jnp.float32),
        "inflow_map": jax.vmap(lambda own: jax.random.permutation(own, CN))(jax.random.split(streams_of[7], NS * NSPAN)).reshape((NS, NSPAN, CN)).astype(jnp.int32),
    }


PRECISE = lax.Precision.HIGHEST


def stream_face(values_in, j):
    shape_lead = values_in.shape[:-1]
    nodal = values_in.reshape(shape_lead + (NVAR, NB, NB * NB))
    return nodal[..., :, j, :].reshape(shape_lead + (FACE,))


def span_face(values_in, j):
    shape_lead = values_in.shape[:-1]
    nodal = values_in.reshape(shape_lead + (NVAR, NB, NB, NB))
    return nodal[..., :, :, j, :].reshape(shape_lead + (FACE,))


def add_stream(values_in, added, j):
    shape_lead = values_in.shape[:-1]
    nodal = values_in.reshape(shape_lead + (NVAR, NB, NB * NB))
    nodal = nodal.at[..., :, j, :].add(added.reshape(shape_lead + (NVAR, NB * NB)))
    return nodal.reshape(values_in.shape)


def add_span(values_in, added, j):
    shape_lead = values_in.shape[:-1]
    nodal = values_in.reshape(shape_lead + (NVAR, NB, NB, NB))
    nodal = nodal.at[..., :, :, j, :].add(added.reshape(shape_lead + (NVAR, NB, NB)))
    return nodal.reshape(values_in.shape)


def stream_cols(matrices, j):
    shape_lead = matrices.shape[:-1]
    nodal = matrices.reshape(shape_lead + (NVAR, NB, NB * NB))
    return nodal[..., :, j, :].reshape(shape_lead + (FACE,))


def blocks_times(blocks, vectors):
    return jnp.einsum('...ngf,...rnf->...rng', blocks, vectors, precision=PRECISE)


def pull_rows(onehot, vectors):
    return jnp.einsum('...mp,...rpf->...rmf', onehot, vectors, precision=PRECISE)


def push_rows(onehot, vectors):
    return jnp.einsum('...mn,...rmf->...rnf', onehot, vectors, precision=PRECISE)


def reference(rhs_field, guess, inverse_diag, lower_block, upper_block, west_block, east_block, inflow_map):
    onehot = (inflow_map[..., None] == jnp.arange(CN, dtype=jnp.int32)).astype(jnp.float32)
    west_term = blocks_times(west_block, span_face(jnp.roll(guess, 1, axis=1), NB - 1))
    east_term = blocks_times(east_block, span_face(jnp.roll(guess, -1, axis=1), 0))
    lagged_all = push_rows(onehot, blocks_times(upper_block, stream_face(guess, 0)))
    lagged = jnp.concatenate([lagged_all[1:], jnp.zeros_like(lagged_all[:1])], axis=0)
    source = add_span(add_span(rhs_field, -west_term, 0), -east_term, NB - 1)
    source = add_stream(source, -lagged, NB - 1)
    out_cols = stream_cols(inverse_diag, NB - 1)

    def forward(outflow, layer_data):
        source_k, inverse_k, lower_k, onehot_k = layer_data
        inflow = blocks_times(lower_k, pull_rows(onehot_k, outflow))
        solved = jnp.einsum('...ned,...rnd->...rne', inverse_k, add_stream(source_k, -inflow, 0), precision=PRECISE)
        return stream_face(solved, NB - 1), solved

    zero_faces = jnp.zeros(rhs_field.shape[1:-1] + (FACE,), jnp.float32)
    _, sweep_one = lax.scan(forward, zero_faces, (source, inverse_diag, lower_block, onehot))

    def backward(coupled, layer_data):
        first_k, cols_k, upper_k, onehot_k, lagged_k = layer_data
        solved = first_k + jnp.einsum('...nef,...rnf->...rne', cols_k, lagged_k - coupled, precision=PRECISE)
        return push_rows(onehot_k, blocks_times(upper_k, stream_face(solved, 0))), solved

    _, updated = lax.scan(backward, zero_faces, (sweep_one, out_cols, upper_block, onehot, lagged), reverse=True)
    return updated
```

```python
import functools

import jax
import jax.numpy as jnp
import numpy as np
from jax import lax
from jax.experimental import pallas as pl
from jax.experimental.pallas import tpu as pltpu
from jax.sharding import PartitionSpec as P

NVAR = 5
NB = 4
FACE = 80
DOF = 320
LANES = 128
VEC = FACE
REST = FACE + 8
HALF = LANES - REST
BF16 = jnp.bfloat16
F32 = jnp.float32
NN = (((1,), (0,)), ((), ()))
NT = (((1,), (1,)), ((), ()))


def split(x):
    hi = x.astype(BF16)
    return hi, (x - hi.astype(F32)).astype(BF16)


def dot(a, b, dims=NN):
    ah, al = split(a)
    bh, bl = split(b)
    one = functools.partial(lax.dot_general, dimension_numbers=dims, preferred_element_type=F32)
    return one(ah, bh) + (one(ah, bl) + one(al, bh))


def pick(x, onehot, dims=NN):
    hi = x.astype(BF16)
    rest = x - hi.astype(F32)
    mid = rest.astype(BF16)
    low = (rest - mid.astype(F32)).astype(BF16)
    one = functools.partial(lax.dot_general, dimension_numbers=dims, preferred_element_type=F32)
    return one(hi, onehot) + one(mid, onehot) + one(low, onehot)


def pick2(x, onehot, dims=NN):
    hi, low = split(x)
    one = functools.partial(lax.dot_general, dimension_numbers=dims, preferred_element_type=F32)
    return one(hi, onehot) + one(low, onehot)


def stream_pick(j):
    s = np.zeros((NVAR, NB, NB * NB, FACE), np.float32)
    for v in range(NVAR):
        for q in range(NB * NB):
            s[v, j, q, v * NB * NB + q] = 1
    return s.reshape(DOF, FACE)


def span_pick(j):
    s = np.zeros((NVAR, NB, NB, NB, FACE), np.float32)
    for v in range(NVAR):
        for a in range(NB):
            for c in range(NB):
                s[v, a, j, c, (v * NB + a) * NB + c] = 1
    return s.reshape(DOF, FACE)


def stream_rows(x, j):
    step = NB * NB
    return jnp.concatenate(
        [x[(v * NB + j) * step : (v * NB + j + 1) * step] for v in range(NVAR)], axis=0
    )


def place_rows(x, j):
    step = NB * NB
    zeros = jnp.zeros((step, x.shape[1]), x.dtype)
    parts = []
    for v in range(NVAR):
        for a in range(NB):
            parts.append(x[v * step : (v + 1) * step] if a == j else zeros)
    return jnp.concatenate(parts, axis=0)


def widen(x):
    return jnp.concatenate([x, jnp.zeros((x.shape[0], LANES - x.shape[1]), x.dtype)], axis=1)


def lane_of(shape):
    return lax.broadcasted_iota(jnp.int32, shape, 1)


def pack(ab, be, d):
    lane = lane_of(ab.shape)
    left = jnp.where(lane < REST, ab, pltpu.roll(d, REST, 1))
    right = jnp.where(lane < REST, be, pltpu.roll(d, REST - HALF, 1))
    return left, right


def unpack_d(left, right):
    lane = lane_of(left.shape)
    return jnp.where(
        lane < HALF, pltpu.roll(left, LANES - REST, 1), pltpu.roll(right, LANES - REST + HALF, 1)
    )


def tall(x):
    return jnp.concatenate([x, jnp.zeros((LANES - FACE, x.shape[1]), x.dtype)], axis=0)


def compose(first, second):
    left1, right1 = first
    left2, right2 = second
    d1, d2 = unpack_d(left1, right1), unpack_d(left2, right2)
    lane = lane_of(left1.shape)
    vec = (lane >= VEC) & (lane < REST)
    through = dot(jnp.concatenate([left2, d2], axis=0), tall(left1))
    ab = through[:FACE] + jnp.where(vec, left2, 0.0)
    back = through[FACE:] + jnp.where(vec, right2, 0.0)
    both = dot(right1, tall(jnp.concatenate([right2, back], axis=1)))
    be = jnp.where(lane < VEC, both[:, :LANES], right1 + both[:, LANES:])
    return pack(ab, be, d1 + both[:, LANES:])


def blocks_kernel(inv, low, up, guess, swap, pin, pout, zin, zout, maps, lag):
    pick_in, pick_out = pin[...], pout[...]
    made = []
    for n in range(2):
        m = inv[n]
        u = up[n]
        z_in = dot(m, place_rows(low[n], 0))
        z_out = pick(m, pick_out)
        zin[n] = z_in
        zout[n] = z_out
        face = pick(guess[:, n, :], pick_in)
        down = dot(u, stream_rows(z_in, 0))
        back = dot(u, stream_rows(z_out, 0))
        made.append((-stream_rows(z_in, 3), -back, -down, dot(face, u, NT)))
    swapped = swap[...] > 0.5
    for p in range(2):
        for i in range(3):
            maps[p, i] = jnp.where(swapped, made[1 - p][i], made[p][i])
        lag[p] = jnp.where(swapped[:8], made[1 - p][3], made[p][3])


def vectors_kernel(
    inv, up, rhs, west_blk, east_blk, from_west, from_east, lag, zout, maps, swap,
    pick_w, pick_e, pin, pout, solved, out,
):
    swapped = swap[...] > 0.5
    made = []
    for n in range(2):
        m = inv[n]
        west = dot(pick(from_west[:, n, :], pick_e[...]), west_blk[n], NT)
        east = dot(pick(from_east[:, n, :], pick_w[...]), east_blk[n], NT)
        h = rhs[:, n, :] - pick(west, pick_w[...], NT) - pick(east, pick_e[...], NT)
        y = dot(h, m, NT)
        solved[n] = y
        y_in = pick(y, pin[...])
        y_out = pick(y, pout[...]) - dot(lag[n], stream_rows(zout[n], 3), NT)
        rows = jnp.zeros((VEC, FACE), F32)
        tail = jnp.zeros((LANES - REST, FACE), F32)
        b = jnp.concatenate([rows, y_out, tail], axis=0).T
        e = dot(up[n], jnp.concatenate([rows, y_in, tail], axis=0), NT)
        made.append((b, e))
    for p in range(2):
        b = jnp.where(swapped, made[1 - p][0], made[p][0])
        e = jnp.where(swapped, made[1 - p][1], made[p][1])
        left, right = pack(widen(maps[p, 0]) + b, widen(maps[p, 1]) + e, widen(maps[p, 2]))
        out[(2 * p) * FACE : (2 * p + 1) * FACE] = left
        out[(2 * p + 1) * FACE : (2 * p + 2) * FACE] = right
    out[4 * FACE :] = jnp.broadcast_to(swap[...][:1], (8, LANES))


def tiles(ref, p):
    return (
        ref[2 * p * FACE : (2 * p + 1) * FACE],
        ref[(2 * p + 1) * FACE : (2 * p + 2) * FACE],
    )


def pair_kernel(level, last, above, own, got, out):
    def put(first, second):
        s1 = first[4 * FACE : 4 * FACE + 1, :]
        s2 = second[4 * FACE : 4 * FACE + 1, :]
        w1 = s1 > 0.5
        near = [tiles(first, p) for p in range(2)]
        far = [tiles(second, p) for p in range(2)]
        both = jnp.abs(s1 - s2)
        for p in range(2):
            left2 = jnp.where(w1, far[1 - p][0], far[p][0])
            right2 = jnp.where(w1, far[1 - p][1], far[p][1])
            left, right = compose(near[p], (left2, right2))
            if last:
                lane = lane_of(left.shape)
                d = unpack_d(left, right)
                tile = jnp.where(lane < VEC, d, left)
                tile = jnp.where(lane < REST, tile, pltpu.roll(right, 8, 1))
                out[p * FACE : (p + 1) * FACE] = jnp.where(
                    lane < REST + 8, tile, jnp.broadcast_to(both, tile.shape)
                )
            else:
                out[2 * p * FACE : (2 * p + 1) * FACE] = left
                out[(2 * p + 1) * FACE : (2 * p + 2) * FACE] = right
        if not last:
            out[4 * FACE :] = jnp.broadcast_to(both, (8, LANES))

    @pl.when(above[level] == 1)
    def _():
        put(got, own)

    @pl.when(above[level] == 0)
    def _():
        put(own, got)


def down_kernel(levels, above, own_top, got_top, *rest):
    owns, gots = rest[:levels], rest[levels : 2 * levels]
    zin, zout, solved, swap, out, t_ref, c_ref = rest[2 * levels :]
    lane = lane_of((FACE, LANES))
    vec = (lane >= VEC) & (lane < REST)

    def only(x):
        return jnp.where(vec, x, 0.0)

    def top(ref, p):
        return ref[p * FACE : (p + 1) * FACE]

    def choose(flag, pair, p):
        return jnp.where(flag, pair[1 - p], pair[p])

    @pl.when(above[levels] == 1)
    def _():
        w = jnp.broadcast_to(got_top[0:1, LANES - 1 :], (1, LANES)) > 0.5
        for p in range(2):
            t_ref[p] = only(choose(w, [top(got_top, 0), top(got_top, 1)], p))
            c_ref[p] = jnp.zeros((FACE, LANES), F32)

    @pl.when(above[levels] == 0)
    def _():
        w = jnp.broadcast_to(own_top[0:1, LANES - 1 :], (1, LANES)) > 0.5
        for p in range(2):
            t_ref[p] = jnp.zeros((FACE, LANES), F32)
            far = choose(w, [top(got_top, 0), top(got_top, 1)], p)
            b = only(top(own_top, p))
            c_ref[p] = only(dot(far, tall(b)) + pltpu.roll(far, LANES - 8, 1))

    for level in reversed(range(levels)):
        own, got = owns[level], gots[level]

        @pl.when(above[level] == 1)
        def _():
            w = got[4 * FACE : 4 * FACE + 1, :] > 0.5
            t = []
            c = [c_ref[0], c_ref[1]]
            for p in range(2):
                left, _ = tiles(got, p)
                t.append(only(dot(left, tall(t_ref[p])) + left))
            for p in range(2):
                t_ref[p] = choose(w, t, p)
                c_ref[p] = choose(w, c, p)

        @pl.when(above[level] == 0)
        def _():
            w = own[4 * FACE : 4 * FACE + 1, :] > 0.5
            far = [tiles(got, p) for p in range(2)]
            for p in range(2):
                left, _ = tiles(own, p)
                mid = only(dot(left, tall(t_ref[p])) + left)
                left2 = choose(w, [far[0][0], far[1][0]], p)
                right2 = choose(w, [far[0][1], far[1][1]], p)
                c_ref[p] = only(
                    dot(unpack_d(left2, right2), tall(mid))
                    + dot(right2, tall(c_ref[p]))
                    + right2
                )

    swapped = swap[...] > 0.5
    for n in range(2):
        t = choose(swapped, [t_ref[0], t_ref[1]], n)
        c = choose(swapped, [c_ref[0], c_ref[1]], n)
        t = t.T[VEC:REST]
        c = c.T[VEC:REST]
        out[:, n, :] = solved[n] - dot(t, zin[n], NT) - dot(c, zout[n], NT)


def call(kernel, out_shape, flops=0, scratch=(), smem=False, operands=()):
    specs = [pl.BlockSpec(memory_space=pltpu.VMEM) for _ in operands]
    if smem:
        specs[0] = pl.BlockSpec(memory_space=pltpu.SMEM)
    return pl.pallas_call(
        kernel,
        out_shape=out_shape,
        in_specs=specs,
        scratch_shapes=list(scratch),
        compiler_params=pltpu.CompilerParams(vmem_limit_bytes=32 * 1024 * 1024),
    )(*operands)


def f32(*shape):
    return jax.ShapeDtypeStruct(shape, F32)


ACROSS = (1, 2, 6, 8, 16)
TOP = (6, 7, 4, 5, 2, 3, 0, 1)


def per_device(
    rhs_field, guess, inverse_diag, lower_block, upper_block, west_block, east_block, inflow_map
):
    rhs, own_guess = rhs_field[0, 0], guess[0, 0]
    inv, low, up = inverse_diag[0, 0], lower_block[0, 0], upper_block[0, 0]
    west_blk, east_blk = west_block[0, 0], east_block[0, 0]
    wide = lax.axis_size("span")
    layers = lax.axis_size("stream")
    ring = [(i, (i + 1) % wide) for i in range(wide)]
    from_west = lax.ppermute(own_guess, "span", ring)
    from_east = lax.ppermute(own_guess, "span", [(b, a) for a, b in ring])
    swap = jnp.broadcast_to(inflow_map[0, 0, 0].astype(F32), (FACE, LANES))
    place = lax.axis_index("stream")
    above = (place >> jnp.arange(6, dtype=jnp.int32)) & 1
    pin, pout = jnp.asarray(stream_pick(0), BF16), jnp.asarray(stream_pick(3), BF16)
    pick_w, pick_e = jnp.asarray(span_pick(0), BF16), jnp.asarray(span_pick(3), BF16)
    swap_map = swap[:, :FACE]
    zin, zout, maps, lag_out = call(
        blocks_kernel,
        (f32(2, DOF, FACE), f32(2, DOF, FACE), f32(2, 3, FACE, FACE), f32(2, 8, FACE)),
        operands=(inv, low, up, own_guess, swap_map, pin, pout),
    )
    lag = lax.ppermute(lag_out, "stream", [(i + 1, i) for i in range(layers - 1)])
    solved, own = call(
        vectors_kernel,
        (f32(2, 8, DOF), f32(4 * FACE + 8, LANES)),
        operands=(
            inv, up, rhs, west_blk, east_blk, from_west, from_east, lag, zout, maps, swap,
            pick_w, pick_e, pin, pout,
        ),
    )
    owns, gots = [], []
    for level, across in enumerate(ACROSS):
        got = lax.ppermute(own, "stream", [(i, i ^ across) for i in range(layers)])
        owns.append(own)
        gots.append(got)
        last = level == len(ACROSS) - 1
        own = call(
            functools.partial(pair_kernel, level, last),
            f32(2 * FACE, LANES) if last else f32(4 * FACE + 8, LANES),
            smem=True,
            operands=(above, own, got),
        )
    got = lax.ppermute(own, "stream", [(i, TOP[i // 8] * 8 + i % 8) for i in range(layers)])
    out = call(
        functools.partial(down_kernel, len(ACROSS)),
        f32(8, 2, DOF),
        smem=True,
        scratch=(pltpu.VMEM((2, FACE, LANES), F32), pltpu.VMEM((2, FACE, LANES), F32)),
        operands=(above, own, got, *owns, *gots, zin, zout, solved, swap),
    )
    return out[None, None]


def solution(mesh):
    in_specs = (
        P("stream", "span", None, None, None),
        P("stream", "span", None, None, None),
        P("stream", "span", None, None, None),
        P("stream", "span", None, None, None),
        P("stream", "span", None, None, None),
        P("stream", "span", None, None, None),
        P("stream", "span", None, None, None),
        P("stream", "span", None),
    )
    out_specs = P("stream", "span", None, None, None)
    return jax.shard_map(
        per_device, mesh=mesh, in_specs=in_specs, out_specs=out_specs, check_vma=False
    )
```

```python
import functools

import jax
import jax.numpy as jnp
import numpy as np
from jax import lax
from jax.experimental import pallas as pl
from jax.experimental.pallas import tpu as pltpu
from jax.sharding import PartitionSpec as P

NVAR = 5
NB = 4
FACE = 80
DOF = 320
LANES = 128
VEC = FACE
REST = FACE + 8
HALF = LANES - REST
BF16 = jnp.bfloat16
F32 = jnp.float32
NN = (((1,), (0,)), ((), ()))
NT = (((1,), (1,)), ((), ()))


def split(x):
    hi = x.astype(BF16)
    return hi, (x - hi.astype(F32)).astype(BF16)


def dot(a, b, dims=NN):
    ah, al = split(a)
    bh, bl = split(b)
    one = functools.partial(lax.dot_general, dimension_numbers=dims, preferred_element_type=F32)
    return one(ah, bh) + (one(ah, bl) + one(al, bh))


def pick(x, onehot, dims=NN):
    hi = x.astype(BF16)
    rest = x - hi.astype(F32)
    mid = rest.astype(BF16)
    low = (rest - mid.astype(F32)).astype(BF16)
    one = functools.partial(lax.dot_general, dimension_numbers=dims, preferred_element_type=F32)
    return one(hi, onehot) + one(mid, onehot) + one(low, onehot)


def put(onehot, x):
    hi = x.astype(BF16)
    rest = x - hi.astype(F32)
    mid = rest.astype(BF16)
    low = (rest - mid.astype(F32)).astype(BF16)
    one = functools.partial(lax.dot_general, dimension_numbers=NN, preferred_element_type=F32)
    return one(onehot, hi) + one(onehot, mid) + one(onehot, low)


def stream_pick(j):
    s = np.zeros((NVAR, NB, NB * NB, FACE), np.float32)
    for v in range(NVAR):
        for q in range(NB * NB):
            s[v, j, q, v * NB * NB + q] = 1
    return s.reshape(DOF, FACE)


def span_pick(j):
    s = np.zeros((NVAR, NB, NB, NB, FACE), np.float32)
    for v in range(NVAR):
        for a in range(NB):
            for c in range(NB):
                s[v, a, j, c, (v * NB + a) * NB + c] = 1
    return s.reshape(DOF, FACE)


def stream_rows(x, j):
    step = NB * NB
    return jnp.concatenate(
        [x[(v * NB + j) * step : (v * NB + j + 1) * step] for v in range(NVAR)], axis=0
    )


def place_rows(x, j):
    step = NB * NB
    zeros = jnp.zeros((step, x.shape[1]), x.dtype)
    parts = []
    for v in range(NVAR):
        for a in range(NB):
            parts.append(x[v * step : (v + 1) * step] if a == j else zeros)
    return jnp.concatenate(parts, axis=0)


def lane_of(shape):
    return lax.broadcasted_iota(jnp.int32, shape, 1)


def pack(ab, be, d):
    lane = lane_of(ab.shape)
    left = jnp.where(lane < REST, ab, pltpu.roll(d, REST, 1))
    right = jnp.where(lane < REST, be, pltpu.roll(d, REST - HALF, 1))
    return left, right


def unpack_d(left, right):
    lane = lane_of(left.shape)
    return jnp.where(
        lane < HALF, pltpu.roll(left, LANES - REST, 1), pltpu.roll(right, LANES - REST + HALF, 1)
    )


def tall(x):
    return jnp.concatenate([x, jnp.zeros((LANES - FACE, x.shape[1]), x.dtype)], axis=0)


def widen(x):
    return jnp.concatenate([x, jnp.zeros((x.shape[0], LANES - x.shape[1]), x.dtype)], axis=1)


def side(x):
    x = widen(x)
    before = jnp.zeros((VEC, LANES), x.dtype)
    after = jnp.zeros((LANES - REST, LANES), x.dtype)
    return jnp.concatenate([before, x, after], axis=0)


def vec_only(x):
    lane = lane_of(x.shape)
    return jnp.where((lane >= VEC) & (lane < REST), x, 0.0)


class Segment:
    def __init__(self, left, right, swap):
        self.left, self.right, self.swap = left, right, swap

    @staticmethod
    def of(ref):
        left = [ref[2 * p * FACE : (2 * p + 1) * FACE] for p in range(2)]
        right = [ref[(2 * p + 1) * FACE : (2 * p + 2) * FACE] for p in range(2)]
        return Segment(left, right, ref[4 * FACE :])

    def write(self, ref):
        for p in range(2):
            ref[2 * p * FACE : (2 * p + 1) * FACE] = self.left[p]
            ref[(2 * p + 1) * FACE : (2 * p + 2) * FACE] = self.right[p]
        ref[4 * FACE :] = self.swap

    def top(self, ref):
        for p in range(2):
            left, right = self.left[p], self.right[p]
            lane = lane_of(left.shape)
            tile = jnp.where(lane < VEC, unpack_d(left, right), left)
            tile = jnp.where(lane < REST, tile, pltpu.roll(right, 8, 1))
            ref[p * FACE : (p + 1) * FACE] = jnp.where(lane < REST + 8, tile, self.swap[:1])


def behind(swap, pair, p):
    return jnp.where(swap[:1] > 0.5, pair[1 - p], pair[p])


def join(first, second):
    lefts, rights = [], []
    for p in range(2):
        left1, right1 = first.left[p], first.right[p]
        left2, right2 = behind(first.swap, second.left, p), behind(first.swap, second.right, p)
        d1, d2 = unpack_d(left1, right1), unpack_d(left2, right2)
        lane = lane_of(left1.shape)
        through = dot(jnp.concatenate([left2, d2], axis=0), tall(left1))
        ab = through[:FACE] + vec_only(left2)
        back = through[FACE:] + vec_only(right2)
        both = dot(right1, tall(jnp.concatenate([right2, back], axis=1)))
        be = jnp.where(lane < VEC, both[:, :LANES], right1 + both[:, LANES:])
        left, right = pack(ab, be, d1 + both[:, LANES:])
        lefts.append(left)
        rights.append(right)
    return Segment(lefts, rights, jnp.abs(first.swap - second.swap))


def ordered(upper, own, got):
    up = upper[...][:1] > 0.5

    def pair(a, b):
        return jnp.where(up, a, b)

    def seg(a, b):
        return Segment(
            [pair(a.left[p], b.left[p]) for p in range(2)],
            [pair(a.right[p], b.right[p]) for p in range(2)],
            pair(a.swap, b.swap),
        )

    return seg(got, own), seg(own, got)


def fetch(pairs, sems):
    copies = [pltpu.make_async_copy(a, b, sems.at[i]) for i, (a, b) in enumerate(pairs)]
    for copy in copies:
        copy.start()
    for copy in copies:
        copy.wait()


def faces_kernel(guess_hbm, up_hbm, map_hbm, pin, pw, pe, west, east, lag, swap, guess, up, which, sems):
    fetch([(guess_hbm, guess), (up_hbm, up), (map_hbm, which)], sems)
    flag = jnp.full((8, LANES), which[0, 0, 0].astype(F32), F32)
    swap[...] = flag
    swapped = flag[:, :FACE] > 0.5
    made = []
    for n in range(2):
        mine = guess[0, 0, :, n, :]
        west[n] = pick(mine, pw[...])
        east[n] = pick(mine, pe[...])
        made.append(dot(pick(mine, pin[...]), up[0, 0, n], NT))
    for p in range(2):
        lag[p] = jnp.where(swapped, made[1 - p], made[p])


def maps_kernel(
    inv_hbm, low_hbm, up_hbm, west_hbm, east_hbm, rhs_hbm, swap, pout, pw, pe,
    own, zin, zout, zwest, zeast, kwest, keast, solved,
    inv, low, up, west, east, rhs, sems,
):
    fetch(
        [(inv_hbm, inv), (low_hbm, low), (up_hbm, up), (west_hbm, west), (east_hbm, east), (rhs_hbm, rhs)],
        sems,
    )
    made = []
    for n in range(2):
        m, u = inv[0, 0, n], up[0, 0, n]
        sides = jnp.concatenate(
            [
                widen(place_rows(low[0, 0, n], 0)),
                widen(put(pw[...], west[0, 0, n])),
                widen(put(pe[...], east[0, 0, n])),
            ],
            axis=1,
        )
        z = dot(m, sides)
        z_in, z_west, z_east = z[:, :LANES], z[:, LANES : 2 * LANES], z[:, 2 * LANES :]
        z_out = pick(m, pout[...])
        zin[n], zout[n], zwest[n], zeast[n] = z_in, z_out, z_west, z_east
        coupled = dot(
            u, jnp.concatenate([stream_rows(a, 0) for a in (z_in, z_out, z_west, z_east)], axis=1)
        )
        kwest[n] = coupled[:, 2 * LANES : 3 * LANES]
        keast[n] = coupled[:, 3 * LANES :]
        y = dot(rhs[0, 0, :, n, :], m, NT)
        solved[n] = y
        y_in, y_out = [
            jnp.concatenate(
                [y[:, (v * NB + j) * NB * NB : (v * NB + j + 1) * NB * NB] for v in range(NVAR)], axis=1
            )
            for j in (0, 3)
        ]
        b = side(y_out).T[:FACE]
        e = dot(u, side(y_in)[:, :FACE], NT)
        made.append(pack(b - stream_rows(z_in, 3), e - coupled[:, LANES : 2 * LANES], -coupled[:, :LANES]))
    flag = swap[...]
    Segment(
        [behind(flag, [made[0][0], made[1][0]], p) for p in range(2)],
        [behind(flag, [made[0][1], made[1][1]], p) for p in range(2)],
        flag,
    ).write(own)


def vectors_kernel(maps, zout, zwest, zeast, kwest, keast, from_west, from_east, lag, own):
    seg = Segment.of(maps)
    b, e = [], []
    for n in range(2):
        far_west, far_east = side(from_west[n]), side(from_east[n])
        into = jnp.concatenate([stream_rows(z[n], 3) for z in (zwest, zeast, zout)], axis=1)
        b.append(dot(into, jnp.concatenate([far_west, far_east, side(lag[n])], axis=1), NT))
        back = jnp.concatenate([kwest[n], keast[n]], axis=1)
        e.append(dot(back, jnp.concatenate([far_west, far_east], axis=1), NT))
    Segment(
        [seg.left[p] - behind(seg.swap, b, p) for p in range(2)],
        [seg.right[p] - behind(seg.swap, e, p) for p in range(2)],
        seg.swap,
    ).write(own)


def pair_kernel(last, upper, own, got, out):
    both = join(*ordered(upper, Segment.of(own), Segment.of(got)))
    if last:
        both.top(out)
    else:
        both.write(out)


def four_kernel(got, out, halves):
    halves_of = [join(Segment.of(got.at[2 * i]), Segment.of(got.at[2 * i + 1])) for i in range(2)]
    join(*halves_of).write(out)
    for i in range(2):
        halves_of[i].write(halves.at[i])


def start_place():
    eye = (lax.broadcasted_iota(jnp.int32, (FACE, LANES), 0) == lane_of((FACE, LANES))).astype(F32)
    zero = jnp.zeros((FACE, LANES), F32)
    return [[eye, zero, eye] for _ in range(2)]


def widen_place(place, upper, own, got):
    lane = lane_of((FACE, LANES))
    keep = lane < REST
    up = upper[:1] > 0.5
    made = []
    for p in range(2):
        near = [behind(got.swap, [place[0][i], place[1][i]], p) for i in range(3)]
        sib = tall(got.left[p])
        moved = dot(jnp.concatenate([near[0], near[1]], axis=0), sib)
        above = [
            jnp.where(keep, moved[:FACE], 0.0) + vec_only(near[0]),
            jnp.where(keep, moved[FACE:], 0.0) + vec_only(near[1]),
            near[2],
        ]
        left2, right2 = behind(own.swap, got.left, p), behind(own.swap, got.right, p)
        back = dot(unpack_d(left2, right2), tall(own.left[p])) + vec_only(right2)
        turned = dot(place[p][2], tall(jnp.concatenate([back, right2], axis=1)))
        below = [
            place[p][0],
            place[p][1] + jnp.where(keep, turned[:, :LANES], 0.0),
            jnp.where(lane < VEC, turned[:, LANES:], 0.0),
        ]
        made.append([jnp.where(up, above[i], below[i]) for i in range(3)])
    return made


def read_place(ref):
    return [[ref[p, i] for i in range(3)] for p in range(2)]


def write_place(ref, place):
    for p in range(2):
        for i in range(3):
            ref[p, i] = place[p][i]


def first_place_kernel(upper, own, got, out, swap_out):
    mine, other = Segment.of(own), Segment.of(got)
    write_place(out, widen_place(start_place(), upper[...], mine, other))
    swap_out[...] = jnp.abs(mine.swap - jnp.where(upper[...] > 0.5, other.swap, 0.0))


def place_kernel(upper, own, got, place, swap, out, swap_out):
    mine, other = Segment.of(own), Segment.of(got)
    write_place(out, widen_place(read_place(place), upper[...], mine, other))
    swap_out[...] = jnp.abs(swap[...] - jnp.where(upper[...] > 0.5, other.swap, 0.0))


def four_place_kernel(at, uppers, got, halves, place, swap, out, swap_out):
    j = at[0]
    half = j // 2
    mine, other = Segment.of(got.at[j]), Segment.of(got.at[j + 1 - 2 * (j - 2 * half)])
    made = widen_place(read_place(place), uppers[0], mine, other)
    x = jnp.abs(swap[...] - jnp.where(uppers[0] > 0.5, other.swap, 0.0))
    mine, other = Segment.of(halves.at[half]), Segment.of(halves.at[1 - half])
    write_place(out, widen_place(made, uppers[1], mine, other))
    swap_out[...] = jnp.abs(x - jnp.where(uppers[1] > 0.5, other.swap, 0.0))


def answer_kernel(
    upper, own, got, place, swap, zin, zout, zwest, zeast, from_west, from_east, solved,
    fixed, free, turn,
):
    mine, other = Segment.of(own), Segment.of(got)
    made = widen_place(read_place(place), upper[0], mine, other)
    x = jnp.abs(swap[...] - jnp.where(upper[0] > 0.5, other.swap, 0.0))
    turn[...] = x
    up = upper[1][:1] > 0.5
    for n in range(2):
        p0, q0, r0 = [behind(x, [made[0][i], made[1][i]], n) for i in range(3)]
        t = jnp.where(up, p0, vec_only(p0))
        c = jnp.where(up, q0, jnp.where(lane_of(r0.shape) < VEC, r0, 0.0) + vec_only(q0))
        f = dot(jnp.concatenate([zin[n], zout[n]], axis=1), jnp.concatenate([tall(t), tall(c)], axis=0))
        free[n] = f
        sides = jnp.concatenate([widen(from_west[n]), widen(from_east[n])], axis=1)
        fixed[n] = (
            solved[n]
            - dot(sides, jnp.concatenate([zwest[n], zeast[n]], axis=1), NT)
            - f.T[VEC:REST]
        )


def last_kernel(upper, swap, own, got, fixed, free, out):
    up = upper[...][:1] > 0.5
    mine = [own[p * FACE : (p + 1) * FACE] for p in range(2)]
    far = [got[p * FACE : (p + 1) * FACE] for p in range(2)]
    own_swap = jnp.broadcast_to(mine[0][:1, LANES - 1 :], (1, LANES))
    far_swap = jnp.broadcast_to(far[0][:1, LANES - 1 :], (1, LANES))
    unknown = []
    for p in range(2):
        above = behind(far_swap, far, p)
        sib = behind(own_swap, far, p)
        below = dot(sib, tall(vec_only(mine[p]))) + pltpu.roll(sib, LANES - 8, 1)
        unknown.append(jnp.where(up, above, below).T[VEC:REST])
    for n in range(2):
        x = widen(behind(swap[...][:, :FACE], unknown, n))
        out[:, n, :] = fixed[n] - dot(x, free[n], NT)


ANY = pl.BlockSpec(memory_space=pl.ANY)
VMEM = pl.BlockSpec(memory_space=pltpu.VMEM)
SMEM = pl.BlockSpec(memory_space=pltpu.SMEM)


def call(kernel, out_shape, *operands, any_first=0, smem_first=0, scratch=(), flops=0):
    specs = [ANY if i < any_first else SMEM if i < smem_first else VMEM for i in range(len(operands))]
    several = isinstance(out_shape, tuple)
    return pl.pallas_call(
        kernel,
        out_shape=out_shape,
        in_specs=specs,
        out_specs=tuple(VMEM for _ in out_shape) if several else VMEM,
        scratch_shapes=list(scratch),
        cost_estimate=pl.CostEstimate(flops=flops, bytes_accessed=1 << 20, transcendentals=0),
        compiler_params=pltpu.CompilerParams(vmem_limit_bytes=24 * 1024 * 1024),
    )(*operands)


def f32(*shape):
    return jax.ShapeDtypeStruct(shape, F32)


ROWS = 4 * FACE + 8
TOP = (6, 7, 4, 5, 2, 3, 0, 1)


def per_device(
    rhs_field, guess, inverse_diag, lower_block, upper_block, west_block, east_block, inflow_map
):
    wide = lax.axis_size("span")
    layers = lax.axis_size("stream")
    place = lax.axis_index("stream")
    bits = (place >> jnp.arange(6, dtype=jnp.int32)) & 1
    upper = jnp.broadcast_to(bits.astype(F32)[:, None, None], (6, 8, LANES))
    pin, pout = jnp.asarray(stream_pick(0), BF16), jnp.asarray(np.pad(stream_pick(3), ((0, 0), (0, LANES - FACE))), BF16)
    pw, pe = jnp.asarray(span_pick(0), BF16), jnp.asarray(span_pick(3), BF16)
    dma = pltpu.SemaphoreType.DMA
    west_face, east_face, lag_out, swap = call(
        faces_kernel,
        (f32(2, 8, FACE), f32(2, 8, FACE), f32(2, 8, FACE), f32(8, LANES)),
        guess, upper_block, inflow_map, pin, pw, pe,
        any_first=3,
        scratch=(
            pltpu.VMEM(guess.shape, F32), pltpu.VMEM(upper_block.shape, F32),
            pltpu.SMEM(inflow_map.shape, jnp.int32), dma((3,)),
        ),
    )
    ring = [(i, (i + 1) % wide) for i in range(wide)]
    from_west = lax.ppermute(east_face, "span", ring)
    from_east = lax.ppermute(west_face, "span", [(b, a) for a, b in ring])
    lag = lax.ppermute(lag_out, "stream", [(i + 1, i) for i in range(layers - 1)])
    maps, zin, zout, zwest, zeast, kwest, keast, solved = call(
        maps_kernel,
        (
            f32(ROWS, LANES), *(f32(2, DOF, LANES) for _ in range(4)),
            f32(2, FACE, LANES), f32(2, FACE, LANES), f32(2, 8, DOF),
        ),
        inverse_diag, lower_block, upper_block, west_block, east_block, rhs_field, swap, pout, pw, pe,
        any_first=6,
        scratch=(
            *(pltpu.VMEM(a.shape, F32) for a in (inverse_diag, lower_block, upper_block, west_block, east_block, rhs_field)),
            dma((6,)),
        ),
    )
    own = call(
        vectors_kernel, f32(ROWS, LANES),
        maps, zout, zwest, zeast, kwest, keast, from_west, from_east, lag,
    )

    def across(x, distance):
        return lax.ppermute(x, "stream", [(i, i ^ distance) for i in range(layers)])

    got = across(own, 1)
    pair = call(functools.partial(pair_kernel, False), f32(ROWS, LANES), upper[0], own, got)
    here = (f32(2, 3, FACE, LANES), f32(8, LANES))
    spot, turn = call(first_place_kernel, here, upper[0], own, got)
    groups = [[8 * g + c + 2 * j for j in range(4)] for g in range(layers // 8) for c in range(2)]
    four = lax.all_to_all(
        jnp.broadcast_to(pair[None], (4, ROWS, LANES)), "stream", 0, 0, axis_index_groups=groups
    )
    eight, halves = call(four_kernel, (f32(ROWS, LANES), f32(2, ROWS, LANES)), four)
    got = across(eight, 8)
    spot, turn = call(
        four_place_kernel, here,
        ((place >> 1) & 3).reshape(1), upper[1:3], four, halves, spot, turn,
        smem_first=1,
    )
    got, spot, turn = lax.optimization_barrier((got, spot, turn))
    sixteen = call(functools.partial(pair_kernel, False), f32(ROWS, LANES), upper[3], eight, got)
    got2 = across(sixteen, 16)
    spot, turn = call(place_kernel, here, upper[3], eight, got, spot, turn)
    got2, spot, turn = lax.optimization_barrier((got2, spot, turn))
    half = call(functools.partial(pair_kernel, True), f32(2 * FACE, LANES), upper[4], sixteen, got2)
    got3 = lax.ppermute(half, "stream", [(i, TOP[i // 8] * 8 + i % 8) for i in range(layers)])
    fixed, free, turn = call(
        answer_kernel, (f32(2, 8, DOF), f32(2, DOF, LANES), f32(8, LANES)),
        upper[4:6], sixteen, got2, spot, turn, zin, zout, zwest, zeast, from_west, from_east, solved,
    )
    out = call(last_kernel, f32(8, 2, DOF), upper[5], turn, half, got3, fixed, free)
    return out[None, None]


def solution(mesh):
    in_specs = (
        P("stream", "span", None, None, None),
        P("stream", "span", None, None, None),
        P("stream", "span", None, None, None),
        P("stream", "span", None, None, None),
        P("stream", "span", None, None, None),
        P("stream", "span", None, None, None),
        P("stream", "span", None, None, None),
        P("stream", "span", None),
    )
    out_specs = P("stream", "span", None, None, None)
    return jax.shard_map(
        per_device, mesh=mesh, in_specs=in_specs, out_specs=out_specs, check_vma=False
    )
```

```python
import functools

import jax
import jax.numpy as jnp
from jax import lax
from jax.experimental import pallas as pl
from jax.experimental.pallas import tpu as pltpu
from jax.sharding import PartitionSpec as P

NVAR = 5
NB = 4
FACE = 80
DOF = 320
LANES = 128
VEC = FACE
REST = FACE + 8
HALF = LANES - REST
BF16 = jnp.bfloat16
F32 = jnp.float32
NN = (((1,), (0,)), ((), ()))
NT = (((1,), (1,)), ((), ()))


def split(x):
    hi = x.astype(BF16)
    return hi, (x - hi.astype(F32)).astype(BF16)


def dot(a, b, dims=NN):
    ah, al = split(a)
    bh, bl = split(b)
    one = functools.partial(lax.dot_general, dimension_numbers=dims, preferred_element_type=F32)
    return one(ah, bh) + (one(ah, bl) + one(al, bh))


def pick(x, onehot, dims=NN):
    hi = x.astype(BF16).astype(F32)
    mid = (x - hi).astype(BF16).astype(F32)
    low = x - hi - mid
    rows = x.shape[0]
    parts = jnp.concatenate([hi, mid, low], axis=0).astype(BF16)
    made = lax.dot_general(parts, onehot, dimension_numbers=dims, preferred_element_type=F32)
    return made[:rows] + made[rows : 2 * rows] + made[2 * rows :]


def stream_pick(j, width=FACE):
    d = lax.broadcasted_iota(jnp.int32, (DOF, width), 0)
    f = lax.broadcasted_iota(jnp.int32, (DOF, width), 1)
    step = NB * NB
    return ((d == (f // step) * (NB * step) + j * step + f % step) & (f < FACE)).astype(F32).astype(BF16)


def span_pick(j, width=FACE):
    d = lax.broadcasted_iota(jnp.int32, (DOF, width), 0)
    f = lax.broadcasted_iota(jnp.int32, (DOF, width), 1)
    return ((d == (f // NB) * (NB * NB) + j * NB + f % NB) & (f < FACE)).astype(F32).astype(BF16)


def stream_rows(x, j):
    step = NB * NB
    return jnp.concatenate(
        [x[(v * NB + j) * step : (v * NB + j + 1) * step] for v in range(NVAR)], axis=0
    )


def place_rows(x, j):
    step = NB * NB
    zeros = jnp.zeros((step, x.shape[1]), x.dtype)
    parts = []
    for v in range(NVAR):
        for a in range(NB):
            parts.append(x[v * step : (v + 1) * step] if a == j else zeros)
    return jnp.concatenate(parts, axis=0)


def lane_of(shape):
    return lax.broadcasted_iota(jnp.int32, shape, 1)


def pack(ab, be, d):
    lane = lane_of(ab.shape)
    left = jnp.where(lane < REST, ab, pltpu.roll(d, REST, 1))
    right = jnp.where(lane < REST, be, pltpu.roll(d, REST - HALF, 1))
    return left, right


def unpack_d(left, right):
    lane = lane_of(left.shape)
    return jnp.where(
        lane < HALF, pltpu.roll(left, LANES - REST, 1), pltpu.roll(right, LANES - REST + HALF, 1)
    )


def tall(x):
    return jnp.concatenate([x, jnp.zeros((LANES - FACE, x.shape[1]), x.dtype)], axis=0)


def widen(x):
    return jnp.concatenate([x, jnp.zeros((x.shape[0], LANES - x.shape[1]), x.dtype)], axis=1)


def side(x):
    x = widen(x)
    before = jnp.zeros((VEC, LANES), x.dtype)
    after = jnp.zeros((LANES - REST, LANES), x.dtype)
    return jnp.concatenate([before, x, after], axis=0)


def vec_only(x):
    lane = lane_of(x.shape)
    return jnp.where((lane >= VEC) & (lane < REST), x, 0.0)


class Segment:
    def __init__(self, left, right, swap):
        self.left, self.right, self.swap = left, right, swap

    @staticmethod
    def of(ref):
        left = [ref[2 * p * FACE : (2 * p + 1) * FACE] for p in range(2)]
        right = [ref[(2 * p + 1) * FACE : (2 * p + 2) * FACE] for p in range(2)]
        return Segment(left, right, ref[4 * FACE : 4 * FACE + 8])

    def write(self, ref):
        for p in range(2):
            ref[2 * p * FACE : (2 * p + 1) * FACE] = self.left[p]
            ref[(2 * p + 1) * FACE : (2 * p + 2) * FACE] = self.right[p]
        ref[4 * FACE : 4 * FACE + 8] = self.swap

    def top(self, ref):
        for p in range(2):
            left, right = self.left[p], self.right[p]
            lane = lane_of(left.shape)
            tile = jnp.where(lane < VEC, unpack_d(left, right), left)
            tile = jnp.where(lane < REST, tile, pltpu.roll(right, 8, 1))
            ref[p * FACE : (p + 1) * FACE] = jnp.where(lane < REST + 8, tile, self.swap[:1])


def tails_of(ref):
    return [ref[ROWS + p * FACE : ROWS + (p + 1) * FACE] for p in range(2)]


def write_tails(ref, tails):
    for p in range(2):
        ref[ROWS + p * FACE : ROWS + (p + 1) * FACE] = tails[p]


def lagged_left(seg, tails, after):
    return [seg.left[p] - vec_only(dot(tails[p], tall(behind(seg.swap, after, p)))) for p in range(2)]


def behind(swap, pair, p):
    return jnp.where(swap[:1] > 0.5, pair[1 - p], pair[p])


def join(first, second):
    lefts, rights = [], []
    for p in range(2):
        left1, right1 = first.left[p], first.right[p]
        left2, right2 = behind(first.swap, second.left, p), behind(first.swap, second.right, p)
        d1, d2 = unpack_d(left1, right1), unpack_d(left2, right2)
        lane = lane_of(left1.shape)
        through = dot(jnp.concatenate([left2, d2], axis=0), tall(left1))
        ab = through[:FACE] + vec_only(left2)
        back = through[FACE:] + vec_only(right2)
        both = dot(right1, tall(jnp.concatenate([right2, back], axis=1)))
        be = jnp.where(lane < VEC, both[:, :LANES], right1 + both[:, LANES:])
        left, right = pack(ab, be, d1 + both[:, LANES:])
        lefts.append(left)
        rights.append(right)
    return Segment(lefts, rights, jnp.abs(first.swap - second.swap))


def ordered(upper, own, got):
    up = upper[:1] > 0.5

    def pair(a, b):
        return jnp.where(up, a, b)

    def seg(a, b):
        return Segment(
            [pair(a.left[p], b.left[p]) for p in range(2)],
            [pair(a.right[p], b.right[p]) for p in range(2)],
            pair(a.swap, b.swap),
        )

    return seg(got, own), seg(own, got)


def fetch(pairs, sems):
    copies = [pltpu.make_async_copy(a, b, sems.at[i]) for i, (a, b) in enumerate(pairs)]
    for copy in copies:
        copy.start()
    for copy in copies:
        copy.wait()


def columns_of(rows):
    before = jnp.zeros((VEC, DOF), F32)
    after = jnp.zeros((LANES - REST, DOF), F32)
    return jnp.concatenate([before, rows, after], axis=0).T


def make_maps(inv, low, up, rhs, coupled, flag, own):
    tables = jnp.concatenate([span_pick(0, LANES), span_pick(3, LANES), stream_pick(3, LANES)], axis=1)
    lane = lane_of((FACE, LANES))
    made, corners = [], []
    for n in range(2):
        m, u = inv[0, 0, n], up[0, 0, n]
        both = jnp.concatenate([stream_rows(m, 3), dot(u, stream_rows(m, 0))], axis=0)
        z = dot(both, widen(place_rows(low[0, 0, n], 0)) + columns_of(rhs[0, 0, :, n, :]))
        cut = pick(both, tables)
        for i in range(2):
            at = LONG + (2 * n + i) * 2 * FACE
            own[at : at + 2 * FACE] = cut[:, i * LANES : (i + 1) * LANES]
        corners.append(cut[:FACE, 2 * LANES :])
        ahead, down = z[:FACE], z[FACE:]
        made.append(
            pack(
                jnp.where(lane < VEC, -ahead, ahead),
                jnp.where(lane < VEC, -cut[FACE:, 2 * LANES :], down),
                -down,
            )
        )
    Segment(
        [behind(flag, [made[0][0], made[1][0]], p) for p in range(2)],
        [behind(flag, [made[0][1], made[1][1]], p) for p in range(2)],
        flag,
    ).write(own)
    write_tails(own, [behind(flag, corners, p) + side(coupled[p]).T[:FACE] for p in range(2)])


def flag_of(which):
    return jnp.full((8, LANES), which[0, 0, 0].astype(F32), F32)


def faces_kernel(
    guess_hbm, up_hbm, map_hbm, place, west, east, lag, swap, upper, guess, up, which, sems
):
    copies = [
        pltpu.make_async_copy(a, b, sems.at[i])
        for i, (a, b) in enumerate([(guess_hbm, guess), (up_hbm, up), (map_hbm, which)])
    ]
    for copy in copies:
        copy.start()
    for level in range(LEVELS):
        bit = (place[0] >> level) & 1
        upper[level] = jnp.full((8, LANES), bit.astype(F32), F32)
    tables = jnp.concatenate([stream_pick(0, LANES), span_pick(0, LANES), span_pick(3, LANES)], axis=1)
    for copy in copies:
        copy.wait()
    both = pick(jnp.concatenate([guess[0, 0, :, n, :] for n in range(2)], axis=0), tables)
    flag = flag_of(which)
    swap[...] = flag
    swapped = flag[:, :FACE] > 0.5
    made = []
    for n in range(2):
        mine = both[8 * n : 8 * n + 8]
        west[n] = mine[:, LANES : LANES + FACE]
        east[n] = mine[:, 2 * LANES : 2 * LANES + FACE]
        made.append(dot(mine[:, :FACE], up[0, 0, n], NT))
    for p in range(2):
        lag[p] = jnp.where(swapped, made[1 - p], made[p])


def maps_kernel(inv_hbm, low_hbm, up_hbm, rhs_hbm, ahead, swap, own, inv, low, up, rhs, sems):
    fetch([(inv_hbm, inv), (low_hbm, low), (up_hbm, up), (rhs_hbm, rhs)], sems)
    make_maps(inv, low, up, rhs, ahead, swap[...], own)


def vectors_kernel(maps, west, east, from_west, from_east, relayed, own, terms):
    b, e = [], []
    for n in range(2):
        from_w = dot(from_west[n], west[0, 0, n], NT)
        from_e = dot(from_east[n], east[0, 0, n], NT)
        terms[0, 8 * n : 8 * n + 8] = from_w
        terms[1, 8 * n : 8 * n + 8] = from_e
        far = jnp.concatenate([side(from_w), side(from_e)], axis=1)
        at = LONG + 2 * n * 2 * FACE
        cuts = jnp.concatenate([maps[at + i * 2 * FACE : at + (i + 1) * 2 * FACE] for i in range(2)], axis=1)
        both = dot(cuts, far, NT)
        b.append(both[:FACE])
        e.append(both[FACE:])
    seg = Segment.of(maps)
    Segment(
        [seg.left[p] - behind(seg.swap, b, p) for p in range(2)],
        [seg.right[p] - behind(seg.swap, e, p) for p in range(2)],
        seg.swap,
    ).write(own)
    tails = tails_of(maps)
    write_tails(own, [tails[p] + pltpu.roll(side(relayed[p]).T[:FACE], 8, 1) for p in range(2)])


def rest_kernel(inv_hbm, low_hbm, rhs_hbm, terms, zin, zout, base, inv, low, rhs, sems):
    fetch([(inv_hbm, inv), (low_hbm, low), (rhs_hbm, rhs)], sems)
    pout = stream_pick(3, LANES)
    lane = lane_of((DOF, LANES))
    halo = pick(terms[0], span_pick(0), NT) + pick(terms[1], span_pick(3), NT)
    for n in range(2):
        m = inv[0, 0, n]
        h = rhs[0, 0, :, n, :] - halo[8 * n : 8 * n + 8]
        z = dot(m, widen(place_rows(low[0, 0, n], 0)) + columns_of(h))
        zout[n] = pick(m, pout)
        zin[n] = jnp.where(lane < VEC, z, 0.0)
        base[n] = vec_only(z)


def pair_kernel(level, form, upper, own, got, out):
    both = join(*ordered(upper[level], Segment.of(own), Segment.of(got)))
    if form == "top":
        both.top(out)
    else:
        both.write(out)


def first_pair_kernel(upper, own, got, out, lefts):
    first, second = ordered(upper[0], Segment.of(own), Segment.of(got))
    up = upper[0][:1] > 0.5
    mine, other = tails_of(own), tails_of(got)
    tails1 = [jnp.where(up, other[p], mine[p]) for p in range(2)]
    tails2 = [jnp.where(up, mine[p], other[p]) for p in range(2)]
    first = Segment(lagged_left(first, tails1, tails2), first.right, first.swap)
    both = join(first, second)
    lane = lane_of((FACE, LANES))
    tails = [jnp.where(lane < VEC, behind(first.swap, tails2, p), tails1[p]) for p in range(2)]
    for p in range(2):
        lefts[p] = first.left[p]
    both.write(out)
    write_tails(out, tails)


def four_kernel(got, out, halves, parts):
    tails = [tails_of(got.at[i]) for i in range(4)]
    last = [pltpu.roll(tails[0][p], LANES - 8, 1) for p in range(2)]
    segs = []
    for i in range(4):
        seg = Segment.of(got.at[i])
        seg = Segment(lagged_left(seg, tails[i], tails[i + 1] if i < 3 else last), seg.right, seg.swap)
        seg.write(parts.at[i])
        segs.append(seg)
    both = [join(segs[2 * i], segs[2 * i + 1]) for i in range(2)]
    join(*both).write(out)
    for i in range(2):
        both[i].write(halves.at[i])


def start_place():
    eye = (lax.broadcasted_iota(jnp.int32, (FACE, LANES), 0) == lane_of((FACE, LANES))).astype(F32)
    zero = jnp.zeros((FACE, LANES), F32)
    return [[eye, zero, eye] for _ in range(2)]


def widen_place(place, upper, own, got):
    lane = lane_of((FACE, LANES))
    keep = lane < REST
    up = upper[:1] > 0.5
    made = []
    for p in range(2):
        near = [behind(got.swap, [place[0][i], place[1][i]], p) for i in range(3)]
        sib = tall(got.left[p])
        moved = dot(jnp.concatenate([near[0], near[1]], axis=0), sib)
        above = [
            jnp.where(keep, moved[:FACE], 0.0) + vec_only(near[0]),
            jnp.where(keep, moved[FACE:], 0.0) + vec_only(near[1]),
            near[2],
        ]
        left2, right2 = behind(own.swap, got.left, p), behind(own.swap, got.right, p)
        back = dot(unpack_d(left2, right2), tall(own.left[p])) + vec_only(right2)
        turned = dot(place[p][2], tall(jnp.concatenate([back, right2], axis=1)))
        below = [
            place[p][0],
            place[p][1] + jnp.where(keep, turned[:, :LANES], 0.0),
            jnp.where(lane < VEC, turned[:, LANES:], 0.0),
        ]
        made.append([jnp.where(up, above[i], below[i]) for i in range(3)])
    return made


def read_place(ref):
    return [[ref[p, i] for i in range(3)] for p in range(2)]


def write_place(ref, place):
    for p in range(2):
        for i in range(3):
            ref[p, i] = place[p][i]


def place_kernel(level, upper, own, got, place, swap, out, swap_out):
    mine, other = Segment.of(own), Segment.of(got)
    write_place(out, widen_place(read_place(place), upper[level], mine, other))
    swap_out[...] = jnp.abs(swap[...] - jnp.where(upper[level] > 0.5, other.swap, 0.0))


def four_place_kernel(at, upper, one, one_got, lefts, got, halves, out, swap_out):
    mine, other = Segment.of(one), Segment.of(one_got)
    up = upper[0][:1] > 0.5
    mine.left = [jnp.where(up, mine.left[p], lefts[p]) for p in range(2)]
    other.left = [jnp.where(up, lefts[p], other.left[p]) for p in range(2)]
    made = widen_place(start_place(), upper[0], mine, other)
    x = jnp.abs(mine.swap - jnp.where(upper[0] > 0.5, other.swap, 0.0))
    j = (at[0] >> 1) & 3
    half = j >> 1
    mine, other = Segment.of(got.at[j]), Segment.of(got.at[j ^ 1])
    made = widen_place(made, upper[1], mine, other)
    x = jnp.abs(x - jnp.where(upper[1] > 0.5, other.swap, 0.0))
    mine, other = Segment.of(halves.at[half]), Segment.of(halves.at[1 - half])
    write_place(out, widen_place(made, upper[2], mine, other))
    swap_out[...] = jnp.abs(x - jnp.where(upper[2] > 0.5, other.swap, 0.0))


def answer_kernel(upper, own, got, place, swap, zin, zout, base, fixed, free, turn):
    mine, other = Segment.of(own), Segment.of(got)
    made = widen_place(read_place(place), upper[4], mine, other)
    x = jnp.abs(swap[...] - jnp.where(upper[4] > 0.5, other.swap, 0.0))
    turn[...] = x
    up = upper[5][:1] > 0.5
    for n in range(2):
        p0, q0, r0 = [behind(x, [made[0][i], made[1][i]], n) for i in range(3)]
        t = jnp.where(up, p0, vec_only(p0))
        c = jnp.where(up, q0, jnp.where(lane_of(r0.shape) < VEC, r0, 0.0) + vec_only(q0))
        f = dot(jnp.concatenate([zin[n], zout[n]], axis=1), jnp.concatenate([tall(t), tall(c)], axis=0))
        free[n] = f
        fixed[n] = (base[n] - f).T[VEC:REST]


def last_kernel(upper, swap, own, got, fixed, free, out):
    up = upper[5][:1] > 0.5
    mine = [own[p * FACE : (p + 1) * FACE] for p in range(2)]
    far = [got[p * FACE : (p + 1) * FACE] for p in range(2)]
    own_swap = jnp.broadcast_to(mine[0][:1, LANES - 1 :], (1, LANES))
    far_swap = jnp.broadcast_to(far[0][:1, LANES - 1 :], (1, LANES))
    unknown = []
    for p in range(2):
        above = behind(far_swap, far, p)
        sib = behind(own_swap, far, p)
        below = dot(sib, tall(vec_only(mine[p]))) + pltpu.roll(sib, LANES - 8, 1)
        unknown.append(jnp.where(up, above, below).T[VEC:REST])
    for n in range(2):
        x = widen(behind(swap[...][:, :FACE], unknown, n))
        out[:, n, :] = fixed[n] - dot(x, free[n], NT)


HBM = pl.BlockSpec(memory_space=pltpu.HBM)
VMEM = pl.BlockSpec(memory_space=pltpu.VMEM)
SMEM = pl.BlockSpec(memory_space=pltpu.SMEM)


def call(kernel, out_shape, *operands, hbm=(), smem=(), scratch=(), flops=0):
    specs = [HBM if i in hbm else SMEM if i in smem else VMEM for i in range(len(operands))]
    several = isinstance(out_shape, tuple)
    operands = [
        pltpu.with_memory_space_constraint(x, pltpu.HBM) if i in hbm else x for i, x in enumerate(operands)
    ]
    return pl.pallas_call(
        kernel,
        out_shape=out_shape,
        in_specs=specs,
        out_specs=tuple(VMEM for _ in out_shape) if several else VMEM,
        scratch_shapes=list(scratch),
        cost_estimate=pl.CostEstimate(flops=flops, bytes_accessed=1 << 20, transcendentals=0),
        compiler_params=pltpu.CompilerParams(vmem_limit_bytes=24 * 1024 * 1024),
    )(*operands)


def f32(*shape):
    return jax.ShapeDtypeStruct(shape, F32)


LEVELS = 6
ROWS = 4 * FACE + 8
LONG = ROWS + 2 * FACE
TOP = (6, 7, 4, 5, 2, 3, 0, 1)


def per_device(
    rhs_field, guess, inverse_diag, lower_block, upper_block, west_block, east_block, inflow_map
):
    wide = lax.axis_size("span")
    layers = lax.axis_size("stream")
    place = lax.axis_index("stream").astype(jnp.int32).reshape(1)
    dma = pltpu.SemaphoreType.DMA

    def room(*arrays):
        held = [
            pltpu.SMEM(a.shape, a.dtype) if a.dtype == jnp.int32 else pltpu.VMEM(a.shape, F32) for a in arrays
        ]
        return (*held, dma((len(arrays),)))

    face = f32(2, 8, FACE)
    args = (guess, upper_block, inflow_map)
    west_face, east_face, ahead, swap, upper = call(
        faces_kernel, (face, face, face, f32(8, LANES), f32(LEVELS, 8, LANES)), *args, place,
        hbm=range(3), smem=(3,), scratch=room(*args),
    )
    ring = [(i, (i + 1) % wide) for i in range(wide)]
    from_west = lax.ppermute(east_face, "span", ring)
    from_east = lax.ppermute(west_face, "span", [(b, a) for a, b in ring])
    relayed = lax.ppermute(ahead, "stream", [(i + 8, i) for i in range(0, layers - 8, 8)])
    args = (inverse_diag, lower_block, upper_block, rhs_field)
    maps = call(
        maps_kernel, f32(LONG + 8 * FACE, LANES), *args, ahead, swap, hbm=range(4), scratch=room(*args)
    )
    own, terms = call(
        vectors_kernel, (f32(LONG, LANES), f32(2, 16, FACE)),
        maps, west_block, east_block, from_west, from_east, relayed,
    )

    def across(x, distance):
        return lax.ppermute(x, "stream", [(i, i ^ distance) for i in range(layers)])

    got = across(own, 1)
    pairs, lefts = call(
        first_pair_kernel, (f32(LONG, LANES), f32(2, FACE, LANES)), upper, own, got
    )
    groups = [[8 * g + c + 2 * j for j in range(4)] for g in range(layers // 8) for c in range(2)]
    four = lax.all_gather(pairs, "stream", axis_index_groups=groups)
    eight, halves, parts = call(
        four_kernel, (f32(ROWS, LANES), f32(2, ROWS, LANES), f32(4, ROWS, LANES)), four
    )
    here = (f32(2, 3, FACE, LANES), f32(8, LANES))
    got8 = across(eight, 8)
    spot, turn = call(four_place_kernel, here, place, upper, own, got, lefts, parts, halves, smem=(0,))
    got8, spot, turn = lax.optimization_barrier((got8, spot, turn))
    sixteen = call(functools.partial(pair_kernel, 3, ""), f32(ROWS, LANES), upper, eight, got8)
    got16 = across(sixteen, 16)
    args = (inverse_diag, lower_block, rhs_field)
    terms, sixteen = lax.optimization_barrier((terms, sixteen))
    zin, zout, base = call(
        rest_kernel, tuple(f32(2, DOF, LANES) for _ in range(3)), *args, terms,
        hbm=range(3), scratch=room(*args),
    )
    spot, turn = call(functools.partial(place_kernel, 3), here, upper, eight, got8, spot, turn)
    got16, spot, turn, zin, zout, base = lax.optimization_barrier((got16, spot, turn, zin, zout, base))
    half = call(functools.partial(pair_kernel, 4, "top"), f32(2 * FACE, LANES), upper, sixteen, got16)
    got32 = lax.ppermute(half, "stream", [(i, TOP[i // 8] * 8 + i % 8) for i in range(layers)])
    fixed, free, turn = call(
        answer_kernel, (f32(2, 8, DOF), f32(2, DOF, LANES), f32(8, LANES)),
        upper, sixteen, got16, spot, turn, zin, zout, base,
    )
    out = call(last_kernel, f32(8, 2, DOF), upper, turn, half, got32, fixed, free)
    return out[None, None]


def solution(mesh):
    in_specs = (
        P("stream", "span", None, None, None),
        P("stream", "span", None, None, None),
        P("stream", "span", None, None, None),
        P("stream", "span", None, None, None),
        P("stream", "span", None, None, None),
        P("stream", "span", None, None, None),
        P("stream", "span", None, None, None),
        P("stream", "span", None),
    )
    out_specs = P("stream", "span", None, None, None)
    return jax.shard_map(
        per_device, mesh=mesh, in_specs=in_specs, out_specs=out_specs, check_vma=False
    )
```

```python
import functools

import jax
import jax.numpy as jnp
from jax import lax
from jax.experimental import pallas as pl
from jax.experimental.pallas import tpu as pltpu
from jax.sharding import PartitionSpec as P

NVAR = 5
NB = 4
FACE = 80
DOF = 320
LANES = 128
VEC = FACE
REST = FACE + 8
HALF = LANES - REST
BF16 = jnp.bfloat16
F32 = jnp.float32
NN = (((1,), (0,)), ((), ()))
NT = (((1,), (1,)), ((), ()))


def split(x):
    hi = x.astype(BF16)
    return hi, (x - hi.astype(F32)).astype(BF16)


def dot(a, b, dims=NN):
    ah, al = split(a)
    bh, bl = split(b)
    one = functools.partial(lax.dot_general, dimension_numbers=dims, preferred_element_type=F32)
    return one(ah, bh) + (one(ah, bl) + one(al, bh))


def pick(x, onehot, dims=NN):
    hi = x.astype(BF16).astype(F32)
    mid = (x - hi).astype(BF16).astype(F32)
    low = x - hi - mid
    rows = x.shape[0]
    parts = jnp.concatenate([hi, mid, low], axis=0).astype(BF16)
    made = lax.dot_general(parts, onehot, dimension_numbers=dims, preferred_element_type=F32)
    return made[:rows] + made[rows : 2 * rows] + made[2 * rows :]


def stream_pick(j, width=FACE):
    d = lax.broadcasted_iota(jnp.int32, (DOF, width), 0)
    f = lax.broadcasted_iota(jnp.int32, (DOF, width), 1)
    step = NB * NB
    return ((d == (f // step) * (NB * step) + j * step + f % step) & (f < FACE)).astype(F32).astype(BF16)


def span_pick(j, width=FACE):
    d = lax.broadcasted_iota(jnp.int32, (DOF, width), 0)
    f = lax.broadcasted_iota(jnp.int32, (DOF, width), 1)
    return ((d == (f // NB) * (NB * NB) + j * NB + f % NB) & (f < FACE)).astype(F32).astype(BF16)


def stream_rows(x, j):
    step = NB * NB
    return jnp.concatenate(
        [x[(v * NB + j) * step : (v * NB + j + 1) * step] for v in range(NVAR)], axis=0
    )


def place_rows(x, j):
    step = NB * NB
    zeros = jnp.zeros((step, x.shape[1]), x.dtype)
    parts = []
    for v in range(NVAR):
        for a in range(NB):
            parts.append(x[v * step : (v + 1) * step] if a == j else zeros)
    return jnp.concatenate(parts, axis=0)


def lane_of(shape):
    return lax.broadcasted_iota(jnp.int32, shape, 1)


def pack(ab, be, d):
    lane = lane_of(ab.shape)
    left = jnp.where(lane < REST, ab, pltpu.roll(d, REST, 1))
    right = jnp.where(lane < REST, be, pltpu.roll(d, REST - HALF, 1))
    return left, right


def unpack_d(left, right):
    lane = lane_of(left.shape)
    return jnp.where(
        lane < HALF, pltpu.roll(left, LANES - REST, 1), pltpu.roll(right, LANES - REST + HALF, 1)
    )


def tall(x):
    return jnp.concatenate([x, jnp.zeros((LANES - FACE, x.shape[1]), x.dtype)], axis=0)


def widen(x):
    return jnp.concatenate([x, jnp.zeros((x.shape[0], LANES - x.shape[1]), x.dtype)], axis=1)


def side(x):
    x = widen(x)
    before = jnp.zeros((VEC, LANES), x.dtype)
    after = jnp.zeros((LANES - REST, LANES), x.dtype)
    return jnp.concatenate([before, x, after], axis=0)


def vec_only(x):
    lane = lane_of(x.shape)
    return jnp.where((lane >= VEC) & (lane < REST), x, 0.0)


class Segment:
    def __init__(self, left, right, swap):
        self.left, self.right, self.swap = left, right, swap

    @staticmethod
    def of(ref):
        left = [ref[2 * p * FACE : (2 * p + 1) * FACE] for p in range(2)]
        right = [ref[(2 * p + 1) * FACE : (2 * p + 2) * FACE] for p in range(2)]
        return Segment(left, right, ref[4 * FACE : 4 * FACE + 8])

    def write(self, ref):
        for p in range(2):
            ref[2 * p * FACE : (2 * p + 1) * FACE] = self.left[p]
            ref[(2 * p + 1) * FACE : (2 * p + 2) * FACE] = self.right[p]
        ref[4 * FACE : 4 * FACE + 8] = self.swap

    def top(self, ref):
        for p in range(2):
            left, right = self.left[p], self.right[p]
            lane = lane_of(left.shape)
            tile = jnp.where(lane < VEC, unpack_d(left, right), left)
            tile = jnp.where(lane < REST, tile, pltpu.roll(right, 8, 1))
            ref[p * FACE : (p + 1) * FACE] = jnp.where(lane < REST + 8, tile, self.swap[:1])


def tails_of(ref):
    return [ref[ROWS + p * FACE : ROWS + (p + 1) * FACE] for p in range(2)]


def write_tails(ref, tails):
    for p in range(2):
        ref[ROWS + p * FACE : ROWS + (p + 1) * FACE] = tails[p]


def lagged_left(seg, tails, after):
    return [seg.left[p] - vec_only(dot(tails[p], tall(behind(seg.swap, after, p)))) for p in range(2)]


def behind(swap, pair, p):
    return jnp.where(swap[:1] > 0.5, pair[1 - p], pair[p])


def join(first, second):
    lefts, rights = [], []
    for p in range(2):
        left1, right1 = first.left[p], first.right[p]
        left2, right2 = behind(first.swap, second.left, p), behind(first.swap, second.right, p)
        d1, d2 = unpack_d(left1, right1), unpack_d(left2, right2)
        lane = lane_of(left1.shape)
        through = dot(jnp.concatenate([left2, d2], axis=0), tall(left1))
        ab = through[:FACE] + vec_only(left2)
        back = through[FACE:] + vec_only(right2)
        both = dot(right1, tall(jnp.concatenate([right2, back], axis=1)))
        be = jnp.where(lane < VEC, both[:, :LANES], right1 + both[:, LANES:])
        left, right = pack(ab, be, d1 + both[:, LANES:])
        lefts.append(left)
        rights.append(right)
    return Segment(lefts, rights, jnp.abs(first.swap - second.swap))


def ordered(upper, own, got):
    up = upper[:1] > 0.5

    def pair(a, b):
        return jnp.where(up, a, b)

    def seg(a, b):
        return Segment(
            [pair(a.left[p], b.left[p]) for p in range(2)],
            [pair(a.right[p], b.right[p]) for p in range(2)],
            pair(a.swap, b.swap),
        )

    return seg(got, own), seg(own, got)


def fetch(pairs, sems):
    copies = [pltpu.make_async_copy(a, b, sems.at[i]) for i, (a, b) in enumerate(pairs)]
    for copy in copies:
        copy.start()
    for copy in copies:
        copy.wait()


def columns_of(rows):
    before = jnp.zeros((VEC, DOF), F32)
    after = jnp.zeros((LANES - REST, DOF), F32)
    return jnp.concatenate([before, rows, after], axis=0).T


def make_maps(inv, low, up, rhs, coupled, flag, own):
    tables = jnp.concatenate([span_pick(0, LANES), span_pick(3, LANES), stream_pick(3, LANES)], axis=1)
    lane = lane_of((FACE, LANES))
    made, corners = [], []
    for n in range(2):
        m, u = inv[0, 0, n], up[0, 0, n]
        both = jnp.concatenate([stream_rows(m, 3), dot(u, stream_rows(m, 0))], axis=0)
        z = dot(both, widen(place_rows(low[0, 0, n], 0)) + columns_of(rhs[0, 0, :, n, :]))
        cut = pick(both, tables)
        for i in range(2):
            at = LONG + (2 * n + i) * 2 * FACE
            own[at : at + 2 * FACE] = cut[:, i * LANES : (i + 1) * LANES]
        corners.append(cut[:FACE, 2 * LANES :])
        ahead, down = z[:FACE], z[FACE:]
        made.append(
            pack(
                jnp.where(lane < VEC, -ahead, ahead),
                jnp.where(lane < VEC, -cut[FACE:, 2 * LANES :], down),
                -down,
            )
        )
    Segment(
        [behind(flag, [made[0][0], made[1][0]], p) for p in range(2)],
        [behind(flag, [made[0][1], made[1][1]], p) for p in range(2)],
        flag,
    ).write(own)
    write_tails(own, [behind(flag, corners, p) + side(coupled[p]).T[:FACE] for p in range(2)])


def flag_of(which):
    return jnp.full((8, LANES), which[0, 0, 0].astype(F32), F32)


def faces_kernel(
    guess_hbm, up_hbm, map_hbm, place, along, near, far, lag, swap, upper, guess, up, which, sems
):
    copies = [
        pltpu.make_async_copy(a, b, sems.at[i])
        for i, (a, b) in enumerate([(guess_hbm, guess), (up_hbm, up), (map_hbm, which)])
    ]
    for copy in copies:
        copy.start()
    for level in range(LEVELS):
        bit = (place[0] >> level) & 1
        upper[level] = jnp.full((8, LANES), bit.astype(F32), F32)
    upper[LEVELS] = jnp.full((8, LANES), (along[0] & 1).astype(F32), F32)
    odd = upper[LEVELS][:, :FACE] > 0.5
    tables = jnp.concatenate([stream_pick(0, LANES), span_pick(0, LANES), span_pick(3, LANES)], axis=1)
    for copy in copies:
        copy.wait()
    both = pick(jnp.concatenate([guess[0, 0, :, n, :] for n in range(2)], axis=0), tables)
    flag = flag_of(which)
    swap[...] = flag
    swapped = flag[:, :FACE] > 0.5
    made = []
    for n in range(2):
        mine = both[8 * n : 8 * n + 8]
        west = mine[:, LANES : LANES + FACE]
        east = mine[:, 2 * LANES : 2 * LANES + FACE]
        near[n] = jnp.where(odd, west, east)
        far[n] = jnp.where(odd, east, west)
        made.append(dot(mine[:, :FACE], up[0, 0, n], NT))
    for p in range(2):
        lag[p] = jnp.where(swapped, made[1 - p], made[p])


def maps_kernel(inv_hbm, low_hbm, up_hbm, rhs_hbm, ahead, swap, own, inv, low, up, rhs, sems):
    fetch([(inv_hbm, inv), (low_hbm, low), (up_hbm, up), (rhs_hbm, rhs)], sems)
    make_maps(inv, low, up, rhs, ahead, swap[...], own)


def vectors_kernel(maps, west, east, upper, from_near, from_far, relayed, own, terms):
    odd = upper[LEVELS][:, :FACE] > 0.5
    b, e = [], []
    for n in range(2):
        from_w = dot(jnp.where(odd, from_near[n], from_far[n]), west[0, 0, n], NT)
        from_e = dot(jnp.where(odd, from_far[n], from_near[n]), east[0, 0, n], NT)
        terms[0, 8 * n : 8 * n + 8] = from_w
        terms[1, 8 * n : 8 * n + 8] = from_e
        sides = jnp.concatenate([side(from_w), side(from_e)], axis=1)
        at = LONG + 2 * n * 2 * FACE
        cuts = jnp.concatenate([maps[at + i * 2 * FACE : at + (i + 1) * 2 * FACE] for i in range(2)], axis=1)
        both = dot(cuts, sides, NT)
        b.append(both[:FACE])
        e.append(both[FACE:])
    seg = Segment.of(maps)
    Segment(
        [seg.left[p] - behind(seg.swap, b, p) for p in range(2)],
        [seg.right[p] - behind(seg.swap, e, p) for p in range(2)],
        seg.swap,
    ).write(own)
    write_tails(own, tails_of(maps))


def rest_kernel(inv_hbm, low_hbm, rhs_hbm, terms, zin, zout, base, inv, low, rhs, sems):
    fetch([(inv_hbm, inv), (low_hbm, low), (rhs_hbm, rhs)], sems)
    pout = stream_pick(3, LANES)
    lane = lane_of((DOF, LANES))
    halo = pick(terms[0], span_pick(0), NT) + pick(terms[1], span_pick(3), NT)
    for n in range(2):
        m = inv[0, 0, n]
        h = rhs[0, 0, :, n, :] - halo[8 * n : 8 * n + 8]
        z = dot(m, widen(place_rows(low[0, 0, n], 0)) + columns_of(h))
        zout[n] = pick(m, pout)
        zin[n] = jnp.where(lane < VEC, z, 0.0)
        base[n] = vec_only(z)


def pair_kernel(level, form, upper, own, got, out):
    both = join(*ordered(upper[level], Segment.of(own), Segment.of(got)))
    if form == "top":
        both.top(out)
    else:
        both.write(out)


def first_pair_kernel(upper, own, got, relayed, out, lefts):
    first, second = ordered(upper[0], Segment.of(own), Segment.of(got))
    up = upper[0][:1] > 0.5
    mine, other = tails_of(own), tails_of(got)
    tails1 = [jnp.where(up, other[p], mine[p]) for p in range(2)]
    tails2 = [jnp.where(up, mine[p], other[p]) for p in range(2)]
    first = Segment(lagged_left(first, tails1, tails2), first.right, first.swap)
    both = join(first, second)
    lane = lane_of((FACE, LANES))
    tails = [jnp.where(lane < VEC, behind(first.swap, tails2, p), tails1[p]) for p in range(2)]
    behind_eight = sum(pltpu.roll(side(relayed[p]).T[:FACE], 8 * (p + 1), 1) for p in range(2))
    for p in range(2):
        lefts[p] = first.left[p]
    for i, pair in enumerate((both.left, both.right, tails)):
        out[i * FACE : (i + 1) * FACE] = jnp.where(up, pair[1], pair[0]) + (behind_eight if i == 2 else 0.0)
    out[3 * FACE :] = both.swap


def four_kernel(got, out, halves, parts):
    def chain(i, p, tile):
        return got[2 * i + p, tile * FACE : (tile + 1) * FACE]

    tails = [[chain(i, p, 2) for p in range(2)] for i in range(4)]
    last = [pltpu.roll(tails[0][0], LANES - 8 * (p + 1), 1) for p in range(2)]
    segs = []
    for i in range(4):
        seg = Segment([chain(i, p, 0) for p in range(2)], [chain(i, p, 1) for p in range(2)], got[2 * i, 3 * FACE :])
        seg = Segment(lagged_left(seg, tails[i], tails[i + 1] if i < 3 else last), seg.right, seg.swap)
        seg.write(parts.at[i])
        segs.append(seg)
    both = [join(segs[2 * i], segs[2 * i + 1]) for i in range(2)]
    join(*both).write(out)
    for i in range(2):
        both[i].write(halves.at[i])


def start_place():
    eye = (lax.broadcasted_iota(jnp.int32, (FACE, LANES), 0) == lane_of((FACE, LANES))).astype(F32)
    zero = jnp.zeros((FACE, LANES), F32)
    return [[eye, zero, eye] for _ in range(2)]


def widen_place(place, upper, own, got):
    lane = lane_of((FACE, LANES))
    keep = lane < REST
    up = upper[:1] > 0.5
    made = []
    for p in range(2):
        near = [behind(got.swap, [place[0][i], place[1][i]], p) for i in range(3)]
        sib = tall(got.left[p])
        moved = dot(jnp.concatenate([near[0], near[1]], axis=0), sib)
        above = [
            jnp.where(keep, moved[:FACE], 0.0) + vec_only(near[0]),
            jnp.where(keep, moved[FACE:], 0.0) + vec_only(near[1]),
            near[2],
        ]
        left2, right2 = behind(own.swap, got.left, p), behind(own.swap, got.right, p)
        back = dot(unpack_d(left2, right2), tall(own.left[p])) + vec_only(right2)
        turned = dot(place[p][2], tall(jnp.concatenate([back, right2], axis=1)))
        below = [
            place[p][0],
            place[p][1] + jnp.where(keep, turned[:, :LANES], 0.0),
            jnp.where(lane < VEC, turned[:, LANES:], 0.0),
        ]
        made.append([jnp.where(up, above[i], below[i]) for i in range(3)])
    return made


def read_place(ref):
    return [[ref[p, i] for i in range(3)] for p in range(2)]


def write_place(ref, place):
    for p in range(2):
        for i in range(3):
            ref[p, i] = place[p][i]


def place_kernel(level, upper, own, got, place, swap, out, swap_out):
    mine, other = Segment.of(own), Segment.of(got)
    write_place(out, widen_place(read_place(place), upper[level], mine, other))
    swap_out[...] = jnp.abs(swap[...] - jnp.where(upper[level] > 0.5, other.swap, 0.0))


def four_place_kernel(at, upper, one, one_got, lefts, got, halves, out, swap_out):
    mine, other = Segment.of(one), Segment.of(one_got)
    up = upper[0][:1] > 0.5
    mine.left = [jnp.where(up, mine.left[p], lefts[p]) for p in range(2)]
    other.left = [jnp.where(up, lefts[p], other.left[p]) for p in range(2)]
    made = widen_place(start_place(), upper[0], mine, other)
    x = jnp.abs(mine.swap - jnp.where(upper[0] > 0.5, other.swap, 0.0))
    j = (at[0] >> 1) & 3
    half = j >> 1
    mine, other = Segment.of(got.at[j]), Segment.of(got.at[j ^ 1])
    made = widen_place(made, upper[1], mine, other)
    x = jnp.abs(x - jnp.where(upper[1] > 0.5, other.swap, 0.0))
    mine, other = Segment.of(halves.at[half]), Segment.of(halves.at[1 - half])
    write_place(out, widen_place(made, upper[2], mine, other))
    swap_out[...] = jnp.abs(x - jnp.where(upper[2] > 0.5, other.swap, 0.0))


def answer_kernel(upper, own, got, place, swap, zin, zout, base, fixed, free, turn):
    mine, other = Segment.of(own), Segment.of(got)
    made = widen_place(read_place(place), upper[4], mine, other)
    x = jnp.abs(swap[...] - jnp.where(upper[4] > 0.5, other.swap, 0.0))
    turn[...] = x
    up = upper[5][:1] > 0.5
    for n in range(2):
        p0, q0, r0 = [behind(x, [made[0][i], made[1][i]], n) for i in range(3)]
        t = jnp.where(up, p0, vec_only(p0))
        c = jnp.where(up, q0, jnp.where(lane_of(r0.shape) < VEC, r0, 0.0) + vec_only(q0))
        f = dot(jnp.concatenate([zin[n], zout[n]], axis=1), jnp.concatenate([tall(t), tall(c)], axis=0))
        free[n] = f
        fixed[n] = (base[n] - f).T[VEC:REST]


def last_kernel(upper, swap, own, got, fixed, free, out):
    up = upper[5][:1] > 0.5
    mine = [own[p * FACE : (p + 1) * FACE] for p in range(2)]
    far = [got[p * FACE : (p + 1) * FACE] for p in range(2)]
    own_swap = jnp.broadcast_to(mine[0][:1, LANES - 1 :], (1, LANES))
    far_swap = jnp.broadcast_to(far[0][:1, LANES - 1 :], (1, LANES))
    unknown = []
    for p in range(2):
        above = behind(far_swap, far, p)
        sib = behind(own_swap, far, p)
        below = dot(sib, tall(vec_only(mine[p]))) + pltpu.roll(sib, LANES - 8, 1)
        unknown.append(jnp.where(up, above, below).T[VEC:REST])
    for n in range(2):
        x = widen(behind(swap[...][:, :FACE], unknown, n))
        out[:, n, :] = fixed[n] - dot(x, free[n], NT)


HBM = pl.BlockSpec(memory_space=pltpu.HBM)
VMEM = pl.BlockSpec(memory_space=pltpu.VMEM)
SMEM = pl.BlockSpec(memory_space=pltpu.SMEM)


def call(kernel, out_shape, *operands, hbm=(), smem=(), scratch=(), moved=1 << 20):
    specs = [HBM if i in hbm else SMEM if i in smem else VMEM for i in range(len(operands))]
    several = isinstance(out_shape, tuple)
    operands = [
        pltpu.with_memory_space_constraint(x, pltpu.HBM) if i in hbm else x for i, x in enumerate(operands)
    ]
    return pl.pallas_call(
        kernel,
        out_shape=out_shape,
        in_specs=specs,
        out_specs=tuple(VMEM for _ in out_shape) if several else VMEM,
        scratch_shapes=list(scratch),
        cost_estimate=pl.CostEstimate(flops=0, bytes_accessed=moved, transcendentals=0),
        compiler_params=pltpu.CompilerParams(vmem_limit_bytes=24 * 1024 * 1024),
    )(*operands)


def f32(*shape):
    return jax.ShapeDtypeStruct(shape, F32)


LEVELS = 6
ROWS = 4 * FACE + 8
LONG = ROWS + 2 * FACE
TOP = (6, 7, 4, 5, 2, 3, 0, 1)


def per_device(
    rhs_field, guess, inverse_diag, lower_block, upper_block, west_block, east_block, inflow_map
):
    wide = lax.axis_size("span")
    layers = lax.axis_size("stream")
    place = lax.axis_index("stream").astype(jnp.int32).reshape(1)
    along = lax.axis_index("span").astype(jnp.int32).reshape(1)
    dma = pltpu.SemaphoreType.DMA

    def room(*arrays):
        held = [
            pltpu.SMEM(a.shape, a.dtype) if a.dtype == jnp.int32 else pltpu.VMEM(a.shape, F32) for a in arrays
        ]
        return (*held, dma((len(arrays),)))

    face = f32(2, 8, FACE)
    args = (guess, upper_block, inflow_map)
    near_face, far_face, ahead, swap, upper = call(
        faces_kernel, (face, face, face, f32(8, LANES), f32(LEVELS + 1, 8, LANES)), *args, place, along,
        hbm=range(3), smem=(3, 4), scratch=room(*args),
    )
    from_near = lax.ppermute(near_face, "span", [(i, i ^ 1) for i in range(wide)])
    from_far = lax.ppermute(far_face, "span", [(i, (i - 1 + 2 * (i & 1)) % wide) for i in range(wide)])
    args = (inverse_diag, lower_block, upper_block, rhs_field)
    maps = call(
        maps_kernel, f32(LONG + 8 * FACE, LANES), *args, ahead, swap,
        hbm=range(4), scratch=room(*args), moved=0,
    )
    relayed = lax.ppermute(ahead, "stream", [(i + 8, i) for i in range(0, layers - 8, 8)])
    own, terms = call(
        vectors_kernel, (f32(LONG, LANES), f32(2, 16, FACE)),
        maps, west_block, east_block, upper, from_near, from_far, relayed,
    )

    def across(x, distance):
        return lax.ppermute(x, "stream", [(i, i ^ distance) for i in range(layers)])

    got = across(own, 1)
    chain, lefts = call(
        first_pair_kernel, (f32(3 * FACE + 8, LANES), f32(2, FACE, LANES)), upper, own, got, relayed
    )
    groups = [[8 * g + j for j in range(8)] for g in range(layers // 8)]
    chains = lax.all_gather(chain, "stream", axis_index_groups=groups)
    eight, halves, parts = call(
        four_kernel, (f32(ROWS, LANES), f32(2, ROWS, LANES), f32(4, ROWS, LANES)), chains
    )
    here = (f32(2, 3, FACE, LANES), f32(8, LANES))
    got8 = across(eight, 8)
    spot, turn = call(four_place_kernel, here, place, upper, own, got, lefts, parts, halves, smem=(0,))
    got8, spot, turn = lax.optimization_barrier((got8, spot, turn))
    sixteen = call(functools.partial(pair_kernel, 3, ""), f32(ROWS, LANES), upper, eight, got8)
    got16 = across(sixteen, 16)
    args = (inverse_diag, lower_block, rhs_field)
    terms, sixteen = lax.optimization_barrier((terms, sixteen))
    zin, zout, base = call(
        rest_kernel, tuple(f32(2, DOF, LANES) for _ in range(3)), *args, terms,
        hbm=range(3), scratch=room(*args),
    )
    spot, turn = call(functools.partial(place_kernel, 3), here, upper, eight, got8, spot, turn)
    got16, spot, turn, zin, zout, base = lax.optimization_barrier((got16, spot, turn, zin, zout, base))
    half = call(functools.partial(pair_kernel, 4, "top"), f32(2 * FACE, LANES), upper, sixteen, got16)
    got32 = lax.ppermute(half, "stream", [(i, TOP[i // 8] * 8 + i % 8) for i in range(layers)])
    fixed, free, turn = call(
        answer_kernel, (f32(2, 8, DOF), f32(2, DOF, LANES), f32(8, LANES)),
        upper, sixteen, got16, spot, turn, zin, zout, base,
    )
    out = call(last_kernel, f32(8, 2, DOF), upper, turn, half, got32, fixed, free)
    return out[None, None]


def solution(mesh):
    in_specs = (
        P("stream", "span", None, None, None),
        P("stream", "span", None, None, None),
        P("stream", "span", None, None, None),
        P("stream", "span", None, None, None),
        P("stream", "span", None, None, None),
        P("stream", "span", None, None, None),
        P("stream", "span", None, None, None),
        P("stream", "span", None),
    )
    out_specs = P("stream", "span", None, None, None)
    return jax.shard_map(
        per_device, mesh=mesh, in_specs=in_specs, out_specs=out_specs, check_vma=False
    )
```

```python
import functools

import jax
import jax.numpy as jnp
from jax import lax
from jax.experimental import pallas as pl
from jax.experimental.pallas import tpu as pltpu
from jax.sharding import PartitionSpec as P

NVAR = 5
NB = 4
FACE = 80
DOF = 320
LANES = 128
VEC = FACE
REST = FACE + 8
HALF = LANES - REST
BF16 = jnp.bfloat16
F32 = jnp.float32
NN = (((1,), (0,)), ((), ()))
NT = (((1,), (1,)), ((), ()))


def split(x):
    hi = x.astype(BF16)
    return hi, (x - hi.astype(F32)).astype(BF16)


def dot(a, b, dims=NN):
    ah, al = split(a)
    bh, bl = split(b)
    one = functools.partial(lax.dot_general, dimension_numbers=dims, preferred_element_type=F32)
    return one(ah, bh) + (one(ah, bl) + one(al, bh))


def pick(x, onehot, dims=NN):
    hi = x.astype(BF16).astype(F32)
    mid = (x - hi).astype(BF16).astype(F32)
    low = x - hi - mid
    rows = x.shape[0]
    parts = jnp.concatenate([hi, mid, low], axis=0).astype(BF16)
    made = lax.dot_general(parts, onehot, dimension_numbers=dims, preferred_element_type=F32)
    return made[:rows] + made[rows : 2 * rows] + made[2 * rows :]


def stream_pick(j, width=FACE):
    d = lax.broadcasted_iota(jnp.int32, (DOF, width), 0)
    f = lax.broadcasted_iota(jnp.int32, (DOF, width), 1)
    step = NB * NB
    return ((d == (f // step) * (NB * step) + j * step + f % step) & (f < FACE)).astype(F32).astype(BF16)


def span_pick(j, width=FACE):
    d = lax.broadcasted_iota(jnp.int32, (DOF, width), 0)
    f = lax.broadcasted_iota(jnp.int32, (DOF, width), 1)
    return ((d == (f // NB) * (NB * NB) + j * NB + f % NB) & (f < FACE)).astype(F32).astype(BF16)


def stream_rows(x, j):
    step = NB * NB
    return jnp.concatenate(
        [x[(v * NB + j) * step : (v * NB + j + 1) * step] for v in range(NVAR)], axis=0
    )


def place_rows(x, j):
    step = NB * NB
    zeros = jnp.zeros((step, x.shape[1]), x.dtype)
    parts = []
    for v in range(NVAR):
        for a in range(NB):
            parts.append(x[v * step : (v + 1) * step] if a == j else zeros)
    return jnp.concatenate(parts, axis=0)


def lane_of(shape):
    return lax.broadcasted_iota(jnp.int32, shape, 1)


def pack(ab, be, d):
    lane = lane_of(ab.shape)
    left = jnp.where(lane < REST, ab, pltpu.roll(d, REST, 1))
    right = jnp.where(lane < REST, be, pltpu.roll(d, REST - HALF, 1))
    return left, right


def unpack_d(left, right):
    lane = lane_of(left.shape)
    return jnp.where(
        lane < HALF, pltpu.roll(left, LANES - REST, 1), pltpu.roll(right, LANES - REST + HALF, 1)
    )


def tall(x):
    return jnp.concatenate([x, jnp.zeros((LANES - FACE, x.shape[1]), x.dtype)], axis=0)


def widen(x):
    return jnp.concatenate([x, jnp.zeros((x.shape[0], LANES - x.shape[1]), x.dtype)], axis=1)


def side(x):
    x = widen(x)
    before = jnp.zeros((VEC, LANES), x.dtype)
    after = jnp.zeros((LANES - REST, LANES), x.dtype)
    return jnp.concatenate([before, x, after], axis=0)


def vec_only(x):
    lane = lane_of(x.shape)
    return jnp.where((lane >= VEC) & (lane < REST), x, 0.0)


class Segment:
    def __init__(self, left, right, swap):
        self.left, self.right, self.swap = left, right, swap

    @staticmethod
    def of(ref):
        left = [ref[2 * p * FACE : (2 * p + 1) * FACE] for p in range(2)]
        right = [ref[(2 * p + 1) * FACE : (2 * p + 2) * FACE] for p in range(2)]
        return Segment(left, right, ref[4 * FACE : 4 * FACE + 8])

    def write(self, ref):
        for p in range(2):
            ref[2 * p * FACE : (2 * p + 1) * FACE] = self.left[p]
            ref[(2 * p + 1) * FACE : (2 * p + 2) * FACE] = self.right[p]
        ref[4 * FACE : 4 * FACE + 8] = self.swap


def tails_of(ref):
    return [ref[ROWS + p * FACE : ROWS + (p + 1) * FACE] for p in range(2)]


def write_tails(ref, tails):
    for p in range(2):
        ref[ROWS + p * FACE : ROWS + (p + 1) * FACE] = tails[p]


def lagged_left(seg, tails, after):
    return [seg.left[p] - vec_only(dot(tails[p], tall(behind(seg.swap, after, p)))) for p in range(2)]


def behind(swap, pair, p):
    return jnp.where(swap[:1] > 0.5, pair[1 - p], pair[p])


def join(first, second):
    lefts, rights = [], []
    for p in range(2):
        left1, right1 = first.left[p], first.right[p]
        left2, right2 = behind(first.swap, second.left, p), behind(first.swap, second.right, p)
        d1, d2 = unpack_d(left1, right1), unpack_d(left2, right2)
        lane = lane_of(left1.shape)
        through = dot(jnp.concatenate([left2, d2], axis=0), tall(left1))
        ab = through[:FACE] + vec_only(left2)
        back = through[FACE:] + vec_only(right2)
        both = dot(right1, tall(jnp.concatenate([right2, back], axis=1)))
        be = jnp.where(lane < VEC, both[:, :LANES], right1 + both[:, LANES:])
        left, right = pack(ab, be, d1 + both[:, LANES:])
        lefts.append(left)
        rights.append(right)
    return Segment(lefts, rights, jnp.abs(first.swap - second.swap))


def ordered(upper, own, got):
    up = upper[:1] > 0.5

    def pair(a, b):
        return jnp.where(up, a, b)

    def seg(a, b):
        return Segment(
            [pair(a.left[p], b.left[p]) for p in range(2)],
            [pair(a.right[p], b.right[p]) for p in range(2)],
            pair(a.swap, b.swap),
        )

    return seg(got, own), seg(own, got)


def columns_of(rows):
    before = jnp.zeros((VEC, DOF), F32)
    after = jnp.zeros((LANES - REST, DOF), F32)
    return jnp.concatenate([before, rows, after], axis=0).T


def make_maps(inv, low, up, rhs, coupled, flag, own):
    tables = jnp.concatenate([span_pick(0, LANES), span_pick(3, LANES), stream_pick(3, LANES)], axis=1)
    lane = lane_of((FACE, LANES))
    made, corners = [], []
    for n in range(2):
        m, u = inv[0, 0, n], up[0, 0, n]
        both = jnp.concatenate([stream_rows(m, 3), dot(u, stream_rows(m, 0))], axis=0)
        z = dot(both, widen(place_rows(low[0, 0, n], 0)) + columns_of(rhs[0, 0, :, n, :]))
        cut = pick(both, tables)
        for i in range(2):
            at = LONG + (2 * n + i) * 2 * FACE
            own[at : at + 2 * FACE] = cut[:, i * LANES : (i + 1) * LANES]
        corners.append(cut[:FACE, 2 * LANES :])
        ahead, down = z[:FACE], z[FACE:]
        made.append(
            pack(
                jnp.where(lane < VEC, -ahead, ahead),
                jnp.where(lane < VEC, -cut[FACE:, 2 * LANES :], down),
                -down,
            )
        )
    Segment(
        [behind(flag, [made[0][0], made[1][0]], p) for p in range(2)],
        [behind(flag, [made[0][1], made[1][1]], p) for p in range(2)],
        flag,
    ).write(own)
    write_tails(own, [behind(flag, corners, p) + side(coupled[p]).T[:FACE] for p in range(2)])


def flag_of(which):
    return jnp.full((8, LANES), which[0, 0, 0].astype(F32), F32)


def faces_kernel(
    guess_hbm, up_hbm, map_hbm, inv_hbm, low_hbm, rhs_hbm, place, along,
    near, far, lag, swap, upper, inv, low, up, rhs, guess, which, sems,
):
    pairs = [(guess_hbm, guess), (up_hbm, up), (map_hbm, which), (inv_hbm, inv), (low_hbm, low), (rhs_hbm, rhs)]
    copies = [pltpu.make_async_copy(a, b, sems.at[i]) for i, (a, b) in enumerate(pairs)]
    for copy in copies:
        copy.start()
    for level in range(LEVELS):
        bit = (place[0] >> level) & 1
        upper[level] = jnp.full((8, LANES), bit.astype(F32), F32)
    upper[LEVELS] = jnp.full((8, LANES), (along[0] & 1).astype(F32), F32)
    odd = upper[LEVELS][:, :FACE] > 0.5
    tables = jnp.concatenate([stream_pick(0, LANES), span_pick(0, LANES), span_pick(3, LANES)], axis=1)
    for copy in copies[:3]:
        copy.wait()
    both = pick(jnp.concatenate([guess[0, 0, :, n, :] for n in range(2)], axis=0), tables)
    flag = flag_of(which)
    swap[...] = flag
    swapped = flag[:, :FACE] > 0.5
    made = []
    for n in range(2):
        mine = both[8 * n : 8 * n + 8]
        west = mine[:, LANES : LANES + FACE]
        east = mine[:, 2 * LANES : 2 * LANES + FACE]
        near[n] = jnp.where(odd, west, east)
        far[n] = jnp.where(odd, east, west)
        made.append(dot(mine[:, :FACE], up[0, 0, n], NT))
    for p in range(2):
        lag[p] = jnp.where(swapped, made[1 - p], made[p])
    for copy in copies[3:]:
        copy.wait()


def maps_kernel(inv, low, up, rhs, ahead, swap, own):
    make_maps(inv, low, up, rhs, ahead, swap[...], own)


def vectors_kernel(maps, west, east, upper, from_far, from_near, relayed, own, terms):
    odd = upper[LEVELS][:, :FACE] > 0.5
    b, e = [], []
    for n in range(2):
        from_w = dot(jnp.where(odd, from_near[n], from_far[n]), west[0, 0, n], NT)
        from_e = dot(jnp.where(odd, from_far[n], from_near[n]), east[0, 0, n], NT)
        terms[0, 8 * n : 8 * n + 8] = from_w
        terms[1, 8 * n : 8 * n + 8] = from_e
        sides = jnp.concatenate([side(from_w), side(from_e)], axis=1)
        at = LONG + 2 * n * 2 * FACE
        cuts = jnp.concatenate([maps[at + i * 2 * FACE : at + (i + 1) * 2 * FACE] for i in range(2)], axis=1)
        both = dot(cuts, sides, NT)
        b.append(both[:FACE])
        e.append(both[FACE:])
    seg = Segment.of(maps)
    Segment(
        [seg.left[p] - behind(seg.swap, b, p) for p in range(2)],
        [seg.right[p] - behind(seg.swap, e, p) for p in range(2)],
        seg.swap,
    ).write(own)
    write_tails(own, tails_of(maps))


def rest_kernel(inv, low, rhs, terms, zin, zout, base):
    pout = stream_pick(3, LANES)
    lane = lane_of((DOF, LANES))
    halo = pick(terms[0], span_pick(0), NT) + pick(terms[1], span_pick(3), NT)
    for n in range(2):
        m = inv[0, 0, n]
        h = rhs[0, 0, :, n, :] - halo[8 * n : 8 * n + 8]
        z = dot(m, widen(place_rows(low[0, 0, n], 0)) + columns_of(h))
        zout[n] = pick(m, pout)
        zin[n] = jnp.where(lane < VEC, z, 0.0)
        base[n] = vec_only(z)


def sixteen_kernel(upper, own, got, out):
    both = join(*ordered(upper[3], Segment.of(own), Segment.of(got)))
    second = upper[0][:1] > 0.5
    for i, pair in enumerate((both.left, both.right)):
        out[i * FACE : (i + 1) * FACE] = jnp.where(second, pair[1], pair[0])
    out[2 * FACE :] = both.swap


def first_pair_kernel(upper, own, got, relayed, out, lefts):
    first, second = ordered(upper[0], Segment.of(own), Segment.of(got))
    up = upper[0][:1] > 0.5
    mine, other = tails_of(own), tails_of(got)
    tails1 = [jnp.where(up, other[p], mine[p]) for p in range(2)]
    tails2 = [jnp.where(up, mine[p], other[p]) for p in range(2)]
    first = Segment(lagged_left(first, tails1, tails2), first.right, first.swap)
    both = join(first, second)
    lane = lane_of((FACE, LANES))
    tails = [jnp.where(lane < VEC, behind(first.swap, tails2, p), tails1[p]) for p in range(2)]
    behind_eight = sum(pltpu.roll(side(relayed[p]).T[:FACE], 8 * (p + 1), 1) for p in range(2))
    for p in range(2):
        lefts[p] = first.left[p]
    for i, pair in enumerate((both.left, both.right, tails)):
        out[i * FACE : (i + 1) * FACE] = jnp.where(up, pair[1], pair[0]) + (behind_eight if i == 2 else 0.0)
    out[3 * FACE :] = both.swap


def four_kernel(got, out, halves, lefts):
    def chain(i, p, tile):
        return got[2 * i + p, tile * FACE : (tile + 1) * FACE]

    tails = [[chain(i, p, 2) for p in range(2)] for i in range(4)]
    last = [pltpu.roll(tails[0][1], LANES - 8 * (p + 1), 1) for p in range(2)]
    segs = []
    for i in range(4):
        seg = Segment([chain(i, p, 0) for p in range(2)], [chain(i, p, 1) for p in range(2)], got[2 * i, 3 * FACE :])
        seg = Segment(lagged_left(seg, tails[i], tails[i + 1] if i < 3 else last), seg.right, seg.swap)
        for p in range(2):
            lefts[i, p] = seg.left[p]
        segs.append(seg)
    both = [join(segs[2 * i], segs[2 * i + 1]) for i in range(2)]
    join(*both).write(out)
    for i in range(2):
        both[i].write(halves.at[i])


def start_place():
    eye = (lax.broadcasted_iota(jnp.int32, (FACE, LANES), 0) == lane_of((FACE, LANES))).astype(F32)
    zero = jnp.zeros((FACE, LANES), F32)
    return [[eye, zero, eye] for _ in range(2)]


def widen_place(place, upper, own, got):
    lane = lane_of((FACE, LANES))
    keep = lane < REST
    up = upper[:1] > 0.5
    made = []
    for p in range(2):
        near = [behind(got.swap, [place[0][i], place[1][i]], p) for i in range(3)]
        sib = tall(got.left[p])
        moved = dot(jnp.concatenate([near[0], near[1]], axis=0), sib)
        above = [
            jnp.where(keep, moved[:FACE], 0.0) + vec_only(near[0]),
            jnp.where(keep, moved[FACE:], 0.0) + vec_only(near[1]),
            near[2],
        ]
        left2, right2 = behind(own.swap, got.left, p), behind(own.swap, got.right, p)
        back = dot(unpack_d(left2, right2), tall(own.left[p])) + vec_only(right2)
        turned = dot(place[p][2], tall(jnp.concatenate([back, right2], axis=1)))
        below = [
            place[p][0],
            place[p][1] + jnp.where(keep, turned[:, :LANES], 0.0),
            jnp.where(lane < VEC, turned[:, LANES:], 0.0),
        ]
        made.append([jnp.where(up, above[i], below[i]) for i in range(3)])
    return made


def read_place(ref):
    return [[ref[p, i] for i in range(3)] for p in range(2)]


def write_place(ref, place):
    for p in range(2):
        for i in range(3):
            ref[p, i] = place[p][i]


def four_place_kernel(at, upper, one, one_got, lefts, got, pair_lefts, halves, out, swap_out):
    mine, other = Segment.of(one), Segment.of(one_got)
    up = upper[0][:1] > 0.5
    mine.left = [jnp.where(up, mine.left[p], lefts[p]) for p in range(2)]
    other.left = [jnp.where(up, lefts[p], other.left[p]) for p in range(2)]
    made = widen_place(start_place(), upper[0], mine, other)
    x = jnp.abs(mine.swap - jnp.where(upper[0] > 0.5, other.swap, 0.0))
    j = (at[0] >> 1) & 3
    half = j >> 1

    def pair_of(i):
        right = [got[2 * i + p, FACE : 2 * FACE] for p in range(2)]
        return Segment([pair_lefts[i, p] for p in range(2)], right, got[2 * i, 3 * FACE :])

    mine, other = pair_of(j), pair_of(j ^ 1)
    made = widen_place(made, upper[1], mine, other)
    x = jnp.abs(x - jnp.where(upper[1] > 0.5, other.swap, 0.0))
    mine, other = Segment.of(halves.at[half]), Segment.of(halves.at[1 - half])
    write_place(out, widen_place(made, upper[2], mine, other))
    swap_out[...] = jnp.abs(x - jnp.where(upper[2] > 0.5, other.swap, 0.0))


def answer_kernel(place, turn, zin, zout, base, fixed, free):
    made = read_place(place)
    x = turn[...]
    for n in range(2):
        p0, q0, r0 = [behind(x, [made[0][i], made[1][i]], n) for i in range(3)]
        f = dot(jnp.concatenate([zin[n], zout[n]], axis=1), jnp.concatenate([tall(p0), tall(q0)], axis=0))
        free[n] = jnp.concatenate([f, dot(zout[n], tall(r0))], axis=1)
        fixed[n] = (base[n] - f).T[VEC:REST]


def last_kernel(upper, got, own, got8, turn, fixed, free, out):
    def chain(i, p, tile):
        return got[2 * i + p, tile * FACE : (tile + 1) * FACE]

    segs = [
        Segment([chain(i, p, 0) for p in range(2)], [chain(i, p, 1) for p in range(2)], got[2 * i, 2 * FACE :])
        for i in range(4)
    ]
    zero = jnp.zeros((FACE, LANES), F32)
    t, ahead = [[zero, zero]], [None]
    first = [vec_only(segs[0].left[p]) for p in range(2)]
    t.append([behind(segs[0].swap, first, p) for p in range(2)])
    for i in (1, 2, 3):
        through, down = [], []
        for p in range(2):
            left, right = segs[i].left[p], segs[i].right[p]
            both = dot(jnp.concatenate([unpack_d(left, right), left], axis=0), tall(t[i][p]))
            down.append(both[:FACE] + vec_only(right))
            through.append(vec_only(both[FACE:] + left))
        ahead.append(down)
        if i < 3:
            t.append([behind(segs[i].swap, through, p) for p in range(2)])
    c = [None, None, None, [zero, zero]]
    for i in (2, 1, 0):
        arriving = [
            vec_only(ahead[i + 1][p] + (dot(segs[i + 1].right[p], tall(c[i + 1][p])) if i < 2 else 0.0))
            for p in range(2)
        ]
        c[i] = [behind(segs[i].swap, arriving, p) for p in range(2)]

    def here(pairs):
        low, high = upper[4][:1] > 0.5, upper[5][:1] > 0.5
        return [
            jnp.where(high, jnp.where(low, pairs[3][p], pairs[2][p]), jnp.where(low, pairs[1][p], pairs[0][p]))
            for p in range(2)
        ]

    t_in, c_out = here(t), here(c)
    mine, other = Segment.of(own), Segment.of(got8)
    up = upper[3][:1] > 0.5
    lower = [jnp.where(up, other.left[p], mine.left[p]) for p in range(2)]
    swap = jnp.where(up, other.swap, mine.swap)
    middle = [vec_only(dot(lower[p], tall(t_in[p])) + lower[p]) for p in range(2)]
    t_at, c_at = [], []
    for p in range(2):
        left, right = behind(mine.swap, other.left, p), behind(mine.swap, other.right, p)
        back = dot(
            jnp.concatenate([unpack_d(left, right), right], axis=1),
            jnp.concatenate([tall(middle[p]), tall(c_out[p])], axis=0),
        )
        t_at.append(jnp.where(up, behind(swap, middle, p), t_in[p]))
        c_at.append(jnp.where(up, behind(swap, c_out, p), vec_only(back + right)))
    for n in range(2):
        rows = [widen(behind(turn[...], pair, n).T[VEC:REST]) for pair in (t_at, c_at)]
        out[:, n, :] = fixed[n] - dot(jnp.concatenate(rows, axis=1), free[n], NT)


HBM = pl.BlockSpec(memory_space=pltpu.HBM)
VMEM = pl.BlockSpec(memory_space=pltpu.VMEM)
SMEM = pl.BlockSpec(memory_space=pltpu.SMEM)


def call(kernel, out_shape, *operands, hbm=(), smem=(), scratch=()):
    specs = [HBM if i in hbm else SMEM if i in smem else VMEM for i in range(len(operands))]
    several = isinstance(out_shape, tuple)
    operands = [
        pltpu.with_memory_space_constraint(x, pltpu.HBM) if i in hbm else x for i, x in enumerate(operands)
    ]
    return pl.pallas_call(
        kernel,
        out_shape=out_shape,
        in_specs=specs,
        out_specs=tuple(VMEM for _ in out_shape) if several else VMEM,
        scratch_shapes=list(scratch),
        cost_estimate=pl.CostEstimate(flops=0, bytes_accessed=1 << 20, transcendentals=0),
        compiler_params=pltpu.CompilerParams(vmem_limit_bytes=24 * 1024 * 1024),
    )(*operands)


def f32(*shape):
    return jax.ShapeDtypeStruct(shape, F32)


LEVELS = 6
ROWS = 4 * FACE + 8
LONG = ROWS + 2 * FACE


def per_device(
    rhs_field, guess, inverse_diag, lower_block, upper_block, west_block, east_block, inflow_map
):
    wide = lax.axis_size("span")
    layers = lax.axis_size("stream")
    place = lax.axis_index("stream").astype(jnp.int32).reshape(1)
    along = lax.axis_index("span").astype(jnp.int32).reshape(1)
    face = f32(2, 8, FACE)
    args = (guess, upper_block, inflow_map, inverse_diag, lower_block, rhs_field)
    near_face, far_face, ahead, swap, upper, inv, low, up, rhs = call(
        faces_kernel,
        (
            face, face, face, f32(8, LANES), f32(LEVELS + 1, 8, LANES),
            *(f32(*a.shape) for a in (inverse_diag, lower_block, upper_block, rhs_field)),
        ),
        *args, place, along,
        hbm=range(6), smem=(6, 7),
        scratch=(pltpu.VMEM(guess.shape, F32), pltpu.SMEM(inflow_map.shape, jnp.int32), pltpu.SemaphoreType.DMA((6,))),
    )
    from_far = lax.ppermute(far_face, "span", [(i, (i - 1 + 2 * (i & 1)) % wide) for i in range(wide)])
    from_near = lax.ppermute(near_face, "span", [(i, i ^ 1) for i in range(wide)])
    relayed = lax.ppermute(ahead, "stream", [(i + 8, i + 1) for i in range(0, layers - 8, 8)])
    maps = call(maps_kernel, f32(LONG + 8 * FACE, LANES), inv, low, up, rhs, ahead, swap)
    own, terms = call(
        vectors_kernel, (f32(LONG, LANES), f32(2, 16, FACE)),
        maps, west_block, east_block, upper, from_far, from_near, relayed,
    )

    def across(x, distance):
        return lax.ppermute(x, "stream", [(i, i ^ distance) for i in range(layers)])

    got = across(own, 1)
    chain, lefts = call(
        first_pair_kernel, (f32(3 * FACE + 8, LANES), f32(2, FACE, LANES)), upper, own, got, relayed
    )
    groups = [[8 * g + j for j in range(8)] for g in range(layers // 8)]
    chains = lax.all_gather(chain, "stream", axis_index_groups=groups)
    eight, halves, pair_lefts = call(
        four_kernel, (f32(ROWS, LANES), f32(2, ROWS, LANES), f32(4, 2, FACE, LANES)), chains
    )
    here = (f32(2, 3, FACE, LANES), f32(8, LANES))
    got8 = across(eight, 8)
    spot, turn = call(four_place_kernel, here, place, upper, own, got, lefts, chains, pair_lefts, halves, smem=(0,))
    terms, eight = lax.optimization_barrier((terms, eight))
    zin, zout, base = call(rest_kernel, tuple(f32(2, DOF, LANES) for _ in range(3)), inv, low, rhs, terms)
    fixed, free = call(
        answer_kernel, (f32(2, 8, DOF), f32(2, DOF, 2 * LANES)), spot, turn, zin, zout, base
    )
    got8, fixed, free, turn = lax.optimization_barrier((got8, fixed, free, turn))
    chain = call(sixteen_kernel, f32(2 * FACE + 8, LANES), upper, eight, got8)
    groups = [
        [16 * i + 8 * odd + 2 * z + c for i in range(layers // 16) for c in range(2)]
        for odd in range(2)
        for z in range(4)
    ]
    sixteens = lax.all_gather(chain, "stream", axis_index_groups=groups)
    out = call(last_kernel, f32(8, 2, DOF), upper, sixteens, eight, got8, turn, fixed, free)
    return out[None, None]


def solution(mesh):
    in_specs = (
        P("stream", "span", None, None, None),
        P("stream", "span", None, None, None),
        P("stream", "span", None, None, None),
        P("stream", "span", None, None, None),
        P("stream", "span", None, None, None),
        P("stream", "span", None, None, None),
        P("stream", "span", None, None, None),
        P("stream", "span", None),
    )
    out_specs = P("stream", "span", None, None, None)
    return jax.shard_map(
        per_device, mesh=mesh, in_specs=in_specs, out_specs=out_specs, check_vma=False
    )
```

```python
import functools

import jax
import jax.numpy as jnp
from jax import lax
from jax.experimental import pallas as pl
from jax.experimental.pallas import tpu as pltpu
from jax.sharding import PartitionSpec as P

NVAR = 5
NB = 4
FACE = 80
DOF = 320
LANES = 128
VEC = FACE
REST = FACE + 8
HALF = LANES - REST
BF16 = jnp.bfloat16
F32 = jnp.float32
NN = (((1,), (0,)), ((), ()))
NT = (((1,), (1,)), ((), ()))


def split(x):
    hi = x.astype(BF16)
    return hi, (x - hi.astype(F32)).astype(BF16)


def dot(a, b, dims=NN):
    ah, al = split(a)
    bh, bl = split(b)
    one = functools.partial(lax.dot_general, dimension_numbers=dims, preferred_element_type=F32)
    return one(ah, bh) + (one(ah, bl) + one(al, bh))


def pick(x, onehot, dims=NN):
    hi = x.astype(BF16).astype(F32)
    mid = (x - hi).astype(BF16).astype(F32)
    low = x - hi - mid
    rows = x.shape[0]
    parts = jnp.concatenate([hi, mid, low], axis=0).astype(BF16)
    made = lax.dot_general(parts, onehot, dimension_numbers=dims, preferred_element_type=F32)
    return made[:rows] + made[rows : 2 * rows] + made[2 * rows :]


def stream_pick(j, width=FACE):
    d = lax.broadcasted_iota(jnp.int32, (DOF, width), 0)
    f = lax.broadcasted_iota(jnp.int32, (DOF, width), 1)
    step = NB * NB
    return ((d == (f // step) * (NB * step) + j * step + f % step) & (f < FACE)).astype(F32).astype(BF16)


def span_pick(j, width=FACE):
    d = lax.broadcasted_iota(jnp.int32, (DOF, width), 0)
    f = lax.broadcasted_iota(jnp.int32, (DOF, width), 1)
    return ((d == (f // NB) * (NB * NB) + j * NB + f % NB) & (f < FACE)).astype(F32).astype(BF16)


def stream_rows(x, j):
    step = NB * NB
    return jnp.concatenate(
        [x[(v * NB + j) * step : (v * NB + j + 1) * step] for v in range(NVAR)], axis=0
    )


def place_rows(x, j):
    step = NB * NB
    zeros = jnp.zeros((step, x.shape[1]), x.dtype)
    parts = []
    for v in range(NVAR):
        for a in range(NB):
            parts.append(x[v * step : (v + 1) * step] if a == j else zeros)
    return jnp.concatenate(parts, axis=0)


def lane_of(shape):
    return lax.broadcasted_iota(jnp.int32, shape, 1)


def pack(ab, be, d):
    lane = lane_of(ab.shape)
    left = jnp.where(lane < REST, ab, pltpu.roll(d, REST, 1))
    right = jnp.where(lane < REST, be, pltpu.roll(d, REST - HALF, 1))
    return left, right


def unpack_d(left, right):
    lane = lane_of(left.shape)
    return jnp.where(
        lane < HALF, pltpu.roll(left, LANES - REST, 1), pltpu.roll(right, LANES - REST + HALF, 1)
    )


def tall(x):
    return jnp.concatenate([x, jnp.zeros((LANES - FACE, x.shape[1]), x.dtype)], axis=0)


def widen(x):
    return jnp.concatenate([x, jnp.zeros((x.shape[0], LANES - x.shape[1]), x.dtype)], axis=1)


def side(x):
    x = widen(x)
    before = jnp.zeros((VEC, LANES), x.dtype)
    after = jnp.zeros((LANES - REST, LANES), x.dtype)
    return jnp.concatenate([before, x, after], axis=0)


def vec_only(x):
    lane = lane_of(x.shape)
    return jnp.where((lane >= VEC) & (lane < REST), x, 0.0)


class Segment:
    def __init__(self, left, right, swap):
        self.left, self.right, self.swap = left, right, swap

    @staticmethod
    def of(ref):
        left = [ref[2 * p * FACE : (2 * p + 1) * FACE] for p in range(2)]
        right = [ref[(2 * p + 1) * FACE : (2 * p + 2) * FACE] for p in range(2)]
        return Segment(left, right, ref[4 * FACE : 4 * FACE + 8])

    def write(self, ref):
        for p in range(2):
            ref[2 * p * FACE : (2 * p + 1) * FACE] = self.left[p]
            ref[(2 * p + 1) * FACE : (2 * p + 2) * FACE] = self.right[p]
        ref[4 * FACE : 4 * FACE + 8] = self.swap


def tails_of(ref):
    return [ref[ROWS + p * FACE : ROWS + (p + 1) * FACE] for p in range(2)]


def write_tails(ref, tails):
    for p in range(2):
        ref[ROWS + p * FACE : ROWS + (p + 1) * FACE] = tails[p]


def lagged_left(seg, tails, after):
    return [seg.left[p] - vec_only(dot(tails[p], tall(behind(seg.swap, after, p)))) for p in range(2)]


def behind(swap, pair, p):
    return jnp.where(swap[:1] > 0.5, pair[1 - p], pair[p])


def join(first, second):
    lefts, rights = [], []
    for p in range(2):
        left1, right1 = first.left[p], first.right[p]
        left2, right2 = behind(first.swap, second.left, p), behind(first.swap, second.right, p)
        d1, d2 = unpack_d(left1, right1), unpack_d(left2, right2)
        lane = lane_of(left1.shape)
        through = dot(jnp.concatenate([left2, d2], axis=0), tall(left1))
        ab = through[:FACE] + vec_only(left2)
        back = through[FACE:] + vec_only(right2)
        both = dot(right1, tall(jnp.concatenate([right2, back], axis=1)))
        be = jnp.where(lane < VEC, both[:, :LANES], right1 + both[:, LANES:])
        left, right = pack(ab, be, d1 + both[:, LANES:])
        lefts.append(left)
        rights.append(right)
    return Segment(lefts, rights, jnp.abs(first.swap - second.swap))


def ordered(upper, own, got):
    up = upper[:1] > 0.5

    def pair(a, b):
        return jnp.where(up, a, b)

    def seg(a, b):
        return Segment(
            [pair(a.left[p], b.left[p]) for p in range(2)],
            [pair(a.right[p], b.right[p]) for p in range(2)],
            pair(a.swap, b.swap),
        )

    return seg(got, own), seg(own, got)


def columns_of(rows):
    before = jnp.zeros((VEC, DOF), F32)
    after = jnp.zeros((LANES - REST, DOF), F32)
    return jnp.concatenate([before, rows, after], axis=0).T


def make_maps(inv, low, up, rhs, west, east, coupled, flag, own):
    tables = jnp.concatenate([span_pick(0, LANES), span_pick(3, LANES), stream_pick(3, LANES)], axis=1)
    lane = lane_of((FACE, LANES))
    made, corners = [], []
    for n in range(2):
        m, u = inv[0, 0, n], up[0, 0, n]
        both = jnp.concatenate([stream_rows(m, 3), dot(u, stream_rows(m, 0))], axis=0)
        z = dot(both, widen(place_rows(low[0, 0, n], 0)) + columns_of(rhs[0, 0, :, n, :]))
        cut = pick(both, tables)
        for i in range(2):
            at = LONG + (2 * n + i) * 2 * FACE
            block = (west, east)[i][0, 0, n]
            own[at : at + 2 * FACE] = dot(cut[:, i * LANES : (i + 1) * LANES], tall(widen(block)))
        corners.append(cut[:FACE, 2 * LANES :])
        ahead, down = z[:FACE], z[FACE:]
        made.append(
            pack(
                jnp.where(lane < VEC, -ahead, ahead),
                jnp.where(lane < VEC, -cut[FACE:, 2 * LANES :], down),
                -down,
            )
        )
    Segment(
        [behind(flag, [made[0][0], made[1][0]], p) for p in range(2)],
        [behind(flag, [made[0][1], made[1][1]], p) for p in range(2)],
        flag,
    ).write(own)
    write_tails(own, [behind(flag, corners, p) + side(coupled[p]).T[:FACE] for p in range(2)])


def flag_of(which):
    return jnp.full((8, LANES), which[0, 0, 0].astype(F32), F32)


def first_kernel(
    guess_hbm, up_hbm, map_hbm, inv_hbm, low_hbm, rhs_hbm, west_hbm, east_hbm, place, along,
    lag, swap, upper, inv, low, up, rhs, west, east, guess, which, sems,
):
    pairs = [(guess_hbm, guess), (up_hbm, up), (map_hbm, which), (inv_hbm, inv), (low_hbm, low), (rhs_hbm, rhs)]
    pairs += [(west_hbm, west), (east_hbm, east)]
    copies = [pltpu.make_async_copy(a, b, sems.at[i]) for i, (a, b) in enumerate(pairs)]
    for copy in copies:
        copy.start()
    for level in range(LEVELS):
        bit = (place[0] >> level) & 1
        upper[level] = jnp.full((8, LANES), bit.astype(F32), F32)
    upper[LEVELS] = jnp.full((8, LANES), (along[0] & 1).astype(F32), F32)
    pin = stream_pick(0)
    for copy in copies[:3]:
        copy.wait()
    both = pick(jnp.concatenate([guess[0, 0, :, n, :] for n in range(2)], axis=0), pin)
    flag = flag_of(which)
    swap[...] = flag
    swapped = flag[:, :FACE] > 0.5
    made = []
    for n in range(2):
        made.append(dot(both[8 * n : 8 * n + 8], up[0, 0, n], NT))
    for p in range(2):
        lag[p] = jnp.where(swapped, made[1 - p], made[p])
    for copy in copies[3:]:
        copy.wait()


def maps_kernel(inv, low, up, rhs, west, east, ahead, swap, own):
    make_maps(inv, low, up, rhs, west, east, ahead, swap[...], own)


def vectors_kernel(maps, upper, from_far, from_near, relayed, own, terms):
    odd = upper[LEVELS][:1, :1] > 0.5
    near = jnp.concatenate([from_near[0, 0, :, n, :] for n in range(2)], axis=0)
    far = jnp.concatenate([from_far[0, 0, :, n, :] for n in range(2)], axis=0)
    from_west = pick(jnp.where(odd, near, far), span_pick(3))
    from_east = pick(jnp.where(odd, far, near), span_pick(0))
    terms[0], terms[1] = from_west, from_east
    b, e = [], []
    for n in range(2):
        rows = slice(8 * n, 8 * n + 8)
        sides = jnp.concatenate([side(from_west[rows]), side(from_east[rows])], axis=1)
        at = LONG + 2 * n * 2 * FACE
        cuts = jnp.concatenate([maps[at + i * 2 * FACE : at + (i + 1) * 2 * FACE] for i in range(2)], axis=1)
        both = dot(cuts, sides, NT)
        b.append(both[:FACE])
        e.append(both[FACE:])
    seg = Segment.of(maps)
    Segment(
        [seg.left[p] - behind(seg.swap, b, p) for p in range(2)],
        [seg.right[p] - behind(seg.swap, e, p) for p in range(2)],
        seg.swap,
    ).write(own)
    write_tails(own, tails_of(maps))


def rest_kernel(inv, low, rhs, west, east, terms, zin, zout, base):
    pout = stream_pick(3, LANES)
    lane = lane_of((DOF, LANES))
    made = [
        jnp.concatenate([dot(terms[i, 8 * n : 8 * n + 8], block[0, 0, n], NT) for n in range(2)], axis=0)
        for i, block in enumerate((west, east))
    ]
    halo = pick(made[0], span_pick(0), NT) + pick(made[1], span_pick(3), NT)
    for n in range(2):
        m = inv[0, 0, n]
        h = rhs[0, 0, :, n, :] - halo[8 * n : 8 * n + 8]
        z = dot(m, widen(place_rows(low[0, 0, n], 0)) + columns_of(h))
        zout[n] = pick(m, pout)
        zin[n] = jnp.where(lane < VEC, z, 0.0)
        base[n] = vec_only(z)


def sixteen_kernel(upper, own, got, out):
    both = join(*ordered(upper[3], Segment.of(own), Segment.of(got)))
    second = upper[0][:1] > 0.5
    for i, pair in enumerate((both.left, both.right)):
        out[i * FACE : (i + 1) * FACE] = jnp.where(second, pair[1], pair[0])
    out[2 * FACE :] = both.swap


def first_pair_kernel(upper, own, got, relayed, out, lefts):
    first, second = ordered(upper[0], Segment.of(own), Segment.of(got))
    up = upper[0][:1] > 0.5
    mine, other = tails_of(own), tails_of(got)
    tails1 = [jnp.where(up, other[p], mine[p]) for p in range(2)]
    tails2 = [jnp.where(up, mine[p], other[p]) for p in range(2)]
    first = Segment(lagged_left(first, tails1, tails2), first.right, first.swap)
    both = join(first, second)
    lane = lane_of((FACE, LANES))
    tails = [jnp.where(lane < VEC, behind(first.swap, tails2, p), tails1[p]) for p in range(2)]
    behind_eight = sum(pltpu.roll(side(relayed[p]).T[:FACE], 8 * (p + 1), 1) for p in range(2))
    for p in range(2):
        lefts[p] = first.left[p]
    for i, pair in enumerate((both.left, both.right, tails)):
        out[i * FACE : (i + 1) * FACE] = jnp.where(up, pair[1], pair[0]) + (behind_eight if i == 2 else 0.0)
    out[3 * FACE :] = both.swap


def four_kernel(got, out, halves, lefts):
    def chain(i, p, tile):
        return got[2 * i + p, tile * FACE : (tile + 1) * FACE]

    tails = [[chain(i, p, 2) for p in range(2)] for i in range(4)]
    last = [pltpu.roll(tails[0][1], LANES - 8 * (p + 1), 1) for p in range(2)]
    segs = []
    for i in range(4):
        seg = Segment([chain(i, p, 0) for p in range(2)], [chain(i, p, 1) for p in range(2)], got[2 * i, 3 * FACE :])
        seg = Segment(lagged_left(seg, tails[i], tails[i + 1] if i < 3 else last), seg.right, seg.swap)
        for p in range(2):
            lefts[i, p] = seg.left[p]
        segs.append(seg)
    both = [join(segs[2 * i], segs[2 * i + 1]) for i in range(2)]
    join(*both).write(out)
    for i in range(2):
        both[i].write(halves.at[i])


def start_place():
    eye = (lax.broadcasted_iota(jnp.int32, (FACE, LANES), 0) == lane_of((FACE, LANES))).astype(F32)
    zero = jnp.zeros((FACE, LANES), F32)
    return [[eye, zero, eye] for _ in range(2)]


def widen_place(place, upper, own, got):
    lane = lane_of((FACE, LANES))
    keep = lane < REST
    up = upper[:1] > 0.5
    made = []
    for p in range(2):
        near = [behind(got.swap, [place[0][i], place[1][i]], p) for i in range(3)]
        sib = tall(got.left[p])
        moved = dot(jnp.concatenate([near[0], near[1]], axis=0), sib)
        above = [
            jnp.where(keep, moved[:FACE], 0.0) + vec_only(near[0]),
            jnp.where(keep, moved[FACE:], 0.0) + vec_only(near[1]),
            near[2],
        ]
        left2, right2 = behind(own.swap, got.left, p), behind(own.swap, got.right, p)
        back = dot(unpack_d(left2, right2), tall(own.left[p])) + vec_only(right2)
        turned = dot(place[p][2], tall(jnp.concatenate([back, right2], axis=1)))
        below = [
            place[p][0],
            place[p][1] + jnp.where(keep, turned[:, :LANES], 0.0),
            jnp.where(lane < VEC, turned[:, LANES:], 0.0),
        ]
        made.append([jnp.where(up, above[i], below[i]) for i in range(3)])
    return made


def read_place(ref):
    return [[ref[p, i] for i in range(3)] for p in range(2)]


def write_place(ref, place):
    for p in range(2):
        for i in range(3):
            ref[p, i] = place[p][i]


def four_place_kernel(at, upper, one, one_got, lefts, got, pair_lefts, halves, out, swap_out):
    mine, other = Segment.of(one), Segment.of(one_got)
    up = upper[0][:1] > 0.5
    mine.left = [jnp.where(up, mine.left[p], lefts[p]) for p in range(2)]
    other.left = [jnp.where(up, lefts[p], other.left[p]) for p in range(2)]
    made = widen_place(start_place(), upper[0], mine, other)
    x = jnp.abs(mine.swap - jnp.where(upper[0] > 0.5, other.swap, 0.0))
    j = (at[0] >> 1) & 3
    half = j >> 1

    def pair_of(i):
        right = [got[2 * i + p, FACE : 2 * FACE] for p in range(2)]
        return Segment([pair_lefts[i, p] for p in range(2)], right, got[2 * i, 3 * FACE :])

    mine, other = pair_of(j), pair_of(j ^ 1)
    made = widen_place(made, upper[1], mine, other)
    x = jnp.abs(x - jnp.where(upper[1] > 0.5, other.swap, 0.0))
    mine, other = Segment.of(halves.at[half]), Segment.of(halves.at[1 - half])
    write_place(out, widen_place(made, upper[2], mine, other))
    swap_out[...] = jnp.abs(x - jnp.where(upper[2] > 0.5, other.swap, 0.0))


def answer_kernel(place, turn, zin, zout, base, fixed, free):
    made = read_place(place)
    x = turn[...]
    for n in range(2):
        p0, q0, r0 = [behind(x, [made[0][i], made[1][i]], n) for i in range(3)]
        f = dot(jnp.concatenate([zin[n], zout[n]], axis=1), jnp.concatenate([tall(p0), tall(q0)], axis=0))
        free[n] = jnp.concatenate([f, dot(zout[n], tall(r0))], axis=1)
        fixed[n] = (base[n] - f).T[VEC:REST]


def last_kernel(upper, got, own, got8, turn, fixed, free, out):
    def chain(i, p, tile):
        return got[2 * i + p, tile * FACE : (tile + 1) * FACE]

    def stack(*parts):
        return jnp.concatenate(parts, axis=0)

    def beside(*parts):
        return jnp.concatenate(parts, axis=1)

    segs = [
        Segment([chain(i, p, 0) for p in range(2)], [chain(i, p, 1) for p in range(2)], got[2 * i, 2 * FACE :])
        for i in range(4)
    ]
    d = [None] + [[unpack_d(segs[i].left[p], segs[i].right[p]) for p in range(2)] for i in (1, 2, 3)]
    w0, w1, w2 = [seg.swap for seg in segs[:3]]
    mine, other = Segment.of(own), Segment.of(got8)
    up = upper[3][:1] > 0.5
    zero = jnp.zeros((FACE, LANES), F32)

    t1 = [behind(w0, [vec_only(segs[0].left[q]) for q in range(2)], p) for p in range(2)]
    steps = [dot(stack(d[1][p], segs[1].left[p]), tall(t1[p])) for p in range(2)]
    down1 = [steps[p][:FACE] + vec_only(segs[1].right[p]) for p in range(2)]
    t2 = [vec_only(steps[p][FACE:] + segs[1].left[p]) for p in range(2)]
    t2 = [behind(w1, t2, p) for p in range(2)]
    turned = [
        dot(behind(w2, d[3], p), tall(segs[2].left[p])) + vec_only(behind(w2, segs[3].right, p)) for p in range(2)
    ]
    both_back = [dot(segs[1].right[p], tall(behind(w1, segs[2].right, p))) for p in range(2)]
    near_right = [behind(mine.swap, other.right, p) for p in range(2)]
    near_d = [unpack_d(other.left[p], other.right[p]) for p in range(2)]
    near_back = [
        dot(behind(mine.swap, near_d, p), tall(mine.left[p])) + vec_only(near_right[p]) for p in range(2)
    ]

    steps = [dot(stack(d[2][p], turned[p], segs[2].left[p]), tall(t2[p])) for p in range(2)]
    down2 = [vec_only(steps[p][:FACE]) for p in range(2)]
    c2 = [vec_only(steps[p][FACE : 2 * FACE] + turned[p]) for p in range(2)]
    t3 = [vec_only(steps[p][2 * FACE :] + segs[2].left[p]) for p in range(2)]
    t3 = [behind(w2, t3, p) for p in range(2)]

    c1 = [vec_only(dot(segs[2].right[p], tall(c2[p])) + down2[p] + segs[2].right[p]) for p in range(2)]
    c1 = [behind(w1, c1, p) for p in range(2)]
    c0 = []
    for p in range(2):
        made = dot(
            beside(both_back[p], segs[1].right[p]), stack(tall(behind(w1, c2, p)), tall(behind(w1, down2, p)))
        )
        c0.append(vec_only(made + both_back[p] + down1[p]))
    c0 = [behind(w0, c0, p) for p in range(2)]

    def here(a, b, c, e):
        low, high = upper[4][:1] > 0.5, upper[5][:1] > 0.5
        return [jnp.where(high, jnp.where(low, e[p], c[p]), jnp.where(low, b[p], a[p])) for p in range(2)]

    t_in = here([zero, zero], t1, t2, t3)
    c_out = here(c0, c1, c2, [zero, zero])
    through = [vec_only(dot(other.left[p], tall(t_in[p])) + other.left[p]) for p in range(2)]
    t_at, c_at = [], []
    for p in range(2):
        back = dot(beside(near_back[p], near_right[p]), stack(tall(t_in[p]), tall(c_out[p])))
        t_at.append(jnp.where(up, behind(other.swap, through, p), t_in[p]))
        c_at.append(jnp.where(up, behind(other.swap, c_out, p), vec_only(back + near_back[p])))
    for n in range(2):
        rows = [widen(behind(turn[...], pair, n).T[VEC:REST]) for pair in (t_at, c_at)]
        out[:, n, :] = fixed[n] - dot(beside(*rows), free[n], NT)


HBM = pl.BlockSpec(memory_space=pltpu.HBM)
VMEM = pl.BlockSpec(memory_space=pltpu.VMEM)
SMEM = pl.BlockSpec(memory_space=pltpu.SMEM)


def call(kernel, out_shape, *operands, hbm=(), smem=(), scratch=()):
    specs = [HBM if i in hbm else SMEM if i in smem else VMEM for i in range(len(operands))]
    several = isinstance(out_shape, tuple)
    operands = [
        pltpu.with_memory_space_constraint(x, pltpu.HBM) if i in hbm else x for i, x in enumerate(operands)
    ]
    return pl.pallas_call(
        kernel,
        out_shape=out_shape,
        in_specs=specs,
        out_specs=tuple(VMEM for _ in out_shape) if several else VMEM,
        scratch_shapes=list(scratch),
        cost_estimate=pl.CostEstimate(flops=0, bytes_accessed=1 << 20, transcendentals=0),
        compiler_params=pltpu.CompilerParams(vmem_limit_bytes=24 * 1024 * 1024),
    )(*operands)


def f32(*shape):
    return jax.ShapeDtypeStruct(shape, F32)


LEVELS = 6
ROWS = 4 * FACE + 8
LONG = ROWS + 2 * FACE


def per_device(
    rhs_field, guess, inverse_diag, lower_block, upper_block, west_block, east_block, inflow_map
):
    wide = lax.axis_size("span")
    layers = lax.axis_size("stream")
    place = lax.axis_index("stream").astype(jnp.int32).reshape(1)
    along = lax.axis_index("span").astype(jnp.int32).reshape(1)
    from_far = lax.ppermute(guess, "span", [(i, (i - 1 + 2 * (i & 1)) % wide) for i in range(wide)])
    from_near = lax.ppermute(guess, "span", [(i, i ^ 1) for i in range(wide)])
    args = (guess, upper_block, inflow_map, inverse_diag, lower_block, rhs_field, west_block, east_block)
    ahead, swap, upper, inv, low, up, rhs, west, east = call(
        first_kernel,
        (
            f32(2, 8, FACE), f32(8, LANES), f32(LEVELS + 1, 8, LANES),
            *(f32(*a.shape) for a in (inverse_diag, lower_block, upper_block, rhs_field, west_block, east_block)),
        ),
        *args, place, along,
        hbm=range(8), smem=(8, 9),
        scratch=(pltpu.VMEM(guess.shape, F32), pltpu.SMEM(inflow_map.shape, jnp.int32), pltpu.SemaphoreType.DMA((8,))),
    )
    maps = call(maps_kernel, f32(LONG + 8 * FACE, LANES), inv, low, up, rhs, west, east, ahead, swap)
    ahead, maps = lax.optimization_barrier((ahead, maps))
    relayed = lax.ppermute(ahead, "stream", [(i + 8, i + 1) for i in range(0, layers - 8, 8)])
    own, terms = call(
        vectors_kernel, (f32(LONG, LANES), f32(2, 16, FACE)),
        maps, upper, from_far, from_near, relayed,
    )

    def across(x, distance):
        return lax.ppermute(x, "stream", [(i, i ^ distance) for i in range(layers)])

    got = across(own, 1)
    chain, lefts = call(
        first_pair_kernel, (f32(3 * FACE + 8, LANES), f32(2, FACE, LANES)), upper, own, got, relayed
    )
    groups = [[8 * g + j for j in range(8)] for g in range(layers // 8)]
    chains = lax.all_gather(chain, "stream", axis_index_groups=groups)
    eight, halves, pair_lefts = call(
        four_kernel, (f32(ROWS, LANES), f32(2, ROWS, LANES), f32(4, 2, FACE, LANES)), chains
    )
    here = (f32(2, 3, FACE, LANES), f32(8, LANES))
    got8 = across(eight, 8)
    spot, turn = call(four_place_kernel, here, place, upper, own, got, lefts, chains, pair_lefts, halves, smem=(0,))
    terms, eight = lax.optimization_barrier((terms, eight))
    zin, zout, base = call(rest_kernel, tuple(f32(2, DOF, LANES) for _ in range(3)), inv, low, rhs, west, east, terms)
    fixed, free = call(
        answer_kernel, (f32(2, 8, DOF), f32(2, DOF, 2 * LANES)), spot, turn, zin, zout, base
    )
    got8, fixed, free, turn = lax.optimization_barrier((got8, fixed, free, turn))
    chain = call(sixteen_kernel, f32(2 * FACE + 8, LANES), upper, eight, got8)
    groups = [
        [16 * i + 8 * odd + 2 * z + c for i in range(layers // 16) for c in range(2)]
        for odd in range(2)
        for z in range(4)
    ]
    sixteens = lax.all_gather(chain, "stream", axis_index_groups=groups)
    out = call(last_kernel, f32(8, 2, DOF), upper, sixteens, eight, got8, turn, fixed, free)
    return out[None, None]


def solution(mesh):
    in_specs = (
        P("stream", "span", None, None, None),
        P("stream", "span", None, None, None),
        P("stream", "span", None, None, None),
        P("stream", "span", None, None, None),
        P("stream", "span", None, None, None),
        P("stream", "span", None, None, None),
        P("stream", "span", None, None, None),
        P("stream", "span", None),
    )
    out_specs = P("stream", "span", None, None, None)
    return jax.shard_map(
        per_device, mesh=mesh, in_specs=in_specs, out_specs=out_specs, check_vma=False
    )
```

```python
import functools

import jax
import jax.numpy as jnp
from jax import lax
from jax.experimental import pallas as pl
from jax.experimental.pallas import tpu as pltpu
from jax.sharding import PartitionSpec as P

NVAR = 5
NB = 4
FACE = 80
DOF = 320
LANES = 128
VEC = FACE
REST = FACE + 8
HALF = LANES - REST
BF16 = jnp.bfloat16
F32 = jnp.float32
NN = (((1,), (0,)), ((), ()))
NT = (((1,), (1,)), ((), ()))


def split(x):
    hi = x.astype(BF16)
    return hi, (x - hi.astype(F32)).astype(BF16)


def dot(a, b, dims=NN):
    ah, al = split(a)
    bh, bl = split(b)
    one = functools.partial(lax.dot_general, dimension_numbers=dims, preferred_element_type=F32)
    return one(ah, bh) + (one(ah, bl) + one(al, bh))


def pick(x, onehot, dims=NN):
    hi = x.astype(BF16).astype(F32)
    mid = (x - hi).astype(BF16).astype(F32)
    low = x - hi - mid
    rows = x.shape[0]
    parts = jnp.concatenate([hi, mid, low], axis=0).astype(BF16)
    made = lax.dot_general(parts, onehot, dimension_numbers=dims, preferred_element_type=F32)
    return made[:rows] + made[rows : 2 * rows] + made[2 * rows :]


def stream_pick(j, width=FACE):
    d = lax.broadcasted_iota(jnp.int32, (DOF, width), 0)
    f = lax.broadcasted_iota(jnp.int32, (DOF, width), 1)
    step = NB * NB
    return ((d == (f // step) * (NB * step) + j * step + f % step) & (f < FACE)).astype(F32).astype(BF16)


def span_pick(j, width=FACE):
    d = lax.broadcasted_iota(jnp.int32, (DOF, width), 0)
    f = lax.broadcasted_iota(jnp.int32, (DOF, width), 1)
    return ((d == (f // NB) * (NB * NB) + j * NB + f % NB) & (f < FACE)).astype(F32).astype(BF16)


def stream_rows(x, j):
    step = NB * NB
    return jnp.concatenate(
        [x[(v * NB + j) * step : (v * NB + j + 1) * step] for v in range(NVAR)], axis=0
    )


def place_rows(x, j):
    step = NB * NB
    zeros = jnp.zeros((step, x.shape[1]), x.dtype)
    parts = []
    for v in range(NVAR):
        for a in range(NB):
            parts.append(x[v * step : (v + 1) * step] if a == j else zeros)
    return jnp.concatenate(parts, axis=0)


def lane_of(shape):
    return lax.broadcasted_iota(jnp.int32, shape, 1)


def pack(ab, be, d):
    lane = lane_of(ab.shape)
    left = jnp.where(lane < REST, ab, pltpu.roll(d, REST, 1))
    right = jnp.where(lane < REST, be, pltpu.roll(d, REST - HALF, 1))
    return left, right


def unpack_d(left, right):
    lane = lane_of(left.shape)
    return jnp.where(
        lane < HALF, pltpu.roll(left, LANES - REST, 1), pltpu.roll(right, LANES - REST + HALF, 1)
    )


def tall(x):
    return jnp.concatenate([x, jnp.zeros((LANES - FACE, x.shape[1]), x.dtype)], axis=0)


def widen(x):
    return jnp.concatenate([x, jnp.zeros((x.shape[0], LANES - x.shape[1]), x.dtype)], axis=1)


def side(x):
    x = widen(x)
    before = jnp.zeros((VEC, LANES), x.dtype)
    after = jnp.zeros((LANES - REST, LANES), x.dtype)
    return jnp.concatenate([before, x, after], axis=0)


def vec_only(x):
    lane = lane_of(x.shape)
    return jnp.where((lane >= VEC) & (lane < REST), x, 0.0)


class Segment:
    def __init__(self, left, right, swap):
        self.left, self.right, self.swap = left, right, swap

    @staticmethod
    def of(ref):
        left = [ref[2 * p * FACE : (2 * p + 1) * FACE] for p in range(2)]
        right = [ref[(2 * p + 1) * FACE : (2 * p + 2) * FACE] for p in range(2)]
        return Segment(left, right, ref[4 * FACE : 4 * FACE + 8])

    def write(self, ref):
        for p in range(2):
            ref[2 * p * FACE : (2 * p + 1) * FACE] = self.left[p]
            ref[(2 * p + 1) * FACE : (2 * p + 2) * FACE] = self.right[p]
        ref[4 * FACE : 4 * FACE + 8] = self.swap


def tails_of(ref):
    return [ref[ROWS + p * FACE : ROWS + (p + 1) * FACE] for p in range(2)]


def write_tails(ref, tails):
    for p in range(2):
        ref[ROWS + p * FACE : ROWS + (p + 1) * FACE] = tails[p]


def lagged_left(seg, tails, after):
    return [seg.left[p] - vec_only(dot(tails[p], tall(behind(seg.swap, after, p)))) for p in range(2)]


def behind(swap, pair, p):
    return jnp.where(swap[:1] > 0.5, pair[1 - p], pair[p])


def join(first, second):
    lefts, rights = [], []
    for p in range(2):
        left1, right1 = first.left[p], first.right[p]
        left2, right2 = behind(first.swap, second.left, p), behind(first.swap, second.right, p)
        d1, d2 = unpack_d(left1, right1), unpack_d(left2, right2)
        lane = lane_of(left1.shape)
        through = dot(jnp.concatenate([left2, d2], axis=0), tall(left1))
        ab = through[:FACE] + vec_only(left2)
        back = through[FACE:] + vec_only(right2)
        both = dot(right1, tall(jnp.concatenate([right2, back], axis=1)))
        be = jnp.where(lane < VEC, both[:, :LANES], right1 + both[:, LANES:])
        left, right = pack(ab, be, d1 + both[:, LANES:])
        lefts.append(left)
        rights.append(right)
    return Segment(lefts, rights, jnp.abs(first.swap - second.swap))


def ordered(upper, own, got):
    up = upper[:1] > 0.5

    def pair(a, b):
        return jnp.where(up, a, b)

    def seg(a, b):
        return Segment(
            [pair(a.left[p], b.left[p]) for p in range(2)],
            [pair(a.right[p], b.right[p]) for p in range(2)],
            pair(a.swap, b.swap),
        )

    return seg(got, own), seg(own, got)


def columns_of(rows):
    before = jnp.zeros((VEC, DOF), F32)
    after = jnp.zeros((LANES - REST, DOF), F32)
    return jnp.concatenate([before, rows, after], axis=0).T


def make_maps(inv, low, up, rhs, west, east, coupled, flag, own):
    tables = jnp.concatenate([span_pick(0, LANES), span_pick(3, LANES), stream_pick(3, LANES)], axis=1)
    lane = lane_of((FACE, LANES))
    made, corners = [], []
    for n in range(2):
        m, u = inv[0, 0, n], up[0, 0, n]
        both = jnp.concatenate([stream_rows(m, 3), dot(u, stream_rows(m, 0))], axis=0)
        z = dot(both, widen(place_rows(low[0, 0, n], 0)) + columns_of(rhs[0, 0, :, n, :]))
        cut = pick(both, tables)
        for i in range(2):
            at = LONG + (2 * n + i) * 2 * FACE
            block = (west, east)[i][0, 0, n]
            own[at : at + 2 * FACE] = dot(cut[:, i * LANES : (i + 1) * LANES], tall(widen(block)))
        corners.append(cut[:FACE, 2 * LANES :])
        ahead, down = z[:FACE], z[FACE:]
        made.append(
            pack(
                jnp.where(lane < VEC, -ahead, ahead),
                jnp.where(lane < VEC, -cut[FACE:, 2 * LANES :], down),
                -down,
            )
        )
    Segment(
        [behind(flag, [made[0][0], made[1][0]], p) for p in range(2)],
        [behind(flag, [made[0][1], made[1][1]], p) for p in range(2)],
        flag,
    ).write(own)
    write_tails(own, [behind(flag, corners, p) + side(coupled[p]).T[:FACE] for p in range(2)])


def flag_of(which):
    return jnp.full((8, LANES), which[0, 0, 0].astype(F32), F32)


def first_kernel(
    guess_hbm, up_hbm, map_hbm, inv_hbm, low_hbm, rhs_hbm, west_hbm, east_hbm, place, along,
    lag, swap, upper, inv, low, up, rhs, west, east, guess, which, sems,
):
    pairs = [(guess_hbm, guess), (up_hbm, up), (map_hbm, which), (inv_hbm, inv), (low_hbm, low), (rhs_hbm, rhs)]
    pairs += [(west_hbm, west), (east_hbm, east)]
    copies = [pltpu.make_async_copy(a, b, sems.at[i]) for i, (a, b) in enumerate(pairs)]
    for copy in copies:
        copy.start()
    for level in range(LEVELS):
        bit = (place[0] >> level) & 1
        upper[level] = jnp.full((8, LANES), bit.astype(F32), F32)
    upper[LEVELS] = jnp.full((8, LANES), (along[0] & 1).astype(F32), F32)
    pin = stream_pick(0)
    for copy in copies[:3]:
        copy.wait()
    both = pick(jnp.concatenate([guess[0, 0, :, n, :] for n in range(2)], axis=0), pin)
    flag = flag_of(which)
    swap[...] = flag
    swapped = flag[:, :FACE] > 0.5
    made = []
    for n in range(2):
        made.append(dot(both[8 * n : 8 * n + 8], up[0, 0, n], NT))
    for p in range(2):
        lag[p] = jnp.where(swapped, made[1 - p], made[p])
    for copy in copies[3:]:
        copy.wait()


def maps_kernel(inv, low, up, rhs, west, east, ahead, swap, own):
    make_maps(inv, low, up, rhs, west, east, ahead, swap[...], own)


def vectors_kernel(maps, upper, from_near, from_far, relayed, own, terms):
    odd = upper[LEVELS][:1, :1] > 0.5
    near = jnp.concatenate([from_near[0, 0, :, n, :] for n in range(2)], axis=0)
    far = jnp.concatenate([from_far[0, 0, :, n, :] for n in range(2)], axis=0)
    from_west = pick(jnp.where(odd, near, far), span_pick(3))
    from_east = pick(jnp.where(odd, far, near), span_pick(0))
    terms[0], terms[1] = from_west, from_east
    b, e = [], []
    for n in range(2):
        rows = slice(8 * n, 8 * n + 8)
        sides = jnp.concatenate([side(from_west[rows]), side(from_east[rows])], axis=1)
        at = LONG + 2 * n * 2 * FACE
        cuts = jnp.concatenate([maps[at + i * 2 * FACE : at + (i + 1) * 2 * FACE] for i in range(2)], axis=1)
        both = dot(cuts, sides, NT)
        b.append(both[:FACE])
        e.append(both[FACE:])
    seg = Segment.of(maps)
    Segment(
        [seg.left[p] - behind(seg.swap, b, p) for p in range(2)],
        [seg.right[p] - behind(seg.swap, e, p) for p in range(2)],
        seg.swap,
    ).write(own)
    write_tails(own, tails_of(maps))


def rest_kernel(inv, low, rhs, west, east, terms, zin, zout, base):
    pout = stream_pick(3, LANES)
    lane = lane_of((DOF, LANES))
    made = [
        jnp.concatenate([dot(terms[i, 8 * n : 8 * n + 8], block[0, 0, n], NT) for n in range(2)], axis=0)
        for i, block in enumerate((west, east))
    ]
    halo = pick(made[0], span_pick(0), NT) + pick(made[1], span_pick(3), NT)
    for n in range(2):
        m = inv[0, 0, n]
        h = rhs[0, 0, :, n, :] - halo[8 * n : 8 * n + 8]
        z = dot(m, widen(place_rows(low[0, 0, n], 0)) + columns_of(h))
        zout[n] = pick(m, pout)
        zin[n] = jnp.where(lane < VEC, z, 0.0)
        base[n] = vec_only(z)


def sixteen_kernel(upper, own, got, out):
    both = join(*ordered(upper[3], Segment.of(own), Segment.of(got)))
    second = upper[0][:1] > 0.5
    for i, pair in enumerate((both.left, both.right)):
        out[i * FACE : (i + 1) * FACE] = jnp.where(second, pair[1], pair[0])
    out[2 * FACE :] = both.swap


def first_pair_kernel(upper, own, got, relayed, out, lefts):
    first, second = ordered(upper[0], Segment.of(own), Segment.of(got))
    up = upper[0][:1] > 0.5
    mine, other = tails_of(own), tails_of(got)
    tails1 = [jnp.where(up, other[p], mine[p]) for p in range(2)]
    tails2 = [jnp.where(up, mine[p], other[p]) for p in range(2)]
    first = Segment(lagged_left(first, tails1, tails2), first.right, first.swap)
    both = join(first, second)
    lane = lane_of((FACE, LANES))
    tails = [jnp.where(lane < VEC, behind(first.swap, tails2, p), tails1[p]) for p in range(2)]
    behind_eight = sum(pltpu.roll(side(relayed[p]).T[:FACE], 8 * (p + 1), 1) for p in range(2))
    for p in range(2):
        lefts[p] = first.left[p]
    for i, pair in enumerate((both.left, both.right, tails)):
        out[i * FACE : (i + 1) * FACE] = jnp.where(up, pair[1], pair[0]) + (behind_eight if i == 2 else 0.0)
    out[3 * FACE :] = both.swap


def four_kernel(got, out, halves, lefts):
    def chain(i, p, tile):
        return got[2 * i + p, tile * FACE : (tile + 1) * FACE]

    tails = [[chain(i, p, 2) for p in range(2)] for i in range(4)]
    last = [pltpu.roll(tails[0][1], LANES - 8 * (p + 1), 1) for p in range(2)]
    segs = []
    for i in range(4):
        seg = Segment([chain(i, p, 0) for p in range(2)], [chain(i, p, 1) for p in range(2)], got[2 * i, 3 * FACE :])
        seg = Segment(lagged_left(seg, tails[i], tails[i + 1] if i < 3 else last), seg.right, seg.swap)
        for p in range(2):
            lefts[i, p] = seg.left[p]
        segs.append(seg)
    both = [join(segs[2 * i], segs[2 * i + 1]) for i in range(2)]
    join(*both).write(out)
    for i in range(2):
        both[i].write(halves.at[i])


def start_place():
    eye = (lax.broadcasted_iota(jnp.int32, (FACE, LANES), 0) == lane_of((FACE, LANES))).astype(F32)
    zero = jnp.zeros((FACE, LANES), F32)
    return [[eye, zero, eye] for _ in range(2)]


def widen_place(place, upper, own, got):
    lane = lane_of((FACE, LANES))
    keep = lane < REST
    up = upper[:1] > 0.5
    made = []
    for p in range(2):
        near = [behind(got.swap, [place[0][i], place[1][i]], p) for i in range(3)]
        sib = tall(got.left[p])
        moved = dot(jnp.concatenate([near[0], near[1]], axis=0), sib)
        above = [
            jnp.where(keep, moved[:FACE], 0.0) + vec_only(near[0]),
            jnp.where(keep, moved[FACE:], 0.0) + vec_only(near[1]),
            near[2],
        ]
        left2, right2 = behind(own.swap, got.left, p), behind(own.swap, got.right, p)
        back = dot(unpack_d(left2, right2), tall(own.left[p])) + vec_only(right2)
        turned = dot(place[p][2], tall(jnp.concatenate([back, right2], axis=1)))
        below = [
            place[p][0],
            place[p][1] + jnp.where(keep, turned[:, :LANES], 0.0),
            jnp.where(lane < VEC, turned[:, LANES:], 0.0),
        ]
        made.append([jnp.where(up, above[i], below[i]) for i in range(3)])
    return made


def read_place(ref):
    return [[ref[p, i] for i in range(3)] for p in range(2)]


def write_place(ref, place):
    for p in range(2):
        for i in range(3):
            ref[p, i] = place[p][i]


def four_place_kernel(at, upper, one, one_got, lefts, got, pair_lefts, halves, out, swap_out):
    mine, other = Segment.of(one), Segment.of(one_got)
    up = upper[0][:1] > 0.5
    mine.left = [jnp.where(up, mine.left[p], lefts[p]) for p in range(2)]
    other.left = [jnp.where(up, lefts[p], other.left[p]) for p in range(2)]
    made = widen_place(start_place(), upper[0], mine, other)
    x = jnp.abs(mine.swap - jnp.where(upper[0] > 0.5, other.swap, 0.0))
    j = (at[0] >> 1) & 3
    half = j >> 1

    def pair_of(i):
        right = [got[2 * i + p, FACE : 2 * FACE] for p in range(2)]
        return Segment([pair_lefts[i, p] for p in range(2)], right, got[2 * i, 3 * FACE :])

    mine, other = pair_of(j), pair_of(j ^ 1)
    made = widen_place(made, upper[1], mine, other)
    x = jnp.abs(x - jnp.where(upper[1] > 0.5, other.swap, 0.0))
    mine, other = Segment.of(halves.at[half]), Segment.of(halves.at[1 - half])
    write_place(out, widen_place(made, upper[2], mine, other))
    swap_out[...] = jnp.abs(x - jnp.where(upper[2] > 0.5, other.swap, 0.0))


def answer_kernel(place, turn, zin, zout, base, fixed, free):
    made = read_place(place)
    x = turn[...]
    for n in range(2):
        p0, q0, r0 = [behind(x, [made[0][i], made[1][i]], n) for i in range(3)]
        f = dot(jnp.concatenate([zin[n], zout[n]], axis=1), jnp.concatenate([tall(p0), tall(q0)], axis=0))
        free[n] = jnp.concatenate([f, dot(zout[n], tall(r0))], axis=1)
        fixed[n] = (base[n] - f).T[VEC:REST]


def last_kernel(upper, got, own, got8, turn, fixed, free, out):
    def chain(i, p, tile):
        return got[2 * i + p, tile * FACE : (tile + 1) * FACE]

    def stack(*parts):
        return jnp.concatenate(parts, axis=0)

    def beside(*parts):
        return jnp.concatenate(parts, axis=1)

    segs = [
        Segment([chain(i, p, 0) for p in range(2)], [chain(i, p, 1) for p in range(2)], got[2 * i, 2 * FACE :])
        for i in range(4)
    ]
    d = [None] + [[unpack_d(segs[i].left[p], segs[i].right[p]) for p in range(2)] for i in (1, 2, 3)]
    w0, w1, w2 = [seg.swap for seg in segs[:3]]
    mine, other = Segment.of(own), Segment.of(got8)
    up = upper[3][:1] > 0.5
    zero = jnp.zeros((FACE, LANES), F32)

    t1 = [behind(w0, [vec_only(segs[0].left[q]) for q in range(2)], p) for p in range(2)]
    steps = [dot(stack(d[1][p], segs[1].left[p]), tall(t1[p])) for p in range(2)]
    down1 = [steps[p][:FACE] + vec_only(segs[1].right[p]) for p in range(2)]
    t2 = [vec_only(steps[p][FACE:] + segs[1].left[p]) for p in range(2)]
    t2 = [behind(w1, t2, p) for p in range(2)]
    turned = [
        dot(behind(w2, d[3], p), tall(segs[2].left[p])) + vec_only(behind(w2, segs[3].right, p)) for p in range(2)
    ]
    both_back = [dot(segs[1].right[p], tall(behind(w1, segs[2].right, p))) for p in range(2)]
    near_right = [behind(mine.swap, other.right, p) for p in range(2)]
    near_d = [unpack_d(other.left[p], other.right[p]) for p in range(2)]
    near_back = [
        dot(behind(mine.swap, near_d, p), tall(mine.left[p])) + vec_only(near_right[p]) for p in range(2)
    ]

    steps = [dot(stack(d[2][p], turned[p], segs[2].left[p]), tall(t2[p])) for p in range(2)]
    down2 = [vec_only(steps[p][:FACE]) for p in range(2)]
    c2 = [vec_only(steps[p][FACE : 2 * FACE] + turned[p]) for p in range(2)]
    t3 = [vec_only(steps[p][2 * FACE :] + segs[2].left[p]) for p in range(2)]
    t3 = [behind(w2, t3, p) for p in range(2)]

    c1 = [vec_only(dot(segs[2].right[p], tall(c2[p])) + down2[p] + segs[2].right[p]) for p in range(2)]
    c1 = [behind(w1, c1, p) for p in range(2)]
    c0 = []
    for p in range(2):
        made = dot(
            beside(both_back[p], segs[1].right[p]), stack(tall(behind(w1, c2, p)), tall(behind(w1, down2, p)))
        )
        c0.append(vec_only(made + both_back[p] + down1[p]))
    c0 = [behind(w0, c0, p) for p in range(2)]

    def here(a, b, c, e):
        low, high = upper[4][:1] > 0.5, upper[5][:1] > 0.5
        return [jnp.where(high, jnp.where(low, e[p], c[p]), jnp.where(low, b[p], a[p])) for p in range(2)]

    t_in = here([zero, zero], t1, t2, t3)
    c_out = here(c0, c1, c2, [zero, zero])
    through = [vec_only(dot(other.left[p], tall(t_in[p])) + other.left[p]) for p in range(2)]
    t_at, c_at = [], []
    for p in range(2):
        back = dot(beside(near_back[p], near_right[p]), stack(tall(t_in[p]), tall(c_out[p])))
        t_at.append(jnp.where(up, behind(other.swap, through, p), t_in[p]))
        c_at.append(jnp.where(up, behind(other.swap, c_out, p), vec_only(back + near_back[p])))
    for n in range(2):
        rows = [widen(behind(turn[...], pair, n).T[VEC:REST]) for pair in (t_at, c_at)]
        out[:, n, :] = fixed[n] - dot(beside(*rows), free[n], NT)


HBM = pl.BlockSpec(memory_space=pltpu.HBM)
VMEM = pl.BlockSpec(memory_space=pltpu.VMEM)
SMEM = pl.BlockSpec(memory_space=pltpu.SMEM)


def call(kernel, out_shape, *operands, hbm=(), smem=(), scratch=()):
    specs = [HBM if i in hbm else SMEM if i in smem else VMEM for i in range(len(operands))]
    several = isinstance(out_shape, tuple)
    operands = [
        pltpu.with_memory_space_constraint(x, pltpu.HBM) if i in hbm else x for i, x in enumerate(operands)
    ]
    return pl.pallas_call(
        kernel,
        out_shape=out_shape,
        in_specs=specs,
        out_specs=tuple(VMEM for _ in out_shape) if several else VMEM,
        scratch_shapes=list(scratch),
        cost_estimate=pl.CostEstimate(flops=0, bytes_accessed=1 << 20, transcendentals=0),
        compiler_params=pltpu.CompilerParams(vmem_limit_bytes=24 * 1024 * 1024),
    )(*operands)


def f32(*shape):
    return jax.ShapeDtypeStruct(shape, F32)


LEVELS = 6
ROWS = 4 * FACE + 8
LONG = ROWS + 2 * FACE


def per_device(
    rhs_field, guess, inverse_diag, lower_block, upper_block, west_block, east_block, inflow_map
):
    wide = lax.axis_size("span")
    layers = lax.axis_size("stream")
    place = lax.axis_index("stream").astype(jnp.int32).reshape(1)
    along = lax.axis_index("span").astype(jnp.int32).reshape(1)
    from_far = lax.ppermute(guess, "span", [(i, (i - 1 + 2 * (i & 1)) % wide) for i in range(wide)])
    from_near = lax.ppermute(guess, "span", [(i, i ^ 1) for i in range(wide)])
    args = (guess, upper_block, inflow_map, inverse_diag, lower_block, rhs_field, west_block, east_block)
    ahead, swap, upper, inv, low, up, rhs, west, east = call(
        first_kernel,
        (
            f32(2, 8, FACE), f32(8, LANES), f32(LEVELS + 1, 8, LANES),
            *(f32(*a.shape) for a in (inverse_diag, lower_block, upper_block, rhs_field, west_block, east_block)),
        ),
        *args, place, along,
        hbm=range(8), smem=(8, 9),
        scratch=(pltpu.VMEM(guess.shape, F32), pltpu.SMEM(inflow_map.shape, jnp.int32), pltpu.SemaphoreType.DMA((8,))),
    )
    maps = call(maps_kernel, f32(LONG + 8 * FACE, LANES), inv, low, up, rhs, west, east, ahead, swap)
    relayed = lax.ppermute(ahead, "stream", [(i + 8, i + 1) for i in range(0, layers - 8, 8)])
    own, terms = call(
        vectors_kernel, (f32(LONG, LANES), f32(2, 16, FACE)),
        maps, upper, from_near, from_far, relayed,
    )

    def across(x, distance):
        return lax.ppermute(x, "stream", [(i, i ^ distance) for i in range(layers)])

    got = across(own, 1)
    chain, lefts = call(
        first_pair_kernel, (f32(3 * FACE + 8, LANES), f32(2, FACE, LANES)), upper, own, got, relayed
    )
    groups = [[8 * g + j for j in range(8)] for g in range(layers // 8)]
    chains = lax.all_gather(chain, "stream", axis_index_groups=groups)
    eight, halves, pair_lefts = call(
        four_kernel, (f32(ROWS, LANES), f32(2, ROWS, LANES), f32(4, 2, FACE, LANES)), chains
    )
    here = (f32(2, 3, FACE, LANES), f32(8, LANES))
    got8 = across(eight, 8)
    spot, turn = call(four_place_kernel, here, place, upper, own, got, lefts, chains, pair_lefts, halves, smem=(0,))
    terms, eight = lax.optimization_barrier((terms, eight))
    zin, zout, base = call(rest_kernel, tuple(f32(2, DOF, LANES) for _ in range(3)), inv, low, rhs, west, east, terms)
    fixed, free = call(
        answer_kernel, (f32(2, 8, DOF), f32(2, DOF, 2 * LANES)), spot, turn, zin, zout, base
    )
    got8, fixed, free, turn = lax.optimization_barrier((got8, fixed, free, turn))
    chain = call(sixteen_kernel, f32(2 * FACE + 8, LANES), upper, eight, got8)
    groups = [
        [16 * i + 8 * odd + 2 * z + c for i in range(layers // 16) for c in range(2)]
        for odd in range(2)
        for z in range(4)
    ]
    sixteens = lax.all_gather(chain, "stream", axis_index_groups=groups)
    out = call(last_kernel, f32(8, 2, DOF), upper, sixteens, eight, got8, turn, fixed, free)
    return out[None, None]


def solution(mesh):
    in_specs = (
        P("stream", "span", None, None, None),
        P("stream", "span", None, None, None),
        P("stream", "span", None, None, None),
        P("stream", "span", None, None, None),
        P("stream", "span", None, None, None),
        P("stream", "span", None, None, None),
        P("stream", "span", None, None, None),
        P("stream", "span", None),
    )
    out_specs = P("stream", "span", None, None, None)
    return jax.shard_map(
        per_device, mesh=mesh, in_specs=in_specs, out_specs=out_specs, check_vma=False
    )
```

```python
import functools

import jax
import jax.numpy as jnp
from jax import lax
from jax.experimental import pallas as pl
from jax.experimental.pallas import tpu as pltpu
from jax.sharding import PartitionSpec as P

NVAR = 5
NB = 4
FACE = 80
DOF = 320
LANES = 128
VEC = FACE
REST = FACE + 8
HALF = LANES - REST
BF16 = jnp.bfloat16
F32 = jnp.float32
NN = (((1,), (0,)), ((), ()))
NT = (((1,), (1,)), ((), ()))


def split(x):
    hi = x.astype(BF16)
    return hi, (x - hi.astype(F32)).astype(BF16)


def dot(a, b, dims=NN):
    ah, al = split(a)
    bh, bl = split(b)
    one = functools.partial(lax.dot_general, dimension_numbers=dims, preferred_element_type=F32)
    return one(ah, bh) + (one(ah, bl) + one(al, bh))


def pick(x, onehot, dims=NN):
    hi = x.astype(BF16).astype(F32)
    mid = (x - hi).astype(BF16).astype(F32)
    low = x - hi - mid
    rows = x.shape[0]
    parts = jnp.concatenate([hi, mid, low], axis=0).astype(BF16)
    made = lax.dot_general(parts, onehot, dimension_numbers=dims, preferred_element_type=F32)
    return made[:rows] + made[rows : 2 * rows] + made[2 * rows :]


def stream_pick(j, width=FACE):
    d = lax.broadcasted_iota(jnp.int32, (DOF, width), 0)
    f = lax.broadcasted_iota(jnp.int32, (DOF, width), 1)
    step = NB * NB
    return ((d == (f // step) * (NB * step) + j * step + f % step) & (f < FACE)).astype(F32).astype(BF16)


def span_pick(j, width=FACE):
    d = lax.broadcasted_iota(jnp.int32, (DOF, width), 0)
    f = lax.broadcasted_iota(jnp.int32, (DOF, width), 1)
    return ((d == (f // NB) * (NB * NB) + j * NB + f % NB) & (f < FACE)).astype(F32).astype(BF16)


def stream_rows(x, j):
    step = NB * NB
    return jnp.concatenate(
        [x[(v * NB + j) * step : (v * NB + j + 1) * step] for v in range(NVAR)], axis=0
    )


def place_rows(x, j):
    step = NB * NB
    zeros = jnp.zeros((step, x.shape[1]), x.dtype)
    parts = []
    for v in range(NVAR):
        for a in range(NB):
            parts.append(x[v * step : (v + 1) * step] if a == j else zeros)
    return jnp.concatenate(parts, axis=0)


def lane_of(shape):
    return lax.broadcasted_iota(jnp.int32, shape, 1)


def pack(ab, be, d):
    lane = lane_of(ab.shape)
    left = jnp.where(lane < REST, ab, pltpu.roll(d, REST, 1))
    right = jnp.where(lane < REST, be, pltpu.roll(d, REST - HALF, 1))
    return left, right


def unpack_d(left, right):
    lane = lane_of(left.shape)
    return jnp.where(
        lane < HALF, pltpu.roll(left, LANES - REST, 1), pltpu.roll(right, LANES - REST + HALF, 1)
    )


def tall(x):
    return jnp.concatenate([x, jnp.zeros((LANES - FACE, x.shape[1]), x.dtype)], axis=0)


def widen(x):
    return jnp.concatenate([x, jnp.zeros((x.shape[0], LANES - x.shape[1]), x.dtype)], axis=1)


def side(x):
    x = widen(x)
    before = jnp.zeros((VEC, LANES), x.dtype)
    after = jnp.zeros((LANES - REST, LANES), x.dtype)
    return jnp.concatenate([before, x, after], axis=0)


def vec_only(x):
    lane = lane_of(x.shape)
    return jnp.where((lane >= VEC) & (lane < REST), x, 0.0)


class Segment:
    def __init__(self, left, right, swap):
        self.left, self.right, self.swap = left, right, swap

    @staticmethod
    def of(ref):
        left = [ref[2 * p * FACE : (2 * p + 1) * FACE] for p in range(2)]
        right = [ref[(2 * p + 1) * FACE : (2 * p + 2) * FACE] for p in range(2)]
        return Segment(left, right, ref[4 * FACE : 4 * FACE + 8])

    def write(self, ref):
        for p in range(2):
            ref[2 * p * FACE : (2 * p + 1) * FACE] = self.left[p]
            ref[(2 * p + 1) * FACE : (2 * p + 2) * FACE] = self.right[p]
        ref[4 * FACE : 4 * FACE + 8] = self.swap


def tails_of(ref):
    return [ref[ROWS + p * FACE : ROWS + (p + 1) * FACE] for p in range(2)]


def write_tails(ref, tails):
    for p in range(2):
        ref[ROWS + p * FACE : ROWS + (p + 1) * FACE] = tails[p]


def lagged_left(seg, tails, after):
    return [seg.left[p] - vec_only(dot(tails[p], tall(behind(seg.swap, after, p)))) for p in range(2)]


def behind(swap, pair, p):
    return jnp.where(swap[:1] > 0.5, pair[1 - p], pair[p])


def join(first, second):
    lefts, rights = [], []
    for p in range(2):
        left1, right1 = first.left[p], first.right[p]
        left2, right2 = behind(first.swap, second.left, p), behind(first.swap, second.right, p)
        d1, d2 = unpack_d(left1, right1), unpack_d(left2, right2)
        lane = lane_of(left1.shape)
        through = dot(jnp.concatenate([left2, d2], axis=0), tall(left1))
        ab = through[:FACE] + vec_only(left2)
        back = through[FACE:] + vec_only(right2)
        both = dot(right1, tall(jnp.concatenate([right2, back], axis=1)))
        be = jnp.where(lane < VEC, both[:, :LANES], right1 + both[:, LANES:])
        left, right = pack(ab, be, d1 + both[:, LANES:])
        lefts.append(left)
        rights.append(right)
    return Segment(lefts, rights, jnp.abs(first.swap - second.swap))


def ordered(upper, own, got):
    up = upper[:1] > 0.5

    def pair(a, b):
        return jnp.where(up, a, b)

    def seg(a, b):
        return Segment(
            [pair(a.left[p], b.left[p]) for p in range(2)],
            [pair(a.right[p], b.right[p]) for p in range(2)],
            pair(a.swap, b.swap),
        )

    return seg(got, own), seg(own, got)


def columns_of(rows):
    before = jnp.zeros((VEC, DOF), F32)
    after = jnp.zeros((LANES - REST, DOF), F32)
    return jnp.concatenate([before, rows, after], axis=0).T


def make_maps(inv, low, up, rhs, west, east, coupled, flag, own):
    tables = jnp.concatenate([span_pick(0, LANES), span_pick(3, LANES), stream_pick(3, LANES)], axis=1)
    lane = lane_of((FACE, LANES))
    made, corners = [], []
    for n in range(2):
        m, u = inv[0, 0, n], up[0, 0, n]
        both = jnp.concatenate([stream_rows(m, 3), dot(u, stream_rows(m, 0))], axis=0)
        z = dot(both, widen(place_rows(low[0, 0, n], 0)) + columns_of(rhs[0, 0, :, n, :]))
        cut = pick(both, tables)
        for i in range(2):
            at = LONG + (2 * n + i) * 2 * FACE
            block = (west, east)[i][0, 0, n]
            own[at : at + 2 * FACE] = dot(cut[:, i * LANES : (i + 1) * LANES], tall(widen(block)))
        corners.append(cut[:FACE, 2 * LANES :])
        ahead, down = z[:FACE], z[FACE:]
        made.append(
            pack(
                jnp.where(lane < VEC, -ahead, ahead),
                jnp.where(lane < VEC, -cut[FACE:, 2 * LANES :], down),
                -down,
            )
        )
    Segment(
        [behind(flag, [made[0][0], made[1][0]], p) for p in range(2)],
        [behind(flag, [made[0][1], made[1][1]], p) for p in range(2)],
        flag,
    ).write(own)
    write_tails(own, [behind(flag, corners, p) + side(coupled[p]).T[:FACE] for p in range(2)])


def flag_of(which):
    return jnp.full((8, LANES), which[0, 0, 0].astype(F32), F32)


def first_kernel(
    guess_hbm, up_hbm, map_hbm, inv_hbm, low_hbm, rhs_hbm, west_hbm, east_hbm, place, along,
    lag, swap, upper, inv, low, rhs, west, east, own, guess, up, which, sems,
):
    pairs = [(guess_hbm, guess), (up_hbm, up), (map_hbm, which), (inv_hbm, inv), (low_hbm, low), (rhs_hbm, rhs)]
    pairs += [(west_hbm, west), (east_hbm, east)]
    copies = [pltpu.make_async_copy(a, b, sems.at[i]) for i, (a, b) in enumerate(pairs)]
    for copy in copies:
        copy.start()
    for level in range(LEVELS):
        bit = (place[0] >> level) & 1
        upper[level] = jnp.full((8, LANES), bit.astype(F32), F32)
    upper[LEVELS] = jnp.full((8, LANES), (along[0] & 1).astype(F32), F32)
    pin = stream_pick(0)
    for copy in copies[:3]:
        copy.wait()
    both = pick(jnp.concatenate([guess[0, 0, :, n, :] for n in range(2)], axis=0), pin)
    flag = flag_of(which)
    swap[...] = flag
    swapped = flag[:, :FACE] > 0.5
    made = []
    for n in range(2):
        made.append(dot(both[8 * n : 8 * n + 8], up[0, 0, n], NT))
    for p in range(2):
        lag[p] = jnp.where(swapped, made[1 - p], made[p])
    for copy in copies[3:]:
        copy.wait()
    make_maps(inv, low, up, rhs, west, east, lag, flag, own)


def vectors_kernel(maps, upper, from_near, from_far, relayed, own, terms):
    odd = upper[LEVELS][:1, :1] > 0.5
    near = jnp.concatenate([from_near[0, 0, :, n, :] for n in range(2)], axis=0)
    far = jnp.concatenate([from_far[0, 0, :, n, :] for n in range(2)], axis=0)
    from_west = pick(jnp.where(odd, near, far), span_pick(3))
    from_east = pick(jnp.where(odd, far, near), span_pick(0))
    terms[0], terms[1] = from_west, from_east
    b, e = [], []
    for n in range(2):
        rows = slice(8 * n, 8 * n + 8)
        sides = jnp.concatenate([side(from_west[rows]), side(from_east[rows])], axis=1)
        at = LONG + 2 * n * 2 * FACE
        cuts = jnp.concatenate([maps[at + i * 2 * FACE : at + (i + 1) * 2 * FACE] for i in range(2)], axis=1)
        both = dot(cuts, sides, NT)
        b.append(both[:FACE])
        e.append(both[FACE:])
    seg = Segment.of(maps)
    Segment(
        [seg.left[p] - behind(seg.swap, b, p) for p in range(2)],
        [seg.right[p] - behind(seg.swap, e, p) for p in range(2)],
        seg.swap,
    ).write(own)
    write_tails(own, tails_of(maps))


def rest_kernel(inv, low, rhs, west, east, terms, zin, zout, base):
    pout = stream_pick(3, LANES)
    lane = lane_of((DOF, LANES))
    made = [
        jnp.concatenate([dot(terms[i, 8 * n : 8 * n + 8], block[0, 0, n], NT) for n in range(2)], axis=0)
        for i, block in enumerate((west, east))
    ]
    halo = pick(made[0], span_pick(0), NT) + pick(made[1], span_pick(3), NT)
    for n in range(2):
        m = inv[0, 0, n]
        h = rhs[0, 0, :, n, :] - halo[8 * n : 8 * n + 8]
        z = dot(m, widen(place_rows(low[0, 0, n], 0)) + columns_of(h))
        zout[n] = pick(m, pout)
        zin[n] = jnp.where(lane < VEC, z, 0.0)
        base[n] = vec_only(z)


def sixteen_kernel(upper, own, got, out):
    both = join(*ordered(upper[3], Segment.of(own), Segment.of(got)))
    second = upper[0][:1] > 0.5
    for i, pair in enumerate((both.left, both.right)):
        out[i * FACE : (i + 1) * FACE] = jnp.where(second, pair[1], pair[0])
    out[2 * FACE :] = both.swap


def first_pair_kernel(upper, own, got, relayed, out, lefts):
    first, second = ordered(upper[0], Segment.of(own), Segment.of(got))
    up = upper[0][:1] > 0.5
    mine, other = tails_of(own), tails_of(got)
    tails1 = [jnp.where(up, other[p], mine[p]) for p in range(2)]
    tails2 = [jnp.where(up, mine[p], other[p]) for p in range(2)]
    first = Segment(lagged_left(first, tails1, tails2), first.right, first.swap)
    both = join(first, second)
    lane = lane_of((FACE, LANES))
    tails = [jnp.where(lane < VEC, behind(first.swap, tails2, p), tails1[p]) for p in range(2)]
    behind_eight = sum(pltpu.roll(side(relayed[p]).T[:FACE], 8 * (p + 1), 1) for p in range(2))
    for p in range(2):
        lefts[p] = first.left[p]
    for i, pair in enumerate((both.left, both.right, tails)):
        out[i * FACE : (i + 1) * FACE] = jnp.where(up, pair[1], pair[0]) + (behind_eight if i == 2 else 0.0)
    out[3 * FACE :] = both.swap


def four_kernel(got, out, halves, lefts):
    def chain(i, p, tile):
        return got[2 * i + p, tile * FACE : (tile + 1) * FACE]

    tails = [[chain(i, p, 2) for p in range(2)] for i in range(4)]
    last = [pltpu.roll(tails[0][1], LANES - 8 * (p + 1), 1) for p in range(2)]
    segs = []
    for i in range(4):
        seg = Segment([chain(i, p, 0) for p in range(2)], [chain(i, p, 1) for p in range(2)], got[2 * i, 3 * FACE :])
        seg = Segment(lagged_left(seg, tails[i], tails[i + 1] if i < 3 else last), seg.right, seg.swap)
        for p in range(2):
            lefts[i, p] = seg.left[p]
        segs.append(seg)
    both = [join(segs[2 * i], segs[2 * i + 1]) for i in range(2)]
    join(*both).write(out)
    for i in range(2):
        both[i].write(halves.at[i])


def start_place():
    eye = (lax.broadcasted_iota(jnp.int32, (FACE, LANES), 0) == lane_of((FACE, LANES))).astype(F32)
    zero = jnp.zeros((FACE, LANES), F32)
    return [[eye, zero, eye] for _ in range(2)]


def widen_place(place, upper, own, got):
    lane = lane_of((FACE, LANES))
    keep = lane < REST
    up = upper[:1] > 0.5
    made = []
    for p in range(2):
        near = [behind(got.swap, [place[0][i], place[1][i]], p) for i in range(3)]
        sib = tall(got.left[p])
        moved = dot(jnp.concatenate([near[0], near[1]], axis=0), sib)
        above = [
            jnp.where(keep, moved[:FACE], 0.0) + vec_only(near[0]),
            jnp.where(keep, moved[FACE:], 0.0) + vec_only(near[1]),
            near[2],
        ]
        left2, right2 = behind(own.swap, got.left, p), behind(own.swap, got.right, p)
        back = dot(unpack_d(left2, right2), tall(own.left[p])) + vec_only(right2)
        turned = dot(place[p][2], tall(jnp.concatenate([back, right2], axis=1)))
        below = [
            place[p][0],
            place[p][1] + jnp.where(keep, turned[:, :LANES], 0.0),
            jnp.where(lane < VEC, turned[:, LANES:], 0.0),
        ]
        made.append([jnp.where(up, above[i], below[i]) for i in range(3)])
    return made


def read_place(ref):
    return [[ref[p, i] for i in range(3)] for p in range(2)]


def write_place(ref, place):
    for p in range(2):
        for i in range(3):
            ref[p, i] = place[p][i]


def four_place_kernel(at, upper, one, one_got, lefts, got, pair_lefts, halves, out, swap_out):
    mine, other = Segment.of(one), Segment.of(one_got)
    up = upper[0][:1] > 0.5
    mine.left = [jnp.where(up, mine.left[p], lefts[p]) for p in range(2)]
    other.left = [jnp.where(up, lefts[p], other.left[p]) for p in range(2)]
    made = widen_place(start_place(), upper[0], mine, other)
    x = jnp.abs(mine.swap - jnp.where(upper[0] > 0.5, other.swap, 0.0))
    j = (at[0] >> 1) & 3
    half = j >> 1

    def pair_of(i):
        right = [got[2 * i + p, FACE : 2 * FACE] for p in range(2)]
        return Segment([pair_lefts[i, p] for p in range(2)], right, got[2 * i, 3 * FACE :])

    mine, other = pair_of(j), pair_of(j ^ 1)
    made = widen_place(made, upper[1], mine, other)
    x = jnp.abs(x - jnp.where(upper[1] > 0.5, other.swap, 0.0))
    mine, other = Segment.of(halves.at[half]), Segment.of(halves.at[1 - half])
    write_place(out, widen_place(made, upper[2], mine, other))
    swap_out[...] = jnp.abs(x - jnp.where(upper[2] > 0.5, other.swap, 0.0))


def answer_kernel(place, turn, zin, zout, base, fixed, free):
    made = read_place(place)
    x = turn[...]
    for n in range(2):
        p0, q0, r0 = [behind(x, [made[0][i], made[1][i]], n) for i in range(3)]
        f = dot(jnp.concatenate([zin[n], zout[n]], axis=1), jnp.concatenate([tall(p0), tall(q0)], axis=0))
        free[n] = jnp.concatenate([f, dot(zout[n], tall(r0))], axis=1)
        fixed[n] = (base[n] - f).T[VEC:REST]


def last_kernel(upper, got, own, got8, turn, fixed, free, out):
    def chain(i, p, tile):
        return got[2 * i + p, tile * FACE : (tile + 1) * FACE]

    def stack(*parts):
        return jnp.concatenate(parts, axis=0)

    def beside(*parts):
        return jnp.concatenate(parts, axis=1)

    segs = [
        Segment([chain(i, p, 0) for p in range(2)], [chain(i, p, 1) for p in range(2)], got[2 * i, 2 * FACE :])
        for i in range(4)
    ]
    d = [None] + [[unpack_d(segs[i].left[p], segs[i].right[p]) for p in range(2)] for i in (1, 2, 3)]
    w0, w1, w2 = [seg.swap for seg in segs[:3]]
    mine, other = Segment.of(own), Segment.of(got8)
    up = upper[3][:1] > 0.5
    zero = jnp.zeros((FACE, LANES), F32)

    t1 = [behind(w0, [vec_only(segs[0].left[q]) for q in range(2)], p) for p in range(2)]
    steps = [dot(stack(d[1][p], segs[1].left[p]), tall(t1[p])) for p in range(2)]
    down1 = [steps[p][:FACE] + vec_only(segs[1].right[p]) for p in range(2)]
    t2 = [vec_only(steps[p][FACE:] + segs[1].left[p]) for p in range(2)]
    t2 = [behind(w1, t2, p) for p in range(2)]
    turned = [
        dot(behind(w2, d[3], p), tall(segs[2].left[p])) + vec_only(behind(w2, segs[3].right, p)) for p in range(2)
    ]
    both_back = [dot(segs[1].right[p], tall(behind(w1, segs[2].right, p))) for p in range(2)]
    near_right = [behind(mine.swap, other.right, p) for p in range(2)]
    near_d = [unpack_d(other.left[p], other.right[p]) for p in range(2)]
    near_back = [
        dot(behind(mine.swap, near_d, p), tall(mine.left[p])) + vec_only(near_right[p]) for p in range(2)
    ]

    steps = [dot(stack(d[2][p], turned[p], segs[2].left[p]), tall(t2[p])) for p in range(2)]
    down2 = [vec_only(steps[p][:FACE]) for p in range(2)]
    c2 = [vec_only(steps[p][FACE : 2 * FACE] + turned[p]) for p in range(2)]
    t3 = [vec_only(steps[p][2 * FACE :] + segs[2].left[p]) for p in range(2)]
    t3 = [behind(w2, t3, p) for p in range(2)]

    c1 = [vec_only(dot(segs[2].right[p], tall(c2[p])) + down2[p] + segs[2].right[p]) for p in range(2)]
    c1 = [behind(w1, c1, p) for p in range(2)]
    c0 = []
    for p in range(2):
        made = dot(
            beside(both_back[p], segs[1].right[p]), stack(tall(behind(w1, c2, p)), tall(behind(w1, down2, p)))
        )
        c0.append(vec_only(made + both_back[p] + down1[p]))
    c0 = [behind(w0, c0, p) for p in range(2)]

    def here(a, b, c, e):
        low, high = upper[4][:1] > 0.5, upper[5][:1] > 0.5
        return [jnp.where(high, jnp.where(low, e[p], c[p]), jnp.where(low, b[p], a[p])) for p in range(2)]

    t_in = here([zero, zero], t1, t2, t3)
    c_out = here(c0, c1, c2, [zero, zero])
    through = [vec_only(dot(other.left[p], tall(t_in[p])) + other.left[p]) for p in range(2)]
    t_at, c_at = [], []
    for p in range(2):
        back = dot(beside(near_back[p], near_right[p]), stack(tall(t_in[p]), tall(c_out[p])))
        t_at.append(jnp.where(up, behind(other.swap, through, p), t_in[p]))
        c_at.append(jnp.where(up, behind(other.swap, c_out, p), vec_only(back + near_back[p])))
    for n in range(2):
        rows = [widen(behind(turn[...], pair, n).T[VEC:REST]) for pair in (t_at, c_at)]
        out[:, n, :] = fixed[n] - dot(beside(*rows), free[n], NT)


HBM = pl.BlockSpec(memory_space=pltpu.HBM)
VMEM = pl.BlockSpec(memory_space=pltpu.VMEM)
SMEM = pl.BlockSpec(memory_space=pltpu.SMEM)


def call(kernel, out_shape, *operands, hbm=(), smem=(), scratch=()):
    specs = [HBM if i in hbm else SMEM if i in smem else VMEM for i in range(len(operands))]
    several = isinstance(out_shape, tuple)
    operands = [
        pltpu.with_memory_space_constraint(x, pltpu.HBM) if i in hbm else x for i, x in enumerate(operands)
    ]
    return pl.pallas_call(
        kernel,
        out_shape=out_shape,
        in_specs=specs,
        out_specs=tuple(VMEM for _ in out_shape) if several else VMEM,
        scratch_shapes=list(scratch),
        cost_estimate=pl.CostEstimate(flops=0, bytes_accessed=1 << 20, transcendentals=0),
        compiler_params=pltpu.CompilerParams(vmem_limit_bytes=24 * 1024 * 1024),
    )(*operands)


def f32(*shape):
    return jax.ShapeDtypeStruct(shape, F32)


LEVELS = 6
ROWS = 4 * FACE + 8
LONG = ROWS + 2 * FACE


def per_device(
    rhs_field, guess, inverse_diag, lower_block, upper_block, west_block, east_block, inflow_map
):
    wide = lax.axis_size("span")
    layers = lax.axis_size("stream")
    place = lax.axis_index("stream").astype(jnp.int32).reshape(1)
    along = lax.axis_index("span").astype(jnp.int32).reshape(1)
    from_far = lax.ppermute(guess, "span", [(i, (i - 1 + 2 * (i & 1)) % wide) for i in range(wide)])
    from_near = lax.ppermute(guess, "span", [(i, i ^ 1) for i in range(wide)])
    args = (guess, upper_block, inflow_map, inverse_diag, lower_block, rhs_field, west_block, east_block)
    ahead, swap, upper, inv, low, rhs, west, east, maps = call(
        first_kernel,
        (
            f32(2, 8, FACE), f32(8, LANES), f32(LEVELS + 1, 8, LANES),
            *(f32(*a.shape) for a in (inverse_diag, lower_block, rhs_field, west_block, east_block)),
            f32(LONG + 8 * FACE, LANES),
        ),
        *args, place, along,
        hbm=range(8), smem=(8, 9),
        scratch=(pltpu.VMEM(guess.shape, F32), pltpu.VMEM(upper_block.shape, F32), pltpu.SMEM(inflow_map.shape, jnp.int32), pltpu.SemaphoreType.DMA((8,))),
    )
    relayed = lax.ppermute(ahead, "stream", [(i + 8, i + 1) for i in range(0, layers - 8, 8)])
    own, terms = call(
        vectors_kernel, (f32(LONG, LANES), f32(2, 16, FACE)),
        maps, upper, from_near, from_far, relayed,
    )

    def across(x, distance):
        return lax.ppermute(x, "stream", [(i, i ^ distance) for i in range(layers)])

    got = across(own, 1)
    chain, lefts = call(
        first_pair_kernel, (f32(3 * FACE + 8, LANES), f32(2, FACE, LANES)), upper, own, got, relayed
    )
    groups = [[8 * g + j for j in range(8)] for g in range(layers // 8)]
    chains = lax.all_gather(chain, "stream", axis_index_groups=groups)
    eight, halves, pair_lefts = call(
        four_kernel, (f32(ROWS, LANES), f32(2, ROWS, LANES), f32(4, 2, FACE, LANES)), chains
    )
    here = (f32(2, 3, FACE, LANES), f32(8, LANES))
    got8 = across(eight, 8)
    spot, turn = call(four_place_kernel, here, place, upper, own, got, lefts, chains, pair_lefts, halves, smem=(0,))
    terms, eight = lax.optimization_barrier((terms, eight))
    zin, zout, base = call(rest_kernel, tuple(f32(2, DOF, LANES) for _ in range(3)), inv, low, rhs, west, east, terms)
    fixed, free = call(
        answer_kernel, (f32(2, 8, DOF), f32(2, DOF, 2 * LANES)), spot, turn, zin, zout, base
    )
    got8, fixed, free, turn = lax.optimization_barrier((got8, fixed, free, turn))
    chain = call(sixteen_kernel, f32(2 * FACE + 8, LANES), upper, eight, got8)
    groups = [
        [16 * i + 8 * odd + 2 * z + c for i in range(layers // 16) for c in range(2)]
        for odd in range(2)
        for z in range(4)
    ]
    sixteens = lax.all_gather(chain, "stream", axis_index_groups=groups)
    out = call(last_kernel, f32(8, 2, DOF), upper, sixteens, eight, got8, turn, fixed, free)
    return out[None, None]


def solution(mesh):
    in_specs = (
        P("stream", "span", None, None, None),
        P("stream", "span", None, None, None),
        P("stream", "span", None, None, None),
        P("stream", "span", None, None, None),
        P("stream", "span", None, None, None),
        P("stream", "span", None, None, None),
        P("stream", "span", None, None, None),
        P("stream", "span", None),
    )
    out_specs = P("stream", "span", None, None, None)
    return jax.shard_map(
        per_device, mesh=mesh, in_specs=in_specs, out_specs=out_specs, check_vma=False
    )
```

```python
import functools

import jax
import jax.numpy as jnp
from jax import lax
from jax.experimental import pallas as pl
from jax.experimental.pallas import tpu as pltpu
from jax.sharding import PartitionSpec as P

NVAR = 5
NB = 4
FACE = 80
DOF = 320
LANES = 128
VEC = FACE
REST = FACE + 8
HALF = LANES - REST
BF16 = jnp.bfloat16
F32 = jnp.float32
NN = (((1,), (0,)), ((), ()))
NT = (((1,), (1,)), ((), ()))


def split(x):
    hi = x.astype(BF16)
    return hi, (x - hi.astype(F32)).astype(BF16)


def dot(a, b, dims=NN):
    ah, al = split(a)
    bh, bl = split(b)
    one = functools.partial(lax.dot_general, dimension_numbers=dims, preferred_element_type=F32)
    return one(ah, bh) + (one(ah, bl) + one(al, bh))


def pick(x, onehot, dims=NN):
    hi = x.astype(BF16).astype(F32)
    mid = (x - hi).astype(BF16).astype(F32)
    low = x - hi - mid
    rows = x.shape[0]
    parts = jnp.concatenate([hi, mid, low], axis=0).astype(BF16)
    made = lax.dot_general(parts, onehot, dimension_numbers=dims, preferred_element_type=F32)
    return made[:rows] + made[rows : 2 * rows] + made[2 * rows :]


def stream_pick(j, width=FACE):
    d = lax.broadcasted_iota(jnp.int32, (DOF, width), 0)
    f = lax.broadcasted_iota(jnp.int32, (DOF, width), 1)
    step = NB * NB
    return ((d == (f // step) * (NB * step) + j * step + f % step) & (f < FACE)).astype(F32).astype(BF16)


def span_pick(j, width=FACE):
    d = lax.broadcasted_iota(jnp.int32, (DOF, width), 0)
    f = lax.broadcasted_iota(jnp.int32, (DOF, width), 1)
    return ((d == (f // NB) * (NB * NB) + j * NB + f % NB) & (f < FACE)).astype(F32).astype(BF16)


def stream_rows(x, j):
    step = NB * NB
    return jnp.concatenate(
        [x[(v * NB + j) * step : (v * NB + j + 1) * step] for v in range(NVAR)], axis=0
    )


def place_rows(x, j):
    step = NB * NB
    zeros = jnp.zeros((step, x.shape[1]), x.dtype)
    parts = []
    for v in range(NVAR):
        for a in range(NB):
            parts.append(x[v * step : (v + 1) * step] if a == j else zeros)
    return jnp.concatenate(parts, axis=0)


def lane_of(shape):
    return lax.broadcasted_iota(jnp.int32, shape, 1)


def pack(ab, be, d):
    lane = lane_of(ab.shape)
    left = jnp.where(lane < REST, ab, pltpu.roll(d, REST, 1))
    right = jnp.where(lane < REST, be, pltpu.roll(d, REST - HALF, 1))
    return left, right


def unpack_d(left, right):
    lane = lane_of(left.shape)
    return jnp.where(
        lane < HALF, pltpu.roll(left, LANES - REST, 1), pltpu.roll(right, LANES - REST + HALF, 1)
    )


def tall(x):
    return jnp.concatenate([x, jnp.zeros((LANES - FACE, x.shape[1]), x.dtype)], axis=0)


def widen(x):
    return jnp.concatenate([x, jnp.zeros((x.shape[0], LANES - x.shape[1]), x.dtype)], axis=1)


def side(x):
    x = widen(x)
    before = jnp.zeros((VEC, LANES), x.dtype)
    after = jnp.zeros((LANES - REST, LANES), x.dtype)
    return jnp.concatenate([before, x, after], axis=0)


def vec_only(x):
    lane = lane_of(x.shape)
    return jnp.where((lane >= VEC) & (lane < REST), x, 0.0)


class Segment:
    def __init__(self, left, right, swap):
        self.left, self.right, self.swap = left, right, swap

    @staticmethod
    def of(ref):
        left = [ref[2 * p * FACE : (2 * p + 1) * FACE] for p in range(2)]
        right = [ref[(2 * p + 1) * FACE : (2 * p + 2) * FACE] for p in range(2)]
        return Segment(left, right, ref[4 * FACE : 4 * FACE + 8])

    def write(self, ref):
        for p in range(2):
            ref[2 * p * FACE : (2 * p + 1) * FACE] = self.left[p]
            ref[(2 * p + 1) * FACE : (2 * p + 2) * FACE] = self.right[p]
        ref[4 * FACE : 4 * FACE + 8] = self.swap


def tails_of(ref):
    return [ref[ROWS + p * FACE : ROWS + (p + 1) * FACE] for p in range(2)]


def write_tails(ref, tails):
    for p in range(2):
        ref[ROWS + p * FACE : ROWS + (p + 1) * FACE] = tails[p]


def lagged_left(seg, tails, after):
    return [seg.left[p] - vec_only(dot(tails[p], tall(behind(seg.swap, after, p)))) for p in range(2)]


def behind(swap, pair, p):
    return jnp.where(swap[:1] > 0.5, pair[1 - p], pair[p])


def join(first, second):
    lefts, rights = [], []
    for p in range(2):
        left1, right1 = first.left[p], first.right[p]
        left2, right2 = behind(first.swap, second.left, p), behind(first.swap, second.right, p)
        d1, d2 = unpack_d(left1, right1), unpack_d(left2, right2)
        lane = lane_of(left1.shape)
        through = dot(jnp.concatenate([left2, d2], axis=0), tall(left1))
        ab = through[:FACE] + vec_only(left2)
        back = through[FACE:] + vec_only(right2)
        both = dot(right1, tall(jnp.concatenate([right2, back], axis=1)))
        be = jnp.where(lane < VEC, both[:, :LANES], right1 + both[:, LANES:])
        left, right = pack(ab, be, d1 + both[:, LANES:])
        lefts.append(left)
        rights.append(right)
    return Segment(lefts, rights, jnp.abs(first.swap - second.swap))


def ordered(upper, own, got):
    up = upper[:1] > 0.5

    def pair(a, b):
        return jnp.where(up, a, b)

    def seg(a, b):
        return Segment(
            [pair(a.left[p], b.left[p]) for p in range(2)],
            [pair(a.right[p], b.right[p]) for p in range(2)],
            pair(a.swap, b.swap),
        )

    return seg(got, own), seg(own, got)


def columns_of(rows):
    before = jnp.zeros((VEC, DOF), F32)
    after = jnp.zeros((LANES - REST, DOF), F32)
    return jnp.concatenate([before, rows, after], axis=0).T


def make_maps(inv, low, up, rhs, west, east, coupled, flag, own):
    tables = jnp.concatenate([span_pick(0, LANES), span_pick(3, LANES), stream_pick(3, LANES)], axis=1)
    lane = lane_of((FACE, LANES))
    made, corners = [], []
    for n in range(2):
        m, u = inv[0, 0, n], up[0, 0, n]
        both = jnp.concatenate([stream_rows(m, 3), dot(u, stream_rows(m, 0))], axis=0)
        z = dot(both, widen(place_rows(low[0, 0, n], 0)) + columns_of(rhs[0, 0, :, n, :]))
        cut = pick(both, tables)
        for i in range(2):
            at = LONG + (2 * n + i) * 2 * FACE
            block = (west, east)[i][0, 0, n]
            own[at : at + 2 * FACE] = dot(cut[:, i * LANES : (i + 1) * LANES], tall(widen(block)))
        corners.append(cut[:FACE, 2 * LANES :])
        ahead, down = z[:FACE], z[FACE:]
        made.append(
            pack(
                jnp.where(lane < VEC, -ahead, ahead),
                jnp.where(lane < VEC, -cut[FACE:, 2 * LANES :], down),
                -down,
            )
        )
    Segment(
        [behind(flag, [made[0][0], made[1][0]], p) for p in range(2)],
        [behind(flag, [made[0][1], made[1][1]], p) for p in range(2)],
        flag,
    ).write(own)
    write_tails(own, [behind(flag, corners, p) + side(coupled[p]).T[:FACE] for p in range(2)])


def flag_of(which):
    return jnp.full((8, LANES), which[0, 0, 0].astype(F32), F32)


def first_kernel(
    guess_hbm, up_hbm, map_hbm, inv_hbm, low_hbm, rhs_hbm, west_hbm, east_hbm, place, along,
    lag, swap, upper, inv, low, rhs, west, east, own, guess, up, which, sems,
):
    pairs = [(guess_hbm, guess), (up_hbm, up), (map_hbm, which), (inv_hbm, inv), (low_hbm, low), (rhs_hbm, rhs)]
    pairs += [(west_hbm, west), (east_hbm, east)]
    copies = [pltpu.make_async_copy(a, b, sems.at[i]) for i, (a, b) in enumerate(pairs)]
    for copy in copies:
        copy.start()
    for level in range(LEVELS):
        bit = (place[0] >> level) & 1
        upper[level] = jnp.full((8, LANES), bit.astype(F32), F32)
    upper[LEVELS] = jnp.full((8, LANES), (along[0] & 1).astype(F32), F32)
    pin = stream_pick(0)
    for copy in copies[:3]:
        copy.wait()
    both = pick(jnp.concatenate([guess[0, 0, :, n, :] for n in range(2)], axis=0), pin)
    flag = flag_of(which)
    swap[...] = flag
    swapped = flag[:, :FACE] > 0.5
    made = []
    for n in range(2):
        made.append(dot(both[8 * n : 8 * n + 8], up[0, 0, n], NT))
    for p in range(2):
        lag[p] = jnp.where(swapped, made[1 - p], made[p])
    for copy in copies[3:]:
        copy.wait()
    make_maps(inv, low, up, rhs, west, east, lag, flag, own)


def vectors_kernel(maps, upper, from_near, from_far, relayed, own, terms):
    odd = upper[LEVELS][:1, :1] > 0.5
    near = jnp.concatenate([from_near[0, 0, :, n, :] for n in range(2)], axis=0)
    far = jnp.concatenate([from_far[0, 0, :, n, :] for n in range(2)], axis=0)
    from_west = pick(jnp.where(odd, near, far), span_pick(3))
    from_east = pick(jnp.where(odd, far, near), span_pick(0))
    terms[0], terms[1] = from_west, from_east
    b, e = [], []
    for n in range(2):
        rows = slice(8 * n, 8 * n + 8)
        sides = jnp.concatenate([side(from_west[rows]), side(from_east[rows])], axis=1)
        at = LONG + 2 * n * 2 * FACE
        cuts = jnp.concatenate([maps[at + i * 2 * FACE : at + (i + 1) * 2 * FACE] for i in range(2)], axis=1)
        both = dot(cuts, sides, NT)
        b.append(both[:FACE])
        e.append(both[FACE:])
    seg = Segment.of(maps)
    Segment(
        [seg.left[p] - behind(seg.swap, b, p) for p in range(2)],
        [seg.right[p] - behind(seg.swap, e, p) for p in range(2)],
        seg.swap,
    ).write(own)
    write_tails(own, tails_of(maps))


def rest_kernel(inv, low, rhs, west, east, terms, zin, zout, base):
    pout = stream_pick(3, LANES)
    lane = lane_of((DOF, LANES))
    made = [
        jnp.concatenate([dot(terms[i, 8 * n : 8 * n + 8], block[0, 0, n], NT) for n in range(2)], axis=0)
        for i, block in enumerate((west, east))
    ]
    halo = pick(made[0], span_pick(0), NT) + pick(made[1], span_pick(3), NT)
    for n in range(2):
        m = inv[0, 0, n]
        h = rhs[0, 0, :, n, :] - halo[8 * n : 8 * n + 8]
        z = dot(m, widen(place_rows(low[0, 0, n], 0)) + columns_of(h))
        zout[n] = pick(m, pout)
        zin[n] = jnp.where(lane < VEC, z, 0.0)
        base[n] = vec_only(z)


def sixteen_kernel(upper, own, got, out):
    both = join(*ordered(upper[3], Segment.of(own), Segment.of(got)))
    second = upper[0][:1] > 0.5
    for i, pair in enumerate((both.left, both.right)):
        out[i * FACE : (i + 1) * FACE] = jnp.where(second, pair[1], pair[0])
    out[2 * FACE :] = both.swap


def first_pair_kernel(upper, own, got, relayed, out, lefts):
    first, second = ordered(upper[0], Segment.of(own), Segment.of(got))
    up = upper[0][:1] > 0.5
    mine, other = tails_of(own), tails_of(got)
    tails1 = [jnp.where(up, other[p], mine[p]) for p in range(2)]
    tails2 = [jnp.where(up, mine[p], other[p]) for p in range(2)]
    first = Segment(lagged_left(first, tails1, tails2), first.right, first.swap)
    both = join(first, second)
    lane = lane_of((FACE, LANES))
    tails = [jnp.where(lane < VEC, behind(first.swap, tails2, p), tails1[p]) for p in range(2)]
    behind_eight = sum(pltpu.roll(side(relayed[p]).T[:FACE], 8 * (p + 1), 1) for p in range(2))
    for p in range(2):
        lefts[p] = first.left[p]
    for i, pair in enumerate((both.left, both.right, tails)):
        out[i * FACE : (i + 1) * FACE] = jnp.where(up, pair[1], pair[0]) + (behind_eight if i == 2 else 0.0)
    out[3 * FACE :] = both.swap


def four_kernel(got, out, lefts):
    def chain(i, p, tile):
        return got[2 * i + p, tile * FACE : (tile + 1) * FACE]

    tails = [[chain(i, p, 2) for p in range(2)] for i in range(4)]
    last = [pltpu.roll(tails[0][1], LANES - 8 * (p + 1), 1) for p in range(2)]
    segs = []
    for i in range(4):
        seg = Segment([chain(i, p, 0) for p in range(2)], [chain(i, p, 1) for p in range(2)], got[2 * i, 3 * FACE :])
        seg = Segment(lagged_left(seg, tails[i], tails[i + 1] if i < 3 else last), seg.right, seg.swap)
        for p in range(2):
            lefts[i, p] = seg.left[p]
        segs.append(seg)
    both = [join(segs[2 * i], segs[2 * i + 1]) for i in range(2)]
    join(*both).write(out)


def start_place():
    eye = (lax.broadcasted_iota(jnp.int32, (FACE, LANES), 0) == lane_of((FACE, LANES))).astype(F32)
    zero = jnp.zeros((FACE, LANES), F32)
    return [[eye, zero, eye] for _ in range(2)]


def widen_place(place, upper, own, got):
    lane = lane_of((FACE, LANES))
    keep = lane < REST
    up = upper[:1] > 0.5
    made = []
    for p in range(2):
        near = [behind(got.swap, [place[0][i], place[1][i]], p) for i in range(3)]
        sib = tall(got.left[p])
        moved = dot(jnp.concatenate([near[0], near[1]], axis=0), sib)
        above = [
            jnp.where(keep, moved[:FACE], 0.0) + vec_only(near[0]),
            jnp.where(keep, moved[FACE:], 0.0) + vec_only(near[1]),
            near[2],
        ]
        left2, right2 = behind(own.swap, got.left, p), behind(own.swap, got.right, p)
        back = dot(unpack_d(left2, right2), tall(own.left[p])) + vec_only(right2)
        turned = dot(place[p][2], tall(jnp.concatenate([back, right2], axis=1)))
        below = [
            place[p][0],
            place[p][1] + jnp.where(keep, turned[:, :LANES], 0.0),
            jnp.where(lane < VEC, turned[:, LANES:], 0.0),
        ]
        made.append([jnp.where(up, above[i], below[i]) for i in range(3)])
    return made


def read_place(ref):
    return [[ref[p, i] for i in range(3)] for p in range(2)]


def write_place(ref, place):
    for p in range(2):
        for i in range(3):
            ref[p, i] = place[p][i]


def four_place_kernel(at, upper, one, one_got, lefts, got, pair_lefts, out, swap_out):
    mine, other = Segment.of(one), Segment.of(one_got)
    up = upper[0][:1] > 0.5
    mine.left = [jnp.where(up, mine.left[p], lefts[p]) for p in range(2)]
    other.left = [jnp.where(up, lefts[p], other.left[p]) for p in range(2)]
    made = widen_place(start_place(), upper[0], mine, other)
    x = jnp.abs(mine.swap - jnp.where(upper[0] > 0.5, other.swap, 0.0))
    j = (at[0] >> 1) & 3
    half = j >> 1

    def pair_of(i):
        right = [got[2 * i + p, FACE : 2 * FACE] for p in range(2)]
        return Segment([pair_lefts[i, p] for p in range(2)], right, got[2 * i, 3 * FACE :])

    mine, other = pair_of(j), pair_of(j ^ 1)
    made = widen_place(made, upper[1], mine, other)
    x = jnp.abs(x - jnp.where(upper[1] > 0.5, other.swap, 0.0))
    mine = join(pair_of(2 * half), pair_of(2 * half + 1))
    other = join(pair_of(2 - 2 * half), pair_of(3 - 2 * half))
    write_place(out, widen_place(made, upper[2], mine, other))
    swap_out[...] = jnp.abs(x - jnp.where(upper[2] > 0.5, other.swap, 0.0))


def answer_kernel(place, turn, zin, zout, base, fixed, free):
    made = read_place(place)
    x = turn[...]
    for n in range(2):
        p0, q0, r0 = [behind(x, [made[0][i], made[1][i]], n) for i in range(3)]
        f = dot(jnp.concatenate([zin[n], zout[n]], axis=1), jnp.concatenate([tall(p0), tall(q0)], axis=0))
        free[n] = jnp.concatenate([f, dot(zout[n], tall(r0))], axis=1)
        fixed[n] = (base[n] - f).T[VEC:REST]


def last_kernel(upper, got, own, got8, turn, fixed, free, out):
    def chain(i, p, tile):
        return got[2 * i + p, tile * FACE : (tile + 1) * FACE]

    def stack(*parts):
        return jnp.concatenate(parts, axis=0)

    def beside(*parts):
        return jnp.concatenate(parts, axis=1)

    segs = [
        Segment([chain(i, p, 0) for p in range(2)], [chain(i, p, 1) for p in range(2)], got[2 * i, 2 * FACE :])
        for i in range(4)
    ]
    d = [None] + [[unpack_d(segs[i].left[p], segs[i].right[p]) for p in range(2)] for i in (1, 2, 3)]
    w0, w1, w2 = [seg.swap for seg in segs[:3]]
    mine, other = Segment.of(own), Segment.of(got8)
    up = upper[3][:1] > 0.5
    zero = jnp.zeros((FACE, LANES), F32)

    t1 = [behind(w0, [vec_only(segs[0].left[q]) for q in range(2)], p) for p in range(2)]
    steps = [dot(stack(d[1][p], segs[1].left[p]), tall(t1[p])) for p in range(2)]
    down1 = [steps[p][:FACE] + vec_only(segs[1].right[p]) for p in range(2)]
    t2 = [vec_only(steps[p][FACE:] + segs[1].left[p]) for p in range(2)]
    t2 = [behind(w1, t2, p) for p in range(2)]
    turned = [
        dot(behind(w2, d[3], p), tall(segs[2].left[p])) + vec_only(behind(w2, segs[3].right, p)) for p in range(2)
    ]
    both_back = [dot(segs[1].right[p], tall(behind(w1, segs[2].right, p))) for p in range(2)]
    near_right = [behind(mine.swap, other.right, p) for p in range(2)]
    near_d = [unpack_d(other.left[p], other.right[p]) for p in range(2)]
    near_back = [
        dot(behind(mine.swap, near_d, p), tall(mine.left[p])) + vec_only(near_right[p]) for p in range(2)
    ]

    steps = [dot(stack(d[2][p], turned[p], segs[2].left[p]), tall(t2[p])) for p in range(2)]
    down2 = [vec_only(steps[p][:FACE]) for p in range(2)]
    c2 = [vec_only(steps[p][FACE : 2 * FACE] + turned[p]) for p in range(2)]
    t3 = [vec_only(steps[p][2 * FACE :] + segs[2].left[p]) for p in range(2)]
    t3 = [behind(w2, t3, p) for p in range(2)]

    c1 = [vec_only(dot(segs[2].right[p], tall(c2[p])) + down2[p] + segs[2].right[p]) for p in range(2)]
    c1 = [behind(w1, c1, p) for p in range(2)]
    c0 = []
    for p in range(2):
        made = dot(
            beside(both_back[p], segs[1].right[p]), stack(tall(behind(w1, c2, p)), tall(behind(w1, down2, p)))
        )
        c0.append(vec_only(made + both_back[p] + down1[p]))
    c0 = [behind(w0, c0, p) for p in range(2)]

    def here(a, b, c, e):
        low, high = upper[4][:1] > 0.5, upper[5][:1] > 0.5
        return [jnp.where(high, jnp.where(low, e[p], c[p]), jnp.where(low, b[p], a[p])) for p in range(2)]

    t_in = here([zero, zero], t1, t2, t3)
    c_out = here(c0, c1, c2, [zero, zero])
    through = [vec_only(dot(other.left[p], tall(t_in[p])) + other.left[p]) for p in range(2)]
    t_at, c_at = [], []
    for p in range(2):
        back = dot(beside(near_back[p], near_right[p]), stack(tall(t_in[p]), tall(c_out[p])))
        t_at.append(jnp.where(up, behind(other.swap, through, p), t_in[p]))
        c_at.append(jnp.where(up, behind(other.swap, c_out, p), vec_only(back + near_back[p])))
    for n in range(2):
        rows = [widen(behind(turn[...], pair, n).T[VEC:REST]) for pair in (t_at, c_at)]
        out[:, n, :] = fixed[n] - dot(beside(*rows), free[n], NT)


HBM = pl.BlockSpec(memory_space=pltpu.HBM)
VMEM = pl.BlockSpec(memory_space=pltpu.VMEM)
SMEM = pl.BlockSpec(memory_space=pltpu.SMEM)


def call(kernel, out_shape, *operands, hbm=(), smem=(), scratch=()):
    specs = [HBM if i in hbm else SMEM if i in smem else VMEM for i in range(len(operands))]
    several = isinstance(out_shape, tuple)
    operands = [
        pltpu.with_memory_space_constraint(x, pltpu.HBM) if i in hbm else x for i, x in enumerate(operands)
    ]
    return pl.pallas_call(
        kernel,
        out_shape=out_shape,
        in_specs=specs,
        out_specs=tuple(VMEM for _ in out_shape) if several else VMEM,
        scratch_shapes=list(scratch),
        cost_estimate=pl.CostEstimate(flops=0, bytes_accessed=1 << 20, transcendentals=0),
        compiler_params=pltpu.CompilerParams(vmem_limit_bytes=24 * 1024 * 1024),
    )(*operands)


def f32(*shape):
    return jax.ShapeDtypeStruct(shape, F32)


LEVELS = 6
ROWS = 4 * FACE + 8
LONG = ROWS + 2 * FACE


def per_device(
    rhs_field, guess, inverse_diag, lower_block, upper_block, west_block, east_block, inflow_map
):
    wide = lax.axis_size("span")
    layers = lax.axis_size("stream")
    place = lax.axis_index("stream").astype(jnp.int32).reshape(1)
    along = lax.axis_index("span").astype(jnp.int32).reshape(1)
    from_far = lax.ppermute(guess, "span", [(i, (i - 1 + 2 * (i & 1)) % wide) for i in range(wide)])
    from_near = lax.ppermute(guess, "span", [(i, i ^ 1) for i in range(wide)])
    args = (guess, upper_block, inflow_map, inverse_diag, lower_block, rhs_field, west_block, east_block)
    ahead, swap, upper, inv, low, rhs, west, east, maps = call(
        first_kernel,
        (
            f32(2, 8, FACE), f32(8, LANES), f32(LEVELS + 1, 8, LANES),
            *(f32(*a.shape) for a in (inverse_diag, lower_block, rhs_field, west_block, east_block)),
            f32(LONG + 8 * FACE, LANES),
        ),
        *args, place, along,
        hbm=range(8), smem=(8, 9),
        scratch=(pltpu.VMEM(guess.shape, F32), pltpu.VMEM(upper_block.shape, F32), pltpu.SMEM(inflow_map.shape, jnp.int32), pltpu.SemaphoreType.DMA((8,))),
    )
    relayed = lax.ppermute(ahead, "stream", [(i + 8, i + 1) for i in range(0, layers - 8, 8)])
    own, terms = call(
        vectors_kernel, (f32(LONG, LANES), f32(2, 16, FACE)),
        maps, upper, from_near, from_far, relayed,
    )

    def across(x, distance):
        return lax.ppermute(x, "stream", [(i, i ^ distance) for i in range(layers)])

    got = across(own, 1)
    chain, lefts = call(
        first_pair_kernel, (f32(3 * FACE + 8, LANES), f32(2, FACE, LANES)), upper, own, got, relayed
    )
    groups = [[8 * g + j for j in range(8)] for g in range(layers // 8)]
    chains = lax.all_gather(chain, "stream", axis_index_groups=groups)
    eight, pair_lefts = call(
        four_kernel, (f32(ROWS, LANES), f32(4, 2, FACE, LANES)), chains
    )
    here = (f32(2, 3, FACE, LANES), f32(8, LANES))
    got8 = across(eight, 8)
    spot, turn = call(four_place_kernel, here, place, upper, own, got, lefts, chains, pair_lefts, smem=(0,))
    terms, eight = lax.optimization_barrier((terms, eight))
    zin, zout, base = call(rest_kernel, tuple(f32(2, DOF, LANES) for _ in range(3)), inv, low, rhs, west, east, terms)
    fixed, free = call(
        answer_kernel, (f32(2, 8, DOF), f32(2, DOF, 2 * LANES)), spot, turn, zin, zout, base
    )
    got8, fixed, free, turn = lax.optimization_barrier((got8, fixed, free, turn))
    chain = call(sixteen_kernel, f32(2 * FACE + 8, LANES), upper, eight, got8)
    groups = [
        [16 * i + 8 * odd + 2 * z + c for i in range(layers // 16) for c in range(2)]
        for odd in range(2)
        for z in range(4)
    ]
    sixteens = lax.all_gather(chain, "stream", axis_index_groups=groups)
    out = call(last_kernel, f32(8, 2, DOF), upper, sixteens, eight, got8, turn, fixed, free)
    return out[None, None]


def solution(mesh):
    in_specs = (
        P("stream", "span", None, None, None),
        P("stream", "span", None, None, None),
        P("stream", "span", None, None, None),
        P("stream", "span", None, None, None),
        P("stream", "span", None, None, None),
        P("stream", "span", None, None, None),
        P("stream", "span", None, None, None),
        P("stream", "span", None),
    )
    out_specs = P("stream", "span", None, None, None)
    return jax.shard_map(
        per_device, mesh=mesh, in_specs=in_specs, out_specs=out_specs, check_vma=False
    )
```

```python
import functools

import jax
import jax.numpy as jnp
from jax import lax
from jax.experimental import pallas as pl
from jax.experimental.pallas import tpu as pltpu
from jax.sharding import PartitionSpec as P

NVAR = 5
NB = 4
FACE = 80
DOF = 320
LANES = 128
VEC = FACE
REST = FACE + 8
HALF = LANES - REST
BF16 = jnp.bfloat16
F32 = jnp.float32
NN = (((1,), (0,)), ((), ()))
NT = (((1,), (1,)), ((), ()))


def split(x):
    hi = x.astype(BF16)
    return hi, (x - hi.astype(F32)).astype(BF16)


def dot(a, b, dims=NN):
    ah, al = split(a)
    bh, bl = split(b)
    one = functools.partial(lax.dot_general, dimension_numbers=dims, preferred_element_type=F32)
    return one(ah, bh) + (one(ah, bl) + one(al, bh))


def pick(x, onehot, dims=NN):
    hi = x.astype(BF16).astype(F32)
    mid = (x - hi).astype(BF16).astype(F32)
    low = x - hi - mid
    rows = x.shape[0]
    parts = jnp.concatenate([hi, mid, low], axis=0).astype(BF16)
    made = lax.dot_general(parts, onehot, dimension_numbers=dims, preferred_element_type=F32)
    return made[:rows] + made[rows : 2 * rows] + made[2 * rows :]


def stream_pick(j, width=FACE):
    d = lax.broadcasted_iota(jnp.int32, (DOF, width), 0)
    f = lax.broadcasted_iota(jnp.int32, (DOF, width), 1)
    step = NB * NB
    return ((d == (f // step) * (NB * step) + j * step + f % step) & (f < FACE)).astype(F32).astype(BF16)


def span_pick(j, width=FACE):
    d = lax.broadcasted_iota(jnp.int32, (DOF, width), 0)
    f = lax.broadcasted_iota(jnp.int32, (DOF, width), 1)
    return ((d == (f // NB) * (NB * NB) + j * NB + f % NB) & (f < FACE)).astype(F32).astype(BF16)


def stream_rows(x, j):
    step = NB * NB
    return jnp.concatenate(
        [x[(v * NB + j) * step : (v * NB + j + 1) * step] for v in range(NVAR)], axis=0
    )


def place_rows(x, j):
    step = NB * NB
    zeros = jnp.zeros((step, x.shape[1]), x.dtype)
    parts = []
    for v in range(NVAR):
        for a in range(NB):
            parts.append(x[v * step : (v + 1) * step] if a == j else zeros)
    return jnp.concatenate(parts, axis=0)


def lane_of(shape):
    return lax.broadcasted_iota(jnp.int32, shape, 1)


def pack(ab, be, d):
    lane = lane_of(ab.shape)
    left = jnp.where(lane < REST, ab, pltpu.roll(d, REST, 1))
    right = jnp.where(lane < REST, be, pltpu.roll(d, REST - HALF, 1))
    return left, right


def unpack_d(left, right):
    lane = lane_of(left.shape)
    return jnp.where(
        lane < HALF, pltpu.roll(left, LANES - REST, 1), pltpu.roll(right, LANES - REST + HALF, 1)
    )


def tall(x):
    return jnp.concatenate([x, jnp.zeros((LANES - FACE, x.shape[1]), x.dtype)], axis=0)


def widen(x):
    return jnp.concatenate([x, jnp.zeros((x.shape[0], LANES - x.shape[1]), x.dtype)], axis=1)


def side(x):
    x = widen(x)
    before = jnp.zeros((VEC, LANES), x.dtype)
    after = jnp.zeros((LANES - REST, LANES), x.dtype)
    return jnp.concatenate([before, x, after], axis=0)


def vec_only(x):
    lane = lane_of(x.shape)
    return jnp.where((lane >= VEC) & (lane < REST), x, 0.0)


class Segment:
    def __init__(self, left, right, swap):
        self.left, self.right, self.swap = left, right, swap

    @staticmethod
    def of(ref):
        left = [ref[2 * p * FACE : (2 * p + 1) * FACE] for p in range(2)]
        right = [ref[(2 * p + 1) * FACE : (2 * p + 2) * FACE] for p in range(2)]
        return Segment(left, right, ref[4 * FACE : 4 * FACE + 8])

    def write(self, ref):
        for p in range(2):
            ref[2 * p * FACE : (2 * p + 1) * FACE] = self.left[p]
            ref[(2 * p + 1) * FACE : (2 * p + 2) * FACE] = self.right[p]
        ref[4 * FACE : 4 * FACE + 8] = self.swap


def tails_of(ref):
    return [ref[ROWS + p * FACE : ROWS + (p + 1) * FACE] for p in range(2)]


def write_tails(ref, tails):
    for p in range(2):
        ref[ROWS + p * FACE : ROWS + (p + 1) * FACE] = tails[p]


def lagged_left(seg, tails, after):
    return [seg.left[p] - vec_only(dot(tails[p], tall(behind(seg.swap, after, p)))) for p in range(2)]


def behind(swap, pair, p):
    return jnp.where(swap[:1] > 0.5, pair[1 - p], pair[p])


def join(first, second):
    lefts, rights = [], []
    for p in range(2):
        left1, right1 = first.left[p], first.right[p]
        left2, right2 = behind(first.swap, second.left, p), behind(first.swap, second.right, p)
        d1, d2 = unpack_d(left1, right1), unpack_d(left2, right2)
        lane = lane_of(left1.shape)
        through = dot(jnp.concatenate([left2, d2], axis=0), tall(left1))
        ab = through[:FACE] + vec_only(left2)
        back = through[FACE:] + vec_only(right2)
        both = dot(right1, tall(jnp.concatenate([right2, back], axis=1)))
        be = jnp.where(lane < VEC, both[:, :LANES], right1 + both[:, LANES:])
        left, right = pack(ab, be, d1 + both[:, LANES:])
        lefts.append(left)
        rights.append(right)
    return Segment(lefts, rights, jnp.abs(first.swap - second.swap))


def ordered(upper, own, got):
    up = upper[:1] > 0.5

    def pair(a, b):
        return jnp.where(up, a, b)

    def seg(a, b):
        return Segment(
            [pair(a.left[p], b.left[p]) for p in range(2)],
            [pair(a.right[p], b.right[p]) for p in range(2)],
            pair(a.swap, b.swap),
        )

    return seg(got, own), seg(own, got)


def columns_of(rows):
    before = jnp.zeros((VEC, DOF), F32)
    after = jnp.zeros((LANES - REST, DOF), F32)
    return jnp.concatenate([before, rows, after], axis=0).T


def make_maps(inv, low, up, rhs, west, east, coupled, flag, own):
    tables = jnp.concatenate([span_pick(0, LANES), span_pick(3, LANES), stream_pick(3, LANES)], axis=1)
    lane = lane_of((FACE, LANES))
    made, corners = [], []
    for n in range(2):
        m, u = inv[0, 0, n], up[0, 0, n]
        both = jnp.concatenate([stream_rows(m, 3), dot(u, stream_rows(m, 0))], axis=0)
        z = dot(both, widen(place_rows(low[0, 0, n], 0)) + columns_of(rhs[0, 0, :, n, :]))
        cut = pick(both, tables)
        for i in range(2):
            at = LONG + (2 * n + i) * 2 * FACE
            block = (west, east)[i][0, 0, n]
            own[at : at + 2 * FACE] = dot(cut[:, i * LANES : (i + 1) * LANES], tall(widen(block)))
        corners.append(cut[:FACE, 2 * LANES :])
        ahead, down = z[:FACE], z[FACE:]
        made.append(
            pack(
                jnp.where(lane < VEC, -ahead, ahead),
                jnp.where(lane < VEC, -cut[FACE:, 2 * LANES :], down),
                -down,
            )
        )
    Segment(
        [behind(flag, [made[0][0], made[1][0]], p) for p in range(2)],
        [behind(flag, [made[0][1], made[1][1]], p) for p in range(2)],
        flag,
    ).write(own)
    write_tails(own, [behind(flag, corners, p) + side(coupled[p]).T[:FACE] for p in range(2)])


def flag_of(which):
    return jnp.full((8, LANES), which[0, 0, 0].astype(F32), F32)


def first_kernel(
    guess_hbm, up_hbm, map_hbm, inv_hbm, low_hbm, rhs_hbm, west_hbm, east_hbm, place, along,
    lag, swap, upper, inv, low, rhs, west, east, own, guess, up, which, sems,
):
    pairs = [(guess_hbm, guess), (up_hbm, up), (map_hbm, which), (inv_hbm, inv), (low_hbm, low), (rhs_hbm, rhs)]
    pairs += [(west_hbm, west), (east_hbm, east)]
    copies = [pltpu.make_async_copy(a, b, sems.at[i]) for i, (a, b) in enumerate(pairs)]
    for copy in copies:
        copy.start()
    for level in range(LEVELS):
        bit = (place[0] >> level) & 1
        upper[level] = jnp.full((8, LANES), bit.astype(F32), F32)
    upper[LEVELS] = jnp.full((8, LANES), (along[0] & 1).astype(F32), F32)
    pin = stream_pick(0)
    for copy in copies[:3]:
        copy.wait()
    both = pick(jnp.concatenate([guess[0, 0, :, n, :] for n in range(2)], axis=0), pin)
    flag = flag_of(which)
    swap[...] = flag
    swapped = flag[:, :FACE] > 0.5
    made = []
    for n in range(2):
        made.append(dot(both[8 * n : 8 * n + 8], up[0, 0, n], NT))
    for p in range(2):
        lag[p] = jnp.where(swapped, made[1 - p], made[p])
    for copy in copies[3:]:
        copy.wait()
    make_maps(inv, low, up, rhs, west, east, lag, flag, own)


def vectors_kernel(maps, upper, from_near, from_far, relayed, own, terms):
    odd = upper[LEVELS][:1, :1] > 0.5
    near = jnp.concatenate([from_near[0, 0, :, n, :] for n in range(2)], axis=0)
    far = jnp.concatenate([from_far[0, 0, :, n, :] for n in range(2)], axis=0)
    from_west = pick(jnp.where(odd, near, far), span_pick(3))
    from_east = pick(jnp.where(odd, far, near), span_pick(0))
    terms[0], terms[1] = from_west, from_east
    b, e = [], []
    for n in range(2):
        rows = slice(8 * n, 8 * n + 8)
        sides = jnp.concatenate([side(from_west[rows]), side(from_east[rows])], axis=1)
        at = LONG + 2 * n * 2 * FACE
        cuts = jnp.concatenate([maps[at + i * 2 * FACE : at + (i + 1) * 2 * FACE] for i in range(2)], axis=1)
        both = dot(cuts, sides, NT)
        b.append(both[:FACE])
        e.append(both[FACE:])
    seg = Segment.of(maps)
    Segment(
        [seg.left[p] - behind(seg.swap, b, p) for p in range(2)],
        [seg.right[p] - behind(seg.swap, e, p) for p in range(2)],
        seg.swap,
    ).write(own)
    write_tails(own, tails_of(maps))


def rest_kernel(inv, low, rhs, west, east, terms, zin, zout, base):
    pout = stream_pick(3, LANES)
    lane = lane_of((DOF, LANES))
    made = [
        jnp.concatenate([dot(terms[i, 8 * n : 8 * n + 8], block[0, 0, n], NT) for n in range(2)], axis=0)
        for i, block in enumerate((west, east))
    ]
    halo = pick(made[0], span_pick(0), NT) + pick(made[1], span_pick(3), NT)
    for n in range(2):
        m = inv[0, 0, n]
        h = rhs[0, 0, :, n, :] - halo[8 * n : 8 * n + 8]
        z = dot(m, widen(place_rows(low[0, 0, n], 0)) + columns_of(h))
        zout[n] = pick(m, pout)
        zin[n] = jnp.where(lane < VEC, z, 0.0)
        base[n] = vec_only(z)


def sixteen_kernel(upper, own, got, out):
    both = join(*ordered(upper[3], Segment.of(own), Segment.of(got)))
    second = upper[0][:1] > 0.5
    for i, pair in enumerate((both.left, both.right)):
        out[i * FACE : (i + 1) * FACE] = jnp.where(second, pair[1], pair[0])
    out[2 * FACE :] = both.swap


def first_pair_kernel(upper, own, got, relayed, out, lefts):
    first, second = ordered(upper[0], Segment.of(own), Segment.of(got))
    up = upper[0][:1] > 0.5
    mine, other = tails_of(own), tails_of(got)
    tails1 = [jnp.where(up, other[p], mine[p]) for p in range(2)]
    tails2 = [jnp.where(up, mine[p], other[p]) for p in range(2)]
    first = Segment(lagged_left(first, tails1, tails2), first.right, first.swap)
    both = join(first, second)
    lane = lane_of((FACE, LANES))
    tails = [jnp.where(lane < VEC, behind(first.swap, tails2, p), tails1[p]) for p in range(2)]
    behind_eight = sum(pltpu.roll(side(relayed[p]).T[:FACE], 8 * (p + 1), 1) for p in range(2))
    for p in range(2):
        lefts[p] = first.left[p]
    for i, pair in enumerate((both.left, both.right, tails)):
        out[i * FACE : (i + 1) * FACE] = jnp.where(up, pair[1], pair[0]) + (behind_eight if i == 2 else 0.0)
    out[2 * FACE : 2 * FACE + 8, LANES - 8 :] = both.swap[:, LANES - 8 :]


def swap_in(rows):
    return jnp.broadcast_to(rows[:, LANES - 1 :], rows.shape)


def four_kernel(got, out, halves, lefts):
    def chain(i, p, tile):
        return got[2 * i + p, tile * FACE : (tile + 1) * FACE]

    tails = [[chain(i, p, 2) for p in range(2)] for i in range(4)]
    last = [pltpu.roll(tails[0][1], LANES - 8 * (p + 1), 1) for p in range(2)]
    segs = []
    for i in range(4):
        seg = Segment([chain(i, p, 0) for p in range(2)], [chain(i, p, 1) for p in range(2)], swap_in(got[2 * i, 2 * FACE : 2 * FACE + 8]))
        seg = Segment(lagged_left(seg, tails[i], tails[i + 1] if i < 3 else last), seg.right, seg.swap)
        for p in range(2):
            lefts[i, p] = seg.left[p]
        segs.append(seg)
    both = [join(segs[2 * i], segs[2 * i + 1]) for i in range(2)]
    join(*both).write(out)
    for i in range(2):
        both[i].write(halves.at[i])


def start_place():
    eye = (lax.broadcasted_iota(jnp.int32, (FACE, LANES), 0) == lane_of((FACE, LANES))).astype(F32)
    zero = jnp.zeros((FACE, LANES), F32)
    return [[eye, zero, eye] for _ in range(2)]


def widen_place(place, upper, own, got):
    lane = lane_of((FACE, LANES))
    keep = lane < REST
    up = upper[:1] > 0.5
    made = []
    for p in range(2):
        near = [behind(got.swap, [place[0][i], place[1][i]], p) for i in range(3)]
        sib = tall(got.left[p])
        moved = dot(jnp.concatenate([near[0], near[1]], axis=0), sib)
        above = [
            jnp.where(keep, moved[:FACE], 0.0) + vec_only(near[0]),
            jnp.where(keep, moved[FACE:], 0.0) + vec_only(near[1]),
            near[2],
        ]
        left2, right2 = behind(own.swap, got.left, p), behind(own.swap, got.right, p)
        back = dot(unpack_d(left2, right2), tall(own.left[p])) + vec_only(right2)
        turned = dot(place[p][2], tall(jnp.concatenate([back, right2], axis=1)))
        below = [
            place[p][0],
            place[p][1] + jnp.where(keep, turned[:, :LANES], 0.0),
            jnp.where(lane < VEC, turned[:, LANES:], 0.0),
        ]
        made.append([jnp.where(up, above[i], below[i]) for i in range(3)])
    return made


def read_place(ref):
    return [[ref[p, i] for i in range(3)] for p in range(2)]


def write_place(ref, place):
    for p in range(2):
        for i in range(3):
            ref[p, i] = place[p][i]


def four_place_kernel(at, upper, one, one_got, lefts, got, pair_lefts, halves, out, swap_out):
    mine, other = Segment.of(one), Segment.of(one_got)
    up = upper[0][:1] > 0.5
    mine.left = [jnp.where(up, mine.left[p], lefts[p]) for p in range(2)]
    other.left = [jnp.where(up, lefts[p], other.left[p]) for p in range(2)]
    made = widen_place(start_place(), upper[0], mine, other)
    x = jnp.abs(mine.swap - jnp.where(upper[0] > 0.5, other.swap, 0.0))
    j = (at[0] >> 1) & 3
    half = j >> 1

    def pair_of(i):
        right = [got[2 * i + p, FACE : 2 * FACE] for p in range(2)]
        return Segment([pair_lefts[i, p] for p in range(2)], right, swap_in(got[2 * i, 2 * FACE : 2 * FACE + 8]))

    mine, other = pair_of(j), pair_of(j ^ 1)
    made = widen_place(made, upper[1], mine, other)
    x = jnp.abs(x - jnp.where(upper[1] > 0.5, other.swap, 0.0))
    mine, other = Segment.of(halves.at[half]), Segment.of(halves.at[1 - half])
    write_place(out, widen_place(made, upper[2], mine, other))
    swap_out[...] = jnp.abs(x - jnp.where(upper[2] > 0.5, other.swap, 0.0))


def answer_kernel(place, turn, zin, zout, base, fixed, free):
    made = read_place(place)
    x = turn[...]
    for n in range(2):
        p0, q0, r0 = [behind(x, [made[0][i], made[1][i]], n) for i in range(3)]
        f = dot(jnp.concatenate([zin[n], zout[n]], axis=1), jnp.concatenate([tall(p0), tall(q0)], axis=0))
        free[n] = jnp.concatenate([f, dot(zout[n], tall(r0))], axis=1)
        fixed[n] = (base[n] - f).T[VEC:REST]


def last_kernel(upper, got, own, got8, turn, fixed, free, out):
    def chain(i, p, tile):
        return got[2 * i + p, tile * FACE : (tile + 1) * FACE]

    def stack(*parts):
        return jnp.concatenate(parts, axis=0)

    def beside(*parts):
        return jnp.concatenate(parts, axis=1)

    segs = [
        Segment([chain(i, p, 0) for p in range(2)], [chain(i, p, 1) for p in range(2)], got[2 * i, 2 * FACE :])
        for i in range(4)
    ]
    d = [None] + [[unpack_d(segs[i].left[p], segs[i].right[p]) for p in range(2)] for i in (1, 2, 3)]
    w0, w1, w2 = [seg.swap for seg in segs[:3]]
    mine, other = Segment.of(own), Segment.of(got8)
    up = upper[3][:1] > 0.5
    zero = jnp.zeros((FACE, LANES), F32)

    t1 = [behind(w0, [vec_only(segs[0].left[q]) for q in range(2)], p) for p in range(2)]
    steps = [dot(stack(d[1][p], segs[1].left[p]), tall(t1[p])) for p in range(2)]
    down1 = [steps[p][:FACE] + vec_only(segs[1].right[p]) for p in range(2)]
    t2 = [vec_only(steps[p][FACE:] + segs[1].left[p]) for p in range(2)]
    t2 = [behind(w1, t2, p) for p in range(2)]
    turned = [
        dot(behind(w2, d[3], p), tall(segs[2].left[p])) + vec_only(behind(w2, segs[3].right, p)) for p in range(2)
    ]
    both_back = [dot(segs[1].right[p], tall(behind(w1, segs[2].right, p))) for p in range(2)]
    near_right = [behind(mine.swap, other.right, p) for p in range(2)]
    near_d = [unpack_d(other.left[p], other.right[p]) for p in range(2)]
    near_back = [
        dot(behind(mine.swap, near_d, p), tall(mine.left[p])) + vec_only(near_right[p]) for p in range(2)
    ]

    steps = [dot(stack(d[2][p], turned[p], segs[2].left[p]), tall(t2[p])) for p in range(2)]
    down2 = [vec_only(steps[p][:FACE]) for p in range(2)]
    c2 = [vec_only(steps[p][FACE : 2 * FACE] + turned[p]) for p in range(2)]
    t3 = [vec_only(steps[p][2 * FACE :] + segs[2].left[p]) for p in range(2)]
    t3 = [behind(w2, t3, p) for p in range(2)]

    c1 = [vec_only(dot(segs[2].right[p], tall(c2[p])) + down2[p] + segs[2].right[p]) for p in range(2)]
    c1 = [behind(w1, c1, p) for p in range(2)]
    c0 = []
    for p in range(2):
        made = dot(
            beside(both_back[p], segs[1].right[p]), stack(tall(behind(w1, c2, p)), tall(behind(w1, down2, p)))
        )
        c0.append(vec_only(made + both_back[p] + down1[p]))
    c0 = [behind(w0, c0, p) for p in range(2)]

    def here(a, b, c, e):
        low, high = upper[4][:1] > 0.5, upper[5][:1] > 0.5
        return [jnp.where(high, jnp.where(low, e[p], c[p]), jnp.where(low, b[p], a[p])) for p in range(2)]

    t_in = here([zero, zero], t1, t2, t3)
    c_out = here(c0, c1, c2, [zero, zero])
    through = [vec_only(dot(other.left[p], tall(t_in[p])) + other.left[p]) for p in range(2)]
    t_at, c_at = [], []
    for p in range(2):
        back = dot(beside(near_back[p], near_right[p]), stack(tall(t_in[p]), tall(c_out[p])))
        t_at.append(jnp.where(up, behind(other.swap, through, p), t_in[p]))
        c_at.append(jnp.where(up, behind(other.swap, c_out, p), vec_only(back + near_back[p])))
    for n in range(2):
        rows = [widen(behind(turn[...], pair, n).T[VEC:REST]) for pair in (t_at, c_at)]
        out[:, n, :] = fixed[n] - dot(beside(*rows), free[n], NT)


HBM = pl.BlockSpec(memory_space=pltpu.HBM)
VMEM = pl.BlockSpec(memory_space=pltpu.VMEM)
SMEM = pl.BlockSpec(memory_space=pltpu.SMEM)


def call(kernel, out_shape, *operands, hbm=(), smem=(), scratch=()):
    specs = [HBM if i in hbm else SMEM if i in smem else VMEM for i in range(len(operands))]
    several = isinstance(out_shape, tuple)
    operands = [
        pltpu.with_memory_space_constraint(x, pltpu.HBM) if i in hbm else x for i, x in enumerate(operands)
    ]
    return pl.pallas_call(
        kernel,
        out_shape=out_shape,
        in_specs=specs,
        out_specs=tuple(VMEM for _ in out_shape) if several else VMEM,
        scratch_shapes=list(scratch),
        cost_estimate=pl.CostEstimate(flops=0, bytes_accessed=1 << 20, transcendentals=0),
        compiler_params=pltpu.CompilerParams(vmem_limit_bytes=24 * 1024 * 1024),
    )(*operands)


def f32(*shape):
    return jax.ShapeDtypeStruct(shape, F32)


LEVELS = 6
ROWS = 4 * FACE + 8
LONG = ROWS + 2 * FACE


def per_device(
    rhs_field, guess, inverse_diag, lower_block, upper_block, west_block, east_block, inflow_map
):
    wide = lax.axis_size("span")
    layers = lax.axis_size("stream")
    place = lax.axis_index("stream").astype(jnp.int32).reshape(1)
    along = lax.axis_index("span").astype(jnp.int32).reshape(1)
    from_far = lax.ppermute(guess, "span", [(i, (i - 1 + 2 * (i & 1)) % wide) for i in range(wide)])
    from_near = lax.ppermute(guess, "span", [(i, i ^ 1) for i in range(wide)])
    args = (guess, upper_block, inflow_map, inverse_diag, lower_block, rhs_field, west_block, east_block)
    ahead, swap, upper, inv, low, rhs, west, east, maps = call(
        first_kernel,
        (
            f32(2, 8, FACE), f32(8, LANES), f32(LEVELS + 1, 8, LANES),
            *(f32(*a.shape) for a in (inverse_diag, lower_block, rhs_field, west_block, east_block)),
            f32(LONG + 8 * FACE, LANES),
        ),
        *args, place, along,
        hbm=range(8), smem=(8, 9),
        scratch=(pltpu.VMEM(guess.shape, F32), pltpu.VMEM(upper_block.shape, F32), pltpu.SMEM(inflow_map.shape, jnp.int32), pltpu.SemaphoreType.DMA((8,))),
    )
    relayed = lax.ppermute(ahead, "stream", [(i + 8, i + 1) for i in range(0, layers - 8, 8)])
    own, terms = call(
        vectors_kernel, (f32(LONG, LANES), f32(2, 16, FACE)),
        maps, upper, from_near, from_far, relayed,
    )

    def across(x, distance):
        return lax.ppermute(x, "stream", [(i, i ^ distance) for i in range(layers)])

    got = across(own, 1)
    chain, lefts = call(
        first_pair_kernel, (f32(3 * FACE, LANES), f32(2, FACE, LANES)), upper, own, got, relayed
    )
    groups = [[8 * g + j for j in range(8)] for g in range(layers // 8)]
    chains = lax.all_gather(chain, "stream", axis_index_groups=groups)
    eight, halves, pair_lefts = call(
        four_kernel, (f32(ROWS, LANES), f32(2, ROWS, LANES), f32(4, 2, FACE, LANES)), chains
    )
    here = (f32(2, 3, FACE, LANES), f32(8, LANES))
    got8 = across(eight, 8)
    spot, turn = call(four_place_kernel, here, place, upper, own, got, lefts, chains, pair_lefts, halves, smem=(0,))
    terms, eight = lax.optimization_barrier((terms, eight))
    zin, zout, base = call(rest_kernel, tuple(f32(2, DOF, LANES) for _ in range(3)), inv, low, rhs, west, east, terms)
    fixed, free = call(
        answer_kernel, (f32(2, 8, DOF), f32(2, DOF, 2 * LANES)), spot, turn, zin, zout, base
    )
    got8, fixed, free, turn = lax.optimization_barrier((got8, fixed, free, turn))
    chain = call(sixteen_kernel, f32(2 * FACE + 8, LANES), upper, eight, got8)
    groups = [
        [16 * i + 8 * odd + 2 * z + c for i in range(layers // 16) for c in range(2)]
        for odd in range(2)
        for z in range(4)
    ]
    sixteens = lax.all_gather(chain, "stream", axis_index_groups=groups)
    out = call(last_kernel, f32(8, 2, DOF), upper, sixteens, eight, got8, turn, fixed, free)
    return out[None, None]


def solution(mesh):
    in_specs = (
        P("stream", "span", None, None, None),
        P("stream", "span", None, None, None),
        P("stream", "span", None, None, None),
        P("stream", "span", None, None, None),
        P("stream", "span", None, None, None),
        P("stream", "span", None, None, None),
        P("stream", "span", None, None, None),
        P("stream", "span", None),
    )
    out_specs = P("stream", "span", None, None, None)
    return jax.shard_map(
        per_device, mesh=mesh, in_specs=in_specs, out_specs=out_specs, check_vma=False
    )
```
